256 devices in a mesh: owner: 8 (over y, x_lo), tile: 32 (over z, x_hi, core).
Axes of the slice: x: 4 (x_hi: 2, x_lo: 2; x = x_hi * 2 + x_lo), y: 4, z: 8, core: 2. Of those that a mesh axis runs over, the one named last changes fastest.
Arguments:
- embeddings: bfloat16 [65536, 768], P(('owner', 'tile'))
- cluster_id: int32 [65536], P(('owner', 'tile')), may hold values from 0 to 15, as said below
- order_rank: int32 [65536], P(('owner', 'tile')), may hold values from 0 to 65535, each once
- row_count: int32 [256], P(('owner', 'tile')), may hold values from 1 to 256, 49152 in all
Outputs:
- dup_score: float32 [65536], P(('owner', 'tile'))
The draws below stay inside these ranges and needn't reach their ends.
Inputs may be any that keep to these rules, and one draw needn't show every extreme that they name: cluster_id mod 8 is the owner group of the cluster; among the live rows of one device at most 48 belong to one owner group, and some device has exactly 48 for one group.
All inputs are finite; a program needn't handle non-finite values. No bound on the sum of `row_count` on one device may be relied on, other than what follows from the above.
Results may differ from the reference program's by a relative error of at most 0.00052.
Values may be sent and summed in bfloat16 or wider, within the bound.
No kernel may reach another device: no remote copies, remote signals or barrier semaphores. Data moves between devices by JAX's collectives and lax.ppermute only.
A program may use at most 128 MiB of HBM per device.

```python
import math
import jax
import jax.numpy as jnp
import numpy as np
from jax import lax

D = 768
ROWS_DEV = 256
CL_OWN = 2
OWNERS = 8
CAP = 48
CLUSTERS = 16
TOTAL = 65536
DEVICES = 256


def route_rows(key):
    device_total = TOTAL // ROWS_DEV

    def one_device(device_key):
        busy_key, seat_key, which_key = jax.random.split(device_key, 3)
        busy_group = jax.random.randint(busy_key, (), 0, OWNERS)
        seats = jnp.arange(OWNERS * CAP, dtype=jnp.int32)
        seat_group = seats // CAP
        seat_score = jax.random.permutation(seat_key, OWNERS * CAP).astype(jnp.int32) + jnp.where(seat_group == busy_group, OWNERS * CAP, 0)
        picked = jnp.argsort(seat_score, stable=True)[:ROWS_DEV - CAP]
        target = jnp.concatenate([jnp.full((CAP,), busy_group, jnp.int32), seat_group[picked]])
        which = jax.random.randint(which_key, (ROWS_DEV,), 0, CL_OWN)
        return (target + OWNERS * which).astype(jnp.int32)
    device_keys = jax.random.split(jax.random.fold_in(key, 101), device_total)
    return jax.vmap(one_device)(device_keys).reshape(TOTAL)


def draw_cluster_id(key, part):
    return route_rows(key)


def draw_embeddings(key, part):
    cluster_of = route_rows(key)
    key = jax.random.fold_in(key, 7)
    center_key, mix_key, noise_key, scale_key = jax.random.split(key, 4)
    centers = jax.random.normal(center_key, (CLUSTERS, D), jnp.float32)
    mixing = jax.random.uniform(mix_key, (TOTAL, 1), jnp.float32, 0.4, 1.6)
    row_scale = jnp.exp(jax.random.uniform(scale_key, (TOTAL, 1), jnp.float32, 0.0, math.log(10.0)))
    noise = jax.random.normal(noise_key, (TOTAL, D), jnp.float32)
    values = row_scale * (mixing * centers[cluster_of] + noise)
    return values.astype(jnp.bfloat16)


def profile(number_of, total, most, skew):
    weights = [(1 << 20) // math.isqrt(grade ** skew) + 1 for grade in range(2, number_of + 1)]
    rest, counts = total - most - (number_of - 1), [1] * (number_of - 1)
    while rest > 0:
        candidates = [i for i in range(number_of - 1) if counts[i] < most]
        mass, left = sum([weights[i] for i in candidates]), rest
        for i in candidates:
            addition = min(most - counts[i], max(1, left * weights[i] // mass), rest)
            counts[i] = counts[i] + addition
            rest = rest - addition
    return np.array([most] + counts)


def ragged_sizes(rng, count, total, bound, slope):
    if count == 2:
        one = jax.random.randint(rng, (), max(1, total - bound), min(bound, total - 1) + 1)
        return jnp.stack([one, total - one])
    tallies = jnp.asarray(profile(count, total, bound, slope), jnp.int32)
    twos = (count - 1) // 2
    giver, sink = tallies[1:1 + 2 * twos:2], tallies[2:2 + 2 * twos:2]
    room = jnp.minimum(giver - 1, bound - sink)
    passed = jax.random.randint(jax.random.fold_in(rng, 1), (twos,), 0, 1 << 20) % (room + 1)
    tallies = tallies.at[1:1 + 2 * twos:2].set(giver - passed).at[2:2 + 2 * twos:2].set(sink + passed)
    return tallies[jax.random.permutation(jax.random.fold_in(rng, 2), count)]


def setup_inputs(seed: int = 0) -> dict:
    arg_keys = jax.random.split(jax.random.key(seed), 5)
    return {
        "embeddings": draw_embeddings(jax.random.fold_in(arg_keys[4], 71), 0),
        "cluster_id": draw_cluster_id(jax.random.fold_in(arg_keys[4], 71), 0),
        "order_rank": jax.random.permutation(arg_keys[2], TOTAL).astype(jnp.int32),
        "row_count": ragged_sizes(arg_keys[3], DEVICES, DEVICES * ROWS_DEV * 3 // 4, ROWS_DEV, 1).astype(jnp.int32),
    }


norm_eps = 1e-06

def reference(embeddings, cluster_id, order_rank, row_count):
    row_total = embeddings.shape[0]
    widened = embeddings.astype(jnp.float32)
    unit_rows = (widened * lax.rsqrt(lax.optimization_barrier(jnp.sum(widened * widened, axis=1, keepdims=True)) + norm_eps)).astype(jnp.bfloat16)
    position = jnp.arange(row_total, dtype=jnp.int32)
    device_of = (position // ROWS_DEV).astype(jnp.int32)
    live_row = position - device_of * ROWS_DEV < row_count[device_of]
    group_id = jnp.where(live_row, cluster_id, -1).astype(jnp.int32)
    sort_key = jnp.where(live_row, cluster_id, CLUSTERS).astype(jnp.int32)
    by_rank = jnp.argsort(order_rank, stable=True).astype(jnp.int32)
    by_cluster = jnp.argsort(sort_key[by_rank], stable=True).astype(jnp.int32)
    ordering = by_rank[by_cluster]
    sorted_rows = unit_rows[ordering]
    sorted_ids = group_id[ordering]
    sorted_ranks = order_rank[ordering]
    change = jnp.concatenate([jnp.ones((1,), bool), sorted_ids[1:] != sorted_ids[:-1]])
    cluster_start = lax.cummax(jnp.where(change, position, 0).astype(jnp.int32), axis=0)
    block_rows = math.gcd(row_total, 512)

    def one_block(block_index):
        first_row = (block_index * block_rows).astype(jnp.int32)
        query_rows = lax.dynamic_slice_in_dim(sorted_rows, first_row, block_rows, 0)
        query_ids = lax.dynamic_slice_in_dim(sorted_ids, first_row, block_rows, 0)
        query_ranks = lax.dynamic_slice_in_dim(sorted_ranks, first_row, block_rows, 0)
        first_id = sorted_ids[first_row]
        start_block = jnp.where(first_id >= 0, cluster_start[first_row] // block_rows, block_index).astype(jnp.int32)

        def key_step(key_block, carried):
            key_first = (key_block * block_rows).astype(jnp.int32)
            key_rows = lax.dynamic_slice_in_dim(sorted_rows, key_first, block_rows, 0)
            key_ids = lax.dynamic_slice_in_dim(sorted_ids, key_first, block_rows, 0)
            key_ranks = lax.dynamic_slice_in_dim(sorted_ranks, key_first, block_rows, 0)
            scores = jnp.dot(query_rows, key_rows.T, preferred_element_type=jnp.float32)
            allowed = (query_ids[:, None] == key_ids[None, :]) & (key_ids[None, :] >= 0) & (key_ranks[None, :] < query_ranks[:, None])
            return jnp.maximum(carried, lax.optimization_barrier(jnp.max(jnp.where(allowed, scores, -1.0), axis=1)))
        return lax.fori_loop(start_block, block_index + 1, key_step, jnp.full((block_rows,), -1.0, jnp.float32))
    best_sorted = lax.map(one_block, jnp.arange(row_total // block_rows, dtype=jnp.int32)).reshape(row_total)
    best_sorted = jnp.where(sorted_ids >= 0, best_sorted, 0.0)
    return jnp.zeros((row_total,), jnp.float32).at[ordering].set(best_sorted)
```

```python
import functools

import jax
import jax.numpy as jnp
from jax import lax
from jax.experimental import pallas as pl
from jax.experimental.pallas import tpu as pltpu
from jax.sharding import Mesh, PartitionSpec as P

norm_eps = 1e-06
ROWS = 256
WIDTH = 768
META = 128
GROUPS = 8
SLOTS = 48
ROUTED = GROUPS * SLOTS
CAP = 304
HELD = CAP - 3
CAPL = 384
LAST = CAP - 16
NEVER = 512.0
PIECES = (1, 1, 2, 1, 1, 1, 1)
OVER = 100.0
VMEM_LIMIT = 50 * 1024 * 1024
PLANE = ("y", "xl", "xh", "core")
COLUMN = ("z", "core")
RETURN = ("xl", "z", "xh", "core")


def dot(a, b, contract):
    return lax.dot_general(a, b, (contract, ((), ())), preferred_element_type=jnp.float32)


def iota(shape, axis):
    return lax.broadcasted_iota(jnp.int32, shape, axis)


def split3(v):
    hi = v.astype(jnp.bfloat16)
    rest = v - hi.astype(jnp.float32)
    mid = rest.astype(jnp.bfloat16)
    low = (rest - mid.astype(jnp.float32)).astype(jnp.bfloat16)
    return hi, mid, low


def pick_rows(v, one_hot):
    n = v.shape[0]
    parts = dot(jnp.concatenate(split3(v), axis=0), one_hot, ((1,), (0,)))
    return (parts[:n] + parts[n : 2 * n]) + parts[2 * n :]


def call(kernel, out, *args, smem=(), smem_out=(), cost=1, scratch=()):
    space = lambda i, scalars: pl.BlockSpec(memory_space=pltpu.SMEM if i in scalars else pltpu.VMEM)
    out_specs = space(0, smem_out)
    if isinstance(out, tuple):
        out_specs = tuple(space(i, smem_out) for i in range(len(out)))
    return pl.pallas_call(
        kernel,
        out_shape=out,
        in_specs=[space(i, smem) for i in range(len(args))],
        out_specs=out_specs,
        scratch_shapes=list(scratch),
        cost_estimate=pl.CostEstimate(
            flops=2 * cost * CAP * CAP * WIDTH, bytes_accessed=4 * CAP * WIDTH, transcendentals=0
        ),
        compiler_params=pltpu.CompilerParams(vmem_limit_bytes=VMEM_LIMIT),
    )(*args)


def signed(core, value):
    return jnp.where(core == 0, value, -value)


def slot_kernel(place_ref, count_ref, id_ref, rank_ref, where_ref, marks_ref, slot_ref):
    ids = id_ref[...]
    ranks = rank_ref[...]
    live = iota((1, ROWS), 1) < count_ref[0]
    target = ids & (GROUPS - 1)
    chosen = jnp.where((iota((GROUPS, ROWS), 0) == target) & live, 1.0, 0.0)
    upper = jnp.where(iota((ROWS, ROWS), 0) < iota((ROWS, ROWS), 1), 1.0, 0.0).astype(jnp.bfloat16)
    before = dot(chosen.astype(jnp.bfloat16), upper, ((1,), (0,)))
    within = jnp.sum(before * chosen, axis=0, keepdims=True).astype(jnp.int32)
    steps = signed(place_ref[1], target - place_ref[2]) & (GROUPS - 1)
    at = jnp.where(steps == 3, 4, jnp.where(steps == 4, 3, steps))
    slot = jnp.where(live, at * SLOTS + within, -1)
    where_to = jnp.where(iota((ROUTED, ROWS), 0) == slot, 1.0, 0.0).astype(jnp.bfloat16)
    high = ranks >> 8
    row = iota((META, ROWS), 0)
    meta = jnp.where(
        row == 0, ids + 1, jnp.where(row == 1, high, jnp.where(row == 2, ranks - (high << 8), 0))
    )
    meta = meta.astype(jnp.float32).astype(jnp.bfloat16)
    where_ref[...] = where_to
    marks_ref[...] = dot(where_to, meta, ((1,), (1,))).astype(jnp.bfloat16)
    slot_ref[0:1, :] = jnp.where(live, target, -1)
    slot_ref[1:2, :] = within
    slot_ref[2:8, :] = jnp.zeros((6, ROWS), jnp.int32)


def piece_kernel(emb_ref, where_ref, marks_ref, *out_refs):
    x = emb_ref[...].astype(jnp.float32)
    unit = (x * lax.rsqrt(jnp.sum(x * x, axis=1, keepdims=True) + norm_eps)).astype(jnp.bfloat16)
    rows = dot(where_ref[...], unit, ((1,), (0,))).astype(jnp.bfloat16)
    at = 0
    for ref in out_refs:
        size = ref.shape[0]
        ref[:, :WIDTH] = rows[at : at + size]
        ref[:, WIDTH:] = marks_ref[at : at + size, :]
        at += size


def collect_kernel(*refs):
    out_ref = refs[-1]
    for i, ref in enumerate(refs[:-1]):
        out_ref[i * SLOTS : (i + 1) * SLOTS, :] = ref[:SLOTS, :]


def compact_kernel(place_ref, *refs):
    *parts, block_ref, both_ref = refs
    both = 2 * ROUTED
    at = 0
    for ref in parts:
        both_ref[at : at + ref.shape[0], :] = ref[...]
        at += ref.shape[0]
    eye = jnp.where(iota((8, META), 0) == iota((8, META), 1), 1.0, 0.0).astype(jnp.bfloat16)
    meta = dot(eye, both_ref[:, WIDTH:], ((1,), (1,)))
    mine = place_ref[2] + GROUPS * place_ref[1] + 1
    ones = jnp.where(meta[0:1, :] == mine.astype(jnp.float32), 1.0, 0.0)
    chunks = [ones[:, i : i + META] for i in range(0, both, META)]
    upper = jnp.where(iota((META, META), 0) < iota((META, META), 1), 1.0, 0.0).astype(jnp.bfloat16)
    stacked = jnp.concatenate(chunks + [jnp.zeros((8 - len(chunks), META), jnp.float32)], axis=0)
    before = dot(stacked.astype(jnp.bfloat16), upper, ((1,), (0,)))
    total, counted = jnp.zeros((1, 1), jnp.float32), []
    for i, chunk in enumerate(chunks):
        counted.append(jnp.where(chunk > 0.5, before[i : i + 1, :] + total, -1.0))
        total = total + jnp.sum(chunk, axis=1, keepdims=True)
    pos = jnp.concatenate(counted, axis=1).astype(jnp.int32)
    where_to = jnp.where((iota((CAPL, both), 0) == pos) & (pos < HELD), 1.0, 0.0).astype(jnp.bfloat16)
    rows = dot(where_to[:CAP, :], both_ref[:, :WIDTH], ((1,), (0,)))
    ranks = dot(meta.astype(jnp.bfloat16), where_to, ((1,), (1,)))
    lane = iota((1, CAPL), 1)
    filled = (lane.astype(jnp.float32) < total) & (lane < HELD)
    high = jnp.where(filled, ranks[1:2, :], NEVER)
    high = jnp.where((lane == CAPL - 1) & (total > HELD), 2 * NEVER, high)
    low = jnp.where(filled, ranks[2:3, :], 0.0)
    place = pos + 1
    marks = (jnp.concatenate([high, low], axis=1), (place >> 8).astype(jnp.float32), (place & 255).astype(jnp.float32))
    row = iota((16, WIDTH), 0)
    last = rows[LAST:, :]
    for i, mark in enumerate(marks):
        last = jnp.where(row == 13 + i, mark, last)
    block_ref[:LAST, :] = rows[:LAST, :].astype(jnp.bfloat16)
    block_ref[LAST:, :] = last.astype(jnp.bfloat16)


def row_ranks(block):
    tail = block[LAST:, :].astype(jnp.float32)
    return (256.0 * tail[13:14, :CAPL] + tail[13:14, CAPL:])[:, :CAP]


def column_ranks(block, eye):
    high = dot(eye, block[LAST:, :CAPL], ((1,), (1,)))
    low = dot(eye, block[LAST:, CAPL:], ((1,), (1,)))
    return 256.0 * high[:, 13:14] + low[:, 13:14]


def slot_places(block):
    both = 2 * ROUTED
    tail = block[LAST:, :].astype(jnp.float32)
    first = iota((16, both), 0) * SLOTS
    lane = iota((16, both), 1)
    here = (lane >= first) & (lane < first + SLOTS)
    parts = jnp.concatenate([jnp.where(here, tail[i : i + 1, :], 0.0) for i in (14, 15)], axis=0)
    slot = iota((both, META), 0)
    slot = slot - SLOTS * ((slot * 1366) >> 16)
    fold = jnp.where(slot == iota((both, META), 1), 1.0, 0.0).astype(jnp.bfloat16)
    folded = dot(parts.astype(jnp.bfloat16), fold, ((1,), (0,)))
    return (256.0 * folded[:16] + folded[16:]).astype(jnp.int32) - 1


def make_eye():
    return jnp.where(iota((CAP, CAPL), 0) == iota((CAP, CAPL), 1), 1.0, 0.0).astype(jnp.bfloat16)


def earlier_best(query, query_ranks, key, key_ranks):
    scores = dot(key[...], query[...], ((1,), (1,)))
    return jnp.max(jnp.where(key_ranks < query_ranks, scores, -1.0), axis=0, keepdims=True)


def by_core(place_ref, run, a, b):
    pl.when(place_ref[1] == 0)(lambda: run(a, b))
    pl.when(place_ref[1] == 1)(lambda: run(b, a))


def near_kernel(place_ref, own, a_first, a_second, b_first, b_second, best_ref, columns_ref, places_ref):
    def run(xs, ys):
        eye = make_eye()
        keys = (own,) + ys
        key_ranks = [column_ranks(key, eye) for key in keys]
        for i, columns in enumerate(key_ranks):
            columns_ref[i] = jnp.broadcast_to(columns, (CAP, META))
        best_ref[...] = jnp.full((8, CAPL), -1.0, jnp.float32)
        for i, query in enumerate((own,) + xs):
            ranks = row_ranks(query)
            best = jnp.full((1, CAP), -1.0, jnp.float32)
            for key, columns in zip(keys, key_ranks):
                best = jnp.maximum(best, earlier_best(query, ranks, key, columns))
            best_ref[i : i + 1, :CAP] = best
            places_ref[16 * i : 16 * (i + 1), :] = slot_places(query)

    by_core(place_ref, run, (a_first, a_second), (b_first, b_second))


def mid_kernel(
    place_ref, own, a_first, a_second, b_first, b_second, a_far, near_ref, columns_ref,
    best_ref, column_ref, places_ref,
):
    best_ref[...] = near_ref[...]

    def x_far(a, b):
        ranks = row_ranks(a_far)
        best = jnp.full((1, CAP), -1.0, jnp.float32)
        for i, key in enumerate((own,) + b):
            best = jnp.maximum(best, earlier_best(a_far, ranks, key, columns_ref[i, :, 0:1]))
        best_ref[3:4, :CAP] = best
        column_ref[...] = jnp.zeros((CAP, META), jnp.float32)
        places_ref[...] = slot_places(a_far)

    def y_far(b, a):
        columns = column_ranks(a_far, make_eye())
        column_ref[...] = jnp.broadcast_to(columns, (CAP, META))
        for i, query in enumerate((own,) + b):
            best = earlier_best(query, row_ranks(query), a_far, columns)
            best_ref[i : i + 1, :CAP] = jnp.maximum(best_ref[i : i + 1, :CAP], best)
        places_ref[...] = jnp.zeros((16, META), jnp.int32)

    a, b = (a_first, a_second), (b_first, b_second)
    pl.when(place_ref[1] == 0)(lambda: x_far(a, b))
    pl.when(place_ref[1] == 1)(lambda: y_far(b, a))


def far_kernel(
    place_ref, own, a_first, a_second, b_first, b_second, a_far, b_far,
    columns_ref, near_places, mid_ref, column_ref, mid_places, out_ref, best_ref, places_ref,
):
    best_ref[...] = mid_ref[...]
    places_ref[:48, :] = near_places[...]

    def y_far():
        columns = column_ranks(b_far, make_eye())
        for i, query in enumerate((own, a_first, a_second, a_far)):
            best = earlier_best(query, row_ranks(query), b_far, columns)
            best_ref[i : i + 1, :CAP] = jnp.maximum(best_ref[i : i + 1, :CAP], best)
        places_ref[48:, :] = mid_places[...]

    def x_far():
        ranks = row_ranks(b_far)
        best = earlier_best(b_far, ranks, a_far, column_ref[:, 0:1])
        for i, key in enumerate((own, a_first, a_second)):
            best = jnp.maximum(best, earlier_best(b_far, ranks, key, columns_ref[i, :, 0:1]))
        best_ref[3:4, :CAP] = best
        places_ref[48:, :] = slot_places(b_far)

    pl.when(place_ref[1] == 0)(y_far)
    pl.when(place_ref[1] == 1)(x_far)
    over = 0.0
    for block in (own, a_first, a_second, b_first, b_second, a_far, b_far):
        tail = block[LAST:, CAPL - META : CAPL].astype(jnp.float32)
        over = jnp.maximum(over, tail[13:14, META - 1 :])
    over = jnp.where(over > NEVER, 1.0, 0.0)
    my_x, my_core, my_z = place_ref[0], place_ref[1], place_ref[2]
    rows = jnp.concatenate([jnp.broadcast_to(best_ref[i : i + 1, :], (16, CAPL)) for i in range(4)], axis=0)
    places = places_ref[...]
    found = jnp.full((64, META), -1.0, jnp.float32)
    for part in range(CAPL // META):
        values = rows[:, part * META : (part + 1) * META]
        picked = jnp.take_along_axis(values, places & (META - 1), axis=1, mode="promise_in_bounds")
        found = jnp.where((places >> 7) == part, picked, found)
    found = found + OVER * over
    messages = GROUPS * 8
    row, column = iota((messages, messages), 0), iota((messages, messages), 1)
    core = row & 1
    away = my_z - ((row >> 2) & 7)
    steps = jnp.where(core == 0, away, -away) & 7
    x_away = signed(my_core, (row >> 5) + (row & 2) - my_x) & 3
    block = jnp.where(x_away == 2, 3, jnp.where(x_away == 3, 2, x_away))
    wanted = block * 16 + (core ^ my_core) * GROUPS + steps
    order = jnp.where(column == wanted, 1.0, 0.0).astype(jnp.bfloat16)
    high, mid, low = split3(found)
    c = ((1,), (0,))
    out = (dot(order, high, c) + dot(order, mid, c)) + dot(order, low, c)
    for i in range(messages):
        out_ref[i] = out[i : i + 1, :]


def final_kernel(slot_ref, ans_ref, out_ref, flag_ref):
    target, within = slot_ref[0:1, :], slot_ref[1:2, :]
    one_hot = jnp.where(iota((META, ROWS), 0) == within, 1.0, 0.0).astype(jnp.bfloat16)
    groups = []
    for g in range(GROUPS):
        rows = [ans_ref[xl * 32 + g * 4 + i] for xl in range(2) for i in range(4)]
        groups.append(functools.reduce(jnp.maximum, rows))
    best = jnp.concatenate(groups, axis=0)
    got = pick_rows(best, one_hot)
    out_ref[...] = jnp.sum(jnp.where(iota((GROUPS, ROWS), 0) == target, got, 0.0), axis=0, keepdims=True)
    flag_ref[0] = jnp.where(jnp.max(best) > 0.5 * OVER, 1, 0).astype(jnp.int32)


def slow_path(arrived, target, within, live):
    flat = arrived
    rows, meta = flat[:, :WIDTH], flat[:, WIDTH : WIDTH + 3].astype(jnp.float32)
    ids = meta[:, 0]
    ranks = 256.0 * meta[:, 1] + meta[:, 2]
    ring = ("y", "xl", "xh", "core")
    size = 32

    def step(_, carry):
        moving, best = carry
        m = moving[:, WIDTH : WIDTH + 3].astype(jnp.float32)
        scores = dot(rows, moving[:, :WIDTH], ((1,), (1,)))
        allowed = (
            (ids[:, None] == m[None, :, 0])
            & (m[None, :, 0] > 0)
            & ((256.0 * m[:, 1] + m[:, 2])[None, :] < ranks[:, None])
        )
        best = jnp.maximum(best, jnp.max(jnp.where(allowed, scores, -1.0), axis=1))
        moving = lax.ppermute(moving, ring, [(i, (i + 1) % size) for i in range(size)])
        return moving, best

    _, best = lax.fori_loop(0, size, step, (flat, jnp.full((ROUTED,), -1.0, jnp.float32)))
    steps = signed(lax.axis_index("core"), lax.axis_index("z") - jnp.arange(GROUPS)) & (GROUPS - 1)
    answered = lax.all_to_all(best.reshape(GROUPS, SLOTS)[steps], "z", 0, 0, tiled=True)
    picked = answered[jnp.maximum(target, 0), jnp.minimum(within, SLOTS - 1)]
    return jnp.where(live, picked, 0.0)


def column_shift(steps):
    pairs = []
    for z in range(8):
        for core in range(2):
            to = (z + (steps if core == 0 else -steps)) % 8
            pairs.append((z * 2 + core, to * 2 + core))
    return pairs


def plane_shift(step, axis):
    def flat(x, y, core):
        return ((y % 4 * 2 + x % 4 % 2) * 2 + x % 4 // 2) * 2 + core

    pairs = []
    for core in range(2):
        s = step if core == 0 else -step
        dx, dy = (s, 0) if core == axis else (0, s)
        for x in range(4):
            for y in range(4):
                pairs.append((flat(x + dx, y + dy, core), flat(x, y, core)))
    return pairs


def body(embeddings, cluster_id, order_rank, row_count):
    f32, bf16, i32 = jnp.float32, jnp.bfloat16, jnp.int32
    shape = jax.ShapeDtypeStruct
    place = jnp.stack(
        [lax.axis_index("xh") * 2 + lax.axis_index("xl"), lax.axis_index("core"), lax.axis_index("z")]
    ).astype(i32)
    where_to, marks, slots = call(
        slot_kernel,
        (shape((ROUTED, ROWS), bf16), shape((ROUTED, META), bf16), shape((8, ROWS), i32)),
        place,
        row_count,
        cluster_id.reshape(1, ROWS),
        order_rank.reshape(1, ROWS),
        smem=(0, 1),
    )
    pieces = call(
        piece_kernel,
        tuple(shape((n * SLOTS, WIDTH + META), bf16) for n in PIECES),
        embeddings,
        where_to,
        marks,
    )
    send = lambda v, steps: lax.ppermute(v, COLUMN, column_shift(steps))
    two_four = send(pieces[2], 2)
    three, five, six = send(pieces[3], 3), send(pieces[4], 5), send(pieces[5], 6)
    four = send(two_four[SLOTS:], 2)
    one, seven = send(pieces[1], 1), send(pieces[6], 7)
    arrived = call(
        collect_kernel,
        shape((ROUTED, WIDTH + META), bf16),
        pieces[0],
        one,
        two_four,
        three,
        four,
        five,
        six,
        seven,
    )
    other = lax.ppermute(arrived, "core", [(0, 1), (1, 0)])
    block = call(
        compact_kernel,
        shape((CAP, WIDTH), bf16),
        place,
        arrived,
        other,
        smem=(0,),
        scratch=[pltpu.VMEM((2 * ROUTED, WIDTH + META), bf16)],
    )
    bring = lambda v, step, axis: lax.ppermute(v, PLANE, plane_shift(step, axis))
    a_first, b_first = bring(block, 1, 0), bring(block, 1, 1)
    a_second, b_second = bring(block, -1, 0), bring(block, -1, 1)
    a_far, b_far = bring(a_first, 1, 0), bring(b_first, 1, 1)
    blocks = (block, a_first, a_second, b_first, b_second)
    best_shape, column_shape, places_shape = shape((8, CAPL), f32), shape((CAP, META), f32), shape((16, META), i32)
    near, columns, near_places = call(
        near_kernel,
        (best_shape, shape((3, CAP, META), f32), shape((48, META), i32)),
        place,
        *blocks,
        smem=(0,),
        cost=9,
    )
    mid, column, mid_places = call(
        mid_kernel,
        (best_shape, column_shape, places_shape),
        place,
        *blocks,
        a_far,
        near,
        columns,
        smem=(0,),
        cost=3,
    )
    message = call(
        far_kernel,
        shape((64, 1, META), f32),
        place,
        *blocks,
        a_far,
        b_far,
        columns,
        near_places,
        mid,
        column,
        mid_places,
        smem=(0,),
        cost=4,
        scratch=[pltpu.VMEM((8, CAPL), f32), pltpu.VMEM((64, META), i32)],
    )
    answer = lax.all_to_all(message, RETURN, split_axis=0, concat_axis=0, tiled=True)
    out, flag = call(final_kernel, (shape((1, ROWS), f32), shape((1,), i32)), slots, answer, smem_out=(1,))
    target, within = slots[0], slots[1]
    return lax.cond(
        flag[0] > 0,
        lambda: slow_path(arrived, target, within, target >= 0),
        lambda: out.reshape(ROWS),
    )


def solution(mesh):
    axes = ("y", "xl", "z", "xh", "core")
    fine = Mesh(mesh.devices.reshape(4, 2, 8, 2, 2), axes)
    return jax.shard_map(
        body,
        mesh=fine,
        in_specs=(P(axes, None), P(axes), P(axes), P(axes)),
        out_specs=P(axes),
        check_vma=False,
    )
```

```python
import functools

import jax
import jax.numpy as jnp
from jax import lax
from jax.experimental import pallas as pl
from jax.experimental.pallas import tpu as pltpu
from jax.sharding import Mesh, PartitionSpec as P

norm_eps = 1e-06
ROWS = 256
WIDTH = 768
META = 128
GROUPS = 8
SLOTS = 48
ROUTED = GROUPS * SLOTS
CAP = 304
HELD = CAP - 3
CAPL = 384
LAST = CAP - 16
NEVER = 512.0
CHUNKS = WIDTH // META
PIECE = CHUNKS * SLOTS + 16
MARKS = 32
PIECES = (1, 1, 2, 1, 1, 1, 1)
OVER = 100.0
VMEM_LIMIT = 50 * 1024 * 1024
PLANE = ("y", "xl", "xh", "core")
COLUMN = ("z", "core")
RETURN = ("xl", "z", "xh", "core")


def dot(a, b, contract):
    return lax.dot_general(a, b, (contract, ((), ())), preferred_element_type=jnp.float32)


def iota(shape, axis):
    return lax.broadcasted_iota(jnp.int32, shape, axis)


def split3(v):
    hi = v.astype(jnp.bfloat16)
    rest = v - hi.astype(jnp.float32)
    mid = rest.astype(jnp.bfloat16)
    low = (rest - mid.astype(jnp.float32)).astype(jnp.bfloat16)
    return hi, mid, low


def pick_rows(v, one_hot):
    n = v.shape[0]
    parts = dot(jnp.concatenate(split3(v), axis=0), one_hot, ((1,), (0,)))
    return (parts[:n] + parts[n : 2 * n]) + parts[2 * n :]


def call(kernel, out, *args, smem=(), smem_out=(), cost=1, scratch=()):
    space = lambda i, scalars: pl.BlockSpec(memory_space=pltpu.SMEM if i in scalars else pltpu.VMEM)
    out_specs = space(0, smem_out)
    if isinstance(out, tuple):
        out_specs = tuple(space(i, smem_out) for i in range(len(out)))
    return pl.pallas_call(
        kernel,
        out_shape=out,
        in_specs=[space(i, smem) for i in range(len(args))],
        out_specs=out_specs,
        scratch_shapes=list(scratch),
        cost_estimate=pl.CostEstimate(
            flops=2 * cost * CAP * CAP * WIDTH, bytes_accessed=4 * CAP * WIDTH, transcendentals=0
        ),
        compiler_params=pltpu.CompilerParams(vmem_limit_bytes=VMEM_LIMIT),
    )(*args)


def signed(core, value):
    return jnp.where(core == 0, value, -value)


def prep_kernel(count_ref, emb_ref, id_ref, rank_ref, *out_refs):
    slot_ref = out_refs[-1]
    x = emb_ref[...].astype(jnp.float32)
    unit = (x * lax.rsqrt(jnp.sum(x * x, axis=1, keepdims=True) + norm_eps)).astype(jnp.bfloat16)
    ids = id_ref[...]
    ranks = rank_ref[...]
    live = iota((1, ROWS), 1) < count_ref[0]
    target = ids & (GROUPS - 1)
    chosen = jnp.where((iota((GROUPS, ROWS), 0) == target) & live, 1.0, 0.0)
    upper = jnp.where(iota((ROWS, ROWS), 0) < iota((ROWS, ROWS), 1), 1.0, 0.0).astype(jnp.bfloat16)
    before = dot(chosen.astype(jnp.bfloat16), upper, ((1,), (0,)))
    within = jnp.sum(before * chosen, axis=0, keepdims=True).astype(jnp.int32)
    steps = signed(lax.axis_index("core"), target - lax.axis_index("z")) & (GROUPS - 1)
    at = jnp.where(steps == 3, 4, jnp.where(steps == 4, 3, steps))
    slot = jnp.where(live, at * SLOTS + within, -1)
    where_to = jnp.where(iota((ROUTED, ROWS), 0) == slot, 1.0, 0.0).astype(jnp.bfloat16)
    high = ranks >> 8
    row = iota((16, ROWS), 0)
    meta = jnp.where(
        row == 0, ids + 1, jnp.where(row == 1, high, jnp.where(row == 2, ranks - (high << 8), 0))
    )
    meta = meta.astype(jnp.float32).astype(jnp.bfloat16)
    rows = dot(where_to, unit, ((1,), (0,))).astype(jnp.bfloat16)
    marks = dot(meta, where_to, ((1,), (1,)))
    at = 0
    for ref in out_refs[:-1]:
        for first in range(0, ref.shape[0], PIECE):
            for i in range(CHUNKS):
                ref[first + i * SLOTS : first + (i + 1) * SLOTS, :] = rows[
                    at : at + SLOTS, i * META : (i + 1) * META
                ]
            tail = jnp.concatenate(
                [marks[:, at : at + SLOTS], jnp.zeros((16, META - SLOTS), jnp.float32)], axis=1
            )
            ref[first + CHUNKS * SLOTS : first + PIECE, :] = tail.astype(jnp.bfloat16)
            at += SLOTS
    slot_ref[0:1, :] = jnp.where(live, target, -1)
    slot_ref[1:2, :] = within
    slot_ref[2:8, :] = jnp.zeros((6, ROWS), jnp.int32)


def collect_kernel(*refs):
    out_ref = refs[-1]
    marks = []
    for j, ref in enumerate(refs[:-1]):
        for i in range(CHUNKS):
            out_ref[j * SLOTS : (j + 1) * SLOTS, i * META : (i + 1) * META] = ref[
                i * SLOTS : (i + 1) * SLOTS, :
            ]
        marks.append(ref[CHUNKS * SLOTS : PIECE, :].astype(jnp.float32))
    by_kind = [mark[i : i + 1, :] for i in range(3) for mark in marks]
    kinds = jnp.concatenate(by_kind + [jnp.zeros((MARKS - 3 * GROUPS, META), jnp.float32)], axis=0)
    out_ref[ROUTED:, :META] = kinds.astype(jnp.bfloat16)
    out_ref[ROUTED:, META:] = jnp.zeros((MARKS, WIDTH - META), jnp.bfloat16)


def slot_fold(both):
    slot = iota((both, META), 0)
    slot = slot - SLOTS * ((slot * 1366) >> 16)
    return jnp.where(slot == iota((both, META), 1), 1.0, 0.0).astype(jnp.bfloat16)


def place_rows(arrived_ref, first):
    marks = arrived_ref[ROUTED:, :META]
    spread = dot(marks, slot_fold(ROUTED), ((1,), (1,)))
    here = iota((GROUPS, ROUTED), 0) == ((iota((GROUPS, ROUTED), 1) * 1366) >> 16)
    meta = [
        jnp.sum(jnp.where(here, spread[GROUPS * i : GROUPS * (i + 1), :], 0.0), axis=0, keepdims=True)
        for i in range(3)
    ]
    mine = lax.axis_index("z") + GROUPS * lax.axis_index("core") + 1
    ones = jnp.where(meta[0] == mine.astype(jnp.float32), 1.0, 0.0)
    chunks = [ones[:, i : i + META] for i in range(0, ROUTED, META)]
    upper = jnp.where(iota((META, META), 0) < iota((META, META), 1), 1.0, 0.0).astype(jnp.bfloat16)
    stacked = jnp.concatenate(chunks + [jnp.zeros((8 - len(chunks), META), jnp.float32)], axis=0)
    before = dot(stacked.astype(jnp.bfloat16), upper, ((1,), (0,)))
    total, counted = first, []
    for i, chunk in enumerate(chunks):
        counted.append(jnp.where(chunk > 0.5, before[i : i + 1, :] + total, -1.0))
        total = total + jnp.sum(chunk, axis=1, keepdims=True)
    pos = jnp.concatenate(counted, axis=1).astype(jnp.int32)
    where_to = jnp.where((iota((CAPL, ROUTED), 0) == pos) & (pos < HELD), 1.0, 0.0).astype(jnp.bfloat16)
    meta = jnp.concatenate(meta + [jnp.zeros((5, ROUTED), jnp.float32)], axis=0)
    ranks = dot(meta.astype(jnp.bfloat16), where_to, ((1,), (1,)))
    return pos, where_to, ranks, total


def first_kernel(own_ref, rows_ref, pos_ref, ranks_ref, total_ref):
    pos, where_to, ranks, total = place_rows(own_ref, jnp.zeros((1, 1), jnp.float32))
    rows_ref[...] = dot(where_to[:CAP, :], own_ref[:ROUTED, :], ((1,), (0,))).astype(jnp.bfloat16)
    pos_ref[...] = jnp.broadcast_to(pos, (8, ROUTED))
    ranks_ref[...] = ranks
    total_ref[...] = jnp.broadcast_to(total, (8, META))


def compact_kernel(other_ref, rows_ref, pos_ref, ranks_ref, total_ref, block_ref):
    other_pos, where_to, other_ranks, total = place_rows(other_ref, total_ref[0:1, 0:1])
    rows = dot(where_to[:CAP, :], other_ref[:ROUTED, :], ((1,), (0,))) + rows_ref[...].astype(jnp.float32)
    pos = jnp.concatenate([pos_ref[0:1, :], other_pos], axis=1)
    ranks = ranks_ref[...] + other_ranks
    lane = iota((1, CAPL), 1)
    filled = (lane.astype(jnp.float32) < total) & (lane < HELD)
    high = jnp.where(filled, ranks[1:2, :], NEVER)
    high = jnp.where((lane == CAPL - 1) & (total > HELD), 2 * NEVER, high)
    low = jnp.where(filled, ranks[2:3, :], 0.0)
    place = pos + 1
    marks = (jnp.concatenate([high, low], axis=1), (place >> 8).astype(jnp.float32), (place & 255).astype(jnp.float32))
    row = iota((16, WIDTH), 0)
    last = rows[LAST:, :]
    for i, mark in enumerate(marks):
        last = jnp.where(row == 13 + i, mark, last)
    block_ref[:LAST, :] = rows[:LAST, :].astype(jnp.bfloat16)
    block_ref[LAST:, :] = last.astype(jnp.bfloat16)


def row_ranks(block):
    tail = block[LAST:, :].astype(jnp.float32)
    return (256.0 * tail[13:14, :CAPL] + tail[13:14, CAPL:])[:, :CAP]


def column_ranks(block, eye):
    high = dot(eye, block[LAST:, :CAPL], ((1,), (1,)))
    low = dot(eye, block[LAST:, CAPL:], ((1,), (1,)))
    return 256.0 * high[:, 13:14] + low[:, 13:14]


def slot_places(block):
    both = 2 * ROUTED
    tail = block[LAST:, :].astype(jnp.float32)
    first = iota((16, both), 0) * SLOTS
    lane = iota((16, both), 1)
    here = (lane >= first) & (lane < first + SLOTS)
    parts = jnp.concatenate([jnp.where(here, tail[i : i + 1, :], 0.0) for i in (14, 15)], axis=0)
    folded = dot(parts.astype(jnp.bfloat16), slot_fold(both), ((1,), (0,)))
    return (256.0 * folded[:16] + folded[16:]).astype(jnp.int32) - 1


def make_eye():
    return jnp.where(iota((CAP, CAPL), 0) == iota((CAP, CAPL), 1), 1.0, 0.0).astype(jnp.bfloat16)


def earlier_best(query, query_ranks, key, key_ranks):
    scores = dot(key[...], query[...], ((1,), (1,)))
    return jnp.max(jnp.where(key_ranks < query_ranks, scores, -1.0), axis=0, keepdims=True)


def own_kernel(own, best_ref, columns_ref, places_ref):
    columns = column_ranks(own, make_eye())
    columns_ref[...] = jnp.broadcast_to(columns, (CAP, META))
    best_ref[...] = jnp.full((8, CAPL), -1.0, jnp.float32)
    best_ref[0:1, :CAP] = earlier_best(own, row_ranks(own), own, columns)
    places_ref[...] = slot_places(own)


def near_kernel(
    own, x_first, x_second, y_first, y_second, own_best, own_columns, best_ref, columns_ref, places_ref
):
    eye = make_eye()
    ys = (y_first, y_second)
    columns = [column_ranks(key, eye) for key in ys]
    for i in range(2):
        columns_ref[i] = jnp.broadcast_to(columns[i], (CAP, META))
    best_ref[...] = own_best[...]
    for i, query in enumerate((own, x_first, x_second)):
        ranks = row_ranks(query)
        if i == 0:
            best = own_best[0:1, :CAP]
        else:
            best = earlier_best(query, ranks, own, own_columns[:, 0:1])
            places_ref[16 * (i - 1) : 16 * i, :] = slot_places(query)
        for key, ranked in zip(ys, columns):
            best = jnp.maximum(best, earlier_best(query, ranks, key, ranked))
        best_ref[i : i + 1, :CAP] = best


def mid_kernel(own, y_first, y_second, x_far, own_columns, columns_ref, out_ref, places_ref):
    ranks = row_ranks(x_far)
    best = earlier_best(x_far, ranks, own, own_columns[:, 0:1])
    for i, key in enumerate((y_first, y_second)):
        best = jnp.maximum(best, earlier_best(x_far, ranks, key, columns_ref[i, :, 0:1]))
    out_ref[...] = jnp.full((8, CAPL), -1.0, jnp.float32)
    out_ref[0:1, :CAP] = best
    places_ref[...] = slot_places(x_far)


def far_kernel(
    own, x_first, x_second, y_first, y_second, x_far, y_far,
    own_places, near_ref, near_places, mid_ref, mid_places, out_ref,
):
    queries, keys = (own, x_first, x_second, x_far), (y_first, y_second, y_far)
    far_columns = column_ranks(y_far, make_eye())
    over = 0.0
    for block in queries + keys:
        tail = block[LAST:, CAPL - META : CAPL].astype(jnp.float32)
        over = jnp.maximum(over, tail[13:14, META - 1 :])
    over = jnp.where(over > NEVER, 1.0, 0.0)
    my_core, my_z = lax.axis_index("core"), lax.axis_index("z")
    my_x = 2 * lax.axis_index("xh") + lax.axis_index("xl")
    rows = []
    for i, query in enumerate(queries):
        best = earlier_best(query, row_ranks(query), y_far, far_columns)
        best = jnp.maximum(best, near_ref[i : i + 1, :CAP] if i < 3 else mid_ref[0:1, :CAP])
        best = jnp.concatenate([best, jnp.full((1, CAPL - CAP), -1.0, jnp.float32)], axis=1)
        rows.append(jnp.broadcast_to(best, (16, CAPL)))
    rows = jnp.concatenate(rows, axis=0)
    places = jnp.concatenate([own_places[...], near_places[...], mid_places[...]], axis=0)
    found = jnp.full((64, META), -1.0, jnp.float32)
    for part in range(CAPL // META):
        values = rows[:, part * META : (part + 1) * META]
        picked = jnp.take_along_axis(values, places & (META - 1), axis=1, mode="promise_in_bounds")
        found = jnp.where((places >> 7) == part, picked, found)
    found = found + OVER * over
    messages = GROUPS * 8
    row, column = iota((messages, messages), 0), iota((messages, messages), 1)
    core = row & 1
    away = my_z - ((row >> 2) & 7)
    steps = jnp.where(core == 0, away, -away) & 7
    x_away = signed(my_core, (row >> 5) + (row & 2) - my_x) & 3
    block = jnp.where(x_away == 2, 3, jnp.where(x_away == 3, 2, x_away))
    wanted = block * 16 + (core ^ my_core) * GROUPS + steps
    order = jnp.where(column == wanted, 1.0, 0.0).astype(jnp.bfloat16)
    out = dot(jnp.concatenate([order] * 3, axis=1), jnp.concatenate(split3(found), axis=0), ((1,), (0,)))
    for i in range(messages):
        out_ref[i] = out[i : i + 1, :]


def final_kernel(slot_ref, ans_ref, out_ref, flag_ref):
    target, within = slot_ref[0:1, :], slot_ref[1:2, :]
    one_hot = jnp.where(iota((META, ROWS), 0) == within, 1.0, 0.0).astype(jnp.bfloat16)
    groups = []
    for g in range(GROUPS):
        rows = [ans_ref[xl * 32 + g * 4 + i] for xl in range(2) for i in range(4)]
        groups.append(functools.reduce(jnp.maximum, rows))
    best = jnp.concatenate(groups, axis=0)
    got = pick_rows(best, one_hot)
    out_ref[...] = jnp.sum(jnp.where(iota((GROUPS, ROWS), 0) == target, got, 0.0), axis=0, keepdims=True)
    flag_ref[0] = jnp.where(jnp.max(best) > 0.5 * OVER, 1, 0).astype(jnp.int32)


def slow_path(arrived, target, within, live):
    def unpack(v):
        marks = v[ROUTED : ROUTED + 3 * GROUPS, :SLOTS].astype(jnp.float32).reshape(3, ROUTED)
        return v[:ROUTED], marks[0], 256.0 * marks[1] + marks[2]

    rows, ids, ranks = unpack(arrived)
    ring = ("y", "xl", "xh", "core")
    size = 32

    def step(_, carry):
        moving, best = carry
        key_rows, key_ids, key_ranks = unpack(moving)
        scores = dot(rows, key_rows, ((1,), (1,)))
        allowed = (
            (ids[:, None] == key_ids[None, :])
            & (key_ids[None, :] > 0)
            & (key_ranks[None, :] < ranks[:, None])
        )
        best = jnp.maximum(best, jnp.max(jnp.where(allowed, scores, -1.0), axis=1))
        moving = lax.ppermute(moving, ring, [(i, (i + 1) % size) for i in range(size)])
        return moving, best

    _, best = lax.fori_loop(0, size, step, (arrived, jnp.full((ROUTED,), -1.0, jnp.float32)))
    steps = signed(lax.axis_index("core"), lax.axis_index("z") - jnp.arange(GROUPS)) & (GROUPS - 1)
    answered = lax.all_to_all(best.reshape(GROUPS, SLOTS)[steps], "z", 0, 0, tiled=True)
    picked = answered[jnp.maximum(target, 0), jnp.minimum(within, SLOTS - 1)]
    return jnp.where(live, picked, 0.0)


def column_shift(steps):
    pairs = []
    for z in range(8):
        for core in range(2):
            to = (z + (steps if core == 0 else -steps)) % 8
            pairs.append((z * 2 + core, to * 2 + core))
    return pairs


def plane_shift(dx, dy):
    def flat(x, y, core):
        return ((y % 4 * 2 + x % 4 % 2) * 2 + x % 4 // 2) * 2 + core

    pairs = []
    for core in range(2):
        s = 1 if core == 0 else -1
        for x in range(4):
            for y in range(4):
                pairs.append((flat(x + s * dx, y + s * dy, core), flat(x, y, core)))
    return pairs


def body(embeddings, cluster_id, order_rank, row_count):
    f32, bf16, i32 = jnp.float32, jnp.bfloat16, jnp.int32
    shape = jax.ShapeDtypeStruct
    *pieces, slots = call(
        prep_kernel,
        tuple(shape((n * PIECE, META), bf16) for n in PIECES) + (shape((8, ROWS), i32),),
        row_count,
        embeddings,
        cluster_id.reshape(1, ROWS),
        order_rank.reshape(1, ROWS),
        smem=(0,),
    )
    send = lambda v, steps: lax.ppermute(v, COLUMN, column_shift(steps))
    two_four = send(pieces[2], 2)
    three, five, six = send(pieces[3], 3), send(pieces[4], 5), send(pieces[5], 6)
    four = send(two_four[PIECE:], 2)
    one, seven = send(pieces[1], 1), send(pieces[6], 7)
    arrived = call(
        collect_kernel,
        shape((ROUTED + MARKS, WIDTH), bf16),
        pieces[0],
        one,
        two_four,
        three,
        four,
        five,
        six,
        seven,
    )
    other = lax.ppermute(arrived, "core", [(0, 1), (1, 0)])
    first = call(
        first_kernel,
        (
            shape((CAP, WIDTH), bf16),
            shape((8, ROUTED), i32),
            shape((8, CAPL), f32),
            shape((8, META), f32),
        ),
        arrived,
    )
    block = call(compact_kernel, shape((CAP, WIDTH), bf16), other, *first)
    bring = lambda v, dx, dy: lax.ppermute(v, PLANE, plane_shift(dx, dy))
    x_first, y_first = bring(block, 1, 0), bring(block, 0, -1)
    best_shape, places_shape = shape((8, CAPL), f32), shape((16, META), i32)
    own_best, own_columns, own_places = call(
        own_kernel, (best_shape, shape((CAP, META), f32), places_shape), block
    )
    own, own_best = lax.optimization_barrier((block, own_best))
    x_second, y_second = bring(own, -1, 0), bring(own, 0, 1)
    x_far, y_far = bring(x_first, 1, 0), bring(y_first, 0, -1)
    near_blocks = (block, x_first, x_second, y_first, y_second)
    near, columns, near_places = call(
        near_kernel,
        (best_shape, shape((2, CAP, META), f32), shape((32, META), i32)),
        *near_blocks,
        own_best,
        own_columns,
        cost=8,
    )
    mid, mid_places = call(
        mid_kernel,
        (best_shape, places_shape),
        block,
        y_first,
        y_second,
        x_far,
        own_columns,
        columns,
        cost=3,
    )
    message = call(
        far_kernel,
        shape((64, 1, META), f32),
        *near_blocks,
        x_far,
        y_far,
        own_places,
        near,
        near_places,
        mid,
        mid_places,
        cost=4,
    )
    answer = lax.all_to_all(message, RETURN, split_axis=0, concat_axis=0, tiled=True)
    out, flag = call(final_kernel, (shape((1, ROWS), f32), shape((1,), i32)), slots, answer, smem_out=(1,))
    target, within = slots[0], slots[1]
    return lax.cond(
        flag[0] > 0,
        lambda: slow_path(arrived, target, within, target >= 0),
        lambda: out.reshape(ROWS),
    )


def solution(mesh):
    axes = ("y", "xl", "z", "xh", "core")
    fine = Mesh(mesh.devices.reshape(4, 2, 8, 2, 2), axes)
    return jax.shard_map(
        body,
        mesh=fine,
        in_specs=(P(axes, None), P(axes), P(axes), P(axes)),
        out_specs=P(axes),
        check_vma=False,
    )
```

```python
import functools

import jax
import jax.numpy as jnp
from jax import lax
from jax.experimental import pallas as pl
from jax.experimental.pallas import tpu as pltpu
from jax.sharding import Mesh, PartitionSpec as P

norm_eps = 1e-06
ROWS = 256
WIDTH = 768
META = 128
GROUPS = 8
SLOTS = 48
ROUTED = GROUPS * SLOTS
CAP = 304
HELD = CAP - 3
CAPL = 384
LAST = CAP - 16
NEVER = 512.0
CHUNKS = WIDTH // META
PIECE = CHUNKS * SLOTS + 16
MARKS = 32
PIECES = (1, 1, 2, 1, 1, 1, 1)
OVER = 100.0
VMEM_LIMIT = 50 * 1024 * 1024
PLANE = ("y", "xl", "xh", "core")
COLUMN = ("z", "core")
RETURN = ("xl", "z", "xh", "core")


def dot(a, b, contract):
    return lax.dot_general(a, b, (contract, ((), ())), preferred_element_type=jnp.float32)


def iota(shape, axis):
    return lax.broadcasted_iota(jnp.int32, shape, axis)


def split3(v):
    hi = v.astype(jnp.bfloat16)
    rest = v - hi.astype(jnp.float32)
    mid = rest.astype(jnp.bfloat16)
    low = (rest - mid.astype(jnp.float32)).astype(jnp.bfloat16)
    return hi, mid, low


def pick_rows(v, one_hot):
    n = v.shape[0]
    parts = dot(jnp.concatenate(split3(v), axis=0), one_hot, ((1,), (0,)))
    return (parts[:n] + parts[n : 2 * n]) + parts[2 * n :]


def call(kernel, out, *args, smem=(), smem_out=(), cost=1, scratch=()):
    space = lambda i, scalars: pl.BlockSpec(memory_space=pltpu.SMEM if i in scalars else pltpu.VMEM)
    out_specs = space(0, smem_out)
    if isinstance(out, tuple):
        out_specs = tuple(space(i, smem_out) for i in range(len(out)))
    return pl.pallas_call(
        kernel,
        out_shape=out,
        in_specs=[space(i, smem) for i in range(len(args))],
        out_specs=out_specs,
        scratch_shapes=list(scratch),
        cost_estimate=pl.CostEstimate(
            flops=2 * cost * CAP * CAP * WIDTH, bytes_accessed=4 * CAP * WIDTH, transcendentals=0
        ),
        compiler_params=pltpu.CompilerParams(vmem_limit_bytes=VMEM_LIMIT),
    )(*args)


def signed(core, value):
    return jnp.where(core == 0, value, -value)


def slot_kernel(both_ref, where_ref, marks_ref, slot_ref):
    ids, ranks = both_ref[...] & 15, both_ref[...] >> 4
    target = ids & (GROUPS - 1)
    chosen = jnp.where(iota((GROUPS, ROWS), 0) == target, 1.0, 0.0)
    upper = jnp.where(iota((ROWS, ROWS), 0) < iota((ROWS, ROWS), 1), 1.0, 0.0).astype(jnp.bfloat16)
    before = dot(chosen.astype(jnp.bfloat16), upper, ((1,), (0,)))
    within = jnp.sum(before * chosen, axis=0, keepdims=True).astype(jnp.int32)
    steps = signed(lax.axis_index("core"), target - lax.axis_index("z")) & (GROUPS - 1)
    at = jnp.where(steps == 3, 4, jnp.where(steps == 4, 3, steps))
    slot = jnp.where(within < SLOTS, at * SLOTS + within, -1)
    where_ref[...] = jnp.where(iota((ROUTED, ROWS), 0) == slot, 1.0, 0.0).astype(jnp.bfloat16)
    high = ranks >> 8
    row = iota((16, ROWS), 0)
    meta = jnp.where(
        row == 0, ids + 1, jnp.where(row == 1, high, jnp.where(row == 2, ranks - (high << 8), 0))
    )
    marks_ref[...] = meta.astype(jnp.float32).astype(jnp.bfloat16)
    slot_ref[0:1, :] = target
    slot_ref[1:2, :] = within
    slot_ref[2:8, :] = jnp.zeros((6, ROWS), jnp.int32)


def piece_kernel(count_ref, emb_ref, where_ref, marks_ref, slot_ref, *refs):
    *out_refs, live_slot_ref = refs
    live = iota((1, ROWS), 1) < count_ref[0]
    live_slot_ref[0:1, :] = jnp.where(live, slot_ref[0:1, :], -1)
    live_slot_ref[1:8, :] = slot_ref[1:8, :]
    x = emb_ref[...].astype(jnp.float32)
    unit = x * lax.rsqrt(jnp.sum(x * x, axis=1, keepdims=True) + norm_eps)
    unit = jnp.where(iota((ROWS, 1), 0) < count_ref[0], unit, 0.0).astype(jnp.bfloat16)
    where_to = where_ref[...]
    rows = dot(where_to, unit, ((1,), (0,))).astype(jnp.bfloat16)
    meta = jnp.where(live, marks_ref[...].astype(jnp.float32), 0.0).astype(jnp.bfloat16)
    marks = dot(meta, where_to, ((1,), (1,)))
    at = 0
    for ref in out_refs:
        for first in range(0, ref.shape[0], PIECE):
            for i in range(CHUNKS):
                ref[first + i * SLOTS : first + (i + 1) * SLOTS, :] = rows[
                    at : at + SLOTS, i * META : (i + 1) * META
                ]
            tail = jnp.concatenate(
                [marks[:, at : at + SLOTS], jnp.zeros((16, META - SLOTS), jnp.float32)], axis=1
            )
            ref[first + CHUNKS * SLOTS : first + PIECE, :] = tail.astype(jnp.bfloat16)
            at += SLOTS


def collect_kernel(*refs):
    out_ref = refs[-1]
    marks = []
    for j, ref in enumerate(refs[:-1]):
        for i in range(CHUNKS):
            out_ref[j * SLOTS : (j + 1) * SLOTS, i * META : (i + 1) * META] = ref[
                i * SLOTS : (i + 1) * SLOTS, :
            ]
        marks.append(ref[CHUNKS * SLOTS : PIECE, :].astype(jnp.float32))
    by_kind = [mark[i : i + 1, :] for i in range(3) for mark in marks]
    kinds = jnp.concatenate(by_kind + [jnp.zeros((MARKS - 3 * GROUPS, META), jnp.float32)], axis=0)
    out_ref[ROUTED:, :META] = kinds.astype(jnp.bfloat16)
    out_ref[ROUTED:, META:] = jnp.zeros((MARKS, WIDTH - META), jnp.bfloat16)


def slot_fold(both):
    slot = iota((both, META), 0)
    slot = slot - SLOTS * ((slot * 1366) >> 16)
    return jnp.where(slot == iota((both, META), 1), 1.0, 0.0).astype(jnp.bfloat16)


def place_rows(arrived_ref, first):
    marks = arrived_ref[ROUTED:, :META]
    spread = dot(marks, slot_fold(ROUTED), ((1,), (1,)))
    here = iota((GROUPS, ROUTED), 0) == ((iota((GROUPS, ROUTED), 1) * 1366) >> 16)
    meta = [
        jnp.sum(jnp.where(here, spread[GROUPS * i : GROUPS * (i + 1), :], 0.0), axis=0, keepdims=True)
        for i in range(3)
    ]
    mine = lax.axis_index("z") + GROUPS * lax.axis_index("core") + 1
    ones = jnp.where(meta[0] == mine.astype(jnp.float32), 1.0, 0.0)
    chunks = [ones[:, i : i + META] for i in range(0, ROUTED, META)]
    upper = jnp.where(iota((META, META), 0) < iota((META, META), 1), 1.0, 0.0).astype(jnp.bfloat16)
    stacked = jnp.concatenate(chunks + [jnp.zeros((8 - len(chunks), META), jnp.float32)], axis=0)
    before = dot(stacked.astype(jnp.bfloat16), upper, ((1,), (0,)))
    total, counted = first, []
    for i, chunk in enumerate(chunks):
        counted.append(jnp.where(chunk > 0.5, before[i : i + 1, :] + total, -1.0))
        total = total + jnp.sum(chunk, axis=1, keepdims=True)
    pos = jnp.concatenate(counted, axis=1).astype(jnp.int32)
    where_to = jnp.where((iota((CAPL, ROUTED), 0) == pos) & (pos < HELD), 1.0, 0.0).astype(jnp.bfloat16)
    meta = jnp.concatenate(meta + [jnp.zeros((5, ROUTED), jnp.float32)], axis=0)
    ranks = dot(meta.astype(jnp.bfloat16), where_to, ((1,), (1,)))
    return pos, where_to, ranks, total


def first_kernel(own_ref, rows_ref, pos_ref, ranks_ref, total_ref):
    pos, where_to, ranks, total = place_rows(own_ref, jnp.zeros((1, 1), jnp.float32))
    rows_ref[...] = dot(where_to[:CAP, :], own_ref[:ROUTED, :], ((1,), (0,))).astype(jnp.bfloat16)
    pos_ref[...] = jnp.broadcast_to(pos, (8, ROUTED))
    ranks_ref[...] = ranks
    total_ref[...] = jnp.broadcast_to(total, (8, META))


def compact_kernel(other_ref, rows_ref, pos_ref, ranks_ref, total_ref, block_ref):
    other_pos, where_to, other_ranks, total = place_rows(other_ref, total_ref[0:1, 0:1])
    rows = dot(where_to[:CAP, :], other_ref[:ROUTED, :], ((1,), (0,))) + rows_ref[...].astype(jnp.float32)
    pos = jnp.concatenate([pos_ref[0:1, :], other_pos], axis=1)
    ranks = ranks_ref[...] + other_ranks
    lane = iota((1, CAPL), 1)
    filled = (lane.astype(jnp.float32) < total) & (lane < HELD)
    high = jnp.where(filled, ranks[1:2, :], NEVER)
    high = jnp.where((lane == CAPL - 1) & (total > HELD), 2 * NEVER, high)
    low = jnp.where(filled, ranks[2:3, :], 0.0)
    place = pos + 1
    marks = (jnp.concatenate([high, low], axis=1), (place >> 8).astype(jnp.float32), (place & 255).astype(jnp.float32))
    row = iota((16, WIDTH), 0)
    last = rows[LAST:, :]
    for i, mark in enumerate(marks):
        last = jnp.where(row == 13 + i, mark, last)
    block_ref[:LAST, :] = rows[:LAST, :].astype(jnp.bfloat16)
    block_ref[LAST:, :] = last.astype(jnp.bfloat16)


def row_ranks(block):
    tail = block[LAST:, :].astype(jnp.float32)
    return (256.0 * tail[13:14, :CAPL] + tail[13:14, CAPL:])[:, :CAP]


def column_ranks(block, eye):
    high = dot(eye, block[LAST:, :CAPL], ((1,), (1,)))
    low = dot(eye, block[LAST:, CAPL:], ((1,), (1,)))
    return 256.0 * high[:, 13:14] + low[:, 13:14]


def slot_places(block):
    both = 2 * ROUTED
    tail = block[LAST:, :].astype(jnp.float32)
    first = iota((16, both), 0) * SLOTS
    lane = iota((16, both), 1)
    here = (lane >= first) & (lane < first + SLOTS)
    parts = jnp.concatenate([jnp.where(here, tail[i : i + 1, :], 0.0) for i in (14, 15)], axis=0)
    folded = dot(parts.astype(jnp.bfloat16), slot_fold(both), ((1,), (0,)))
    return (256.0 * folded[:16] + folded[16:]).astype(jnp.int32) - 1


def make_eye():
    return jnp.where(iota((CAP, CAPL), 0) == iota((CAP, CAPL), 1), 1.0, 0.0).astype(jnp.bfloat16)


def earlier_best(query, query_ranks, key, key_ranks):
    scores = dot(key[...], query[...], ((1,), (1,)))
    return jnp.max(jnp.where(key_ranks < query_ranks, scores, -1.0), axis=0, keepdims=True)


def own_kernel(own, best_ref, columns_ref, places_ref):
    columns = column_ranks(own, make_eye())
    columns_ref[...] = jnp.broadcast_to(columns, (CAP, META))
    best_ref[...] = jnp.full((8, CAPL), -1.0, jnp.float32)
    best_ref[0:1, :CAP] = earlier_best(own, row_ranks(own), own, columns)
    places_ref[...] = slot_places(own)


def near_kernel(
    own, x_first, x_second, y_first, y_second, own_best, own_columns, best_ref, columns_ref, places_ref
):
    eye = make_eye()
    ys = (y_first, y_second)
    columns = [column_ranks(key, eye) for key in ys]
    for i in range(2):
        columns_ref[i] = jnp.broadcast_to(columns[i], (CAP, META))
    best_ref[...] = own_best[...]
    for i, query in enumerate((own, x_first, x_second)):
        ranks = row_ranks(query)
        if i == 0:
            best = own_best[0:1, :CAP]
        else:
            best = earlier_best(query, ranks, own, own_columns[:, 0:1])
            places_ref[16 * (i - 1) : 16 * i, :] = slot_places(query)
        for key, ranked in zip(ys, columns):
            best = jnp.maximum(best, earlier_best(query, ranks, key, ranked))
        best_ref[i : i + 1, :CAP] = best


def mid_kernel(own, y_first, y_second, x_far, own_columns, columns_ref, out_ref, places_ref):
    ranks = row_ranks(x_far)
    best = earlier_best(x_far, ranks, own, own_columns[:, 0:1])
    for i, key in enumerate((y_first, y_second)):
        best = jnp.maximum(best, earlier_best(x_far, ranks, key, columns_ref[i, :, 0:1]))
    out_ref[...] = jnp.full((8, CAPL), -1.0, jnp.float32)
    out_ref[0:1, :CAP] = best
    places_ref[...] = slot_places(x_far)


def far_kernel(
    own, x_first, x_second, y_first, y_second, x_far, y_far,
    own_places, near_ref, near_places, mid_ref, mid_places, out_ref,
):
    queries, keys = (own, x_first, x_second, x_far), (y_first, y_second, y_far)
    far_columns = column_ranks(y_far, make_eye())
    over = 0.0
    for block in queries + keys:
        tail = block[LAST:, CAPL - META : CAPL].astype(jnp.float32)
        over = jnp.maximum(over, tail[13:14, META - 1 :])
    over = jnp.where(over > NEVER, 1.0, 0.0)
    my_core, my_z = lax.axis_index("core"), lax.axis_index("z")
    my_x = 2 * lax.axis_index("xh") + lax.axis_index("xl")
    rows = []
    for i, query in enumerate(queries):
        best = earlier_best(query, row_ranks(query), y_far, far_columns)
        best = jnp.maximum(best, near_ref[i : i + 1, :CAP] if i < 3 else mid_ref[0:1, :CAP])
        best = jnp.concatenate([best, jnp.full((1, CAPL - CAP), -1.0, jnp.float32)], axis=1)
        rows.append(jnp.broadcast_to(best, (16, CAPL)))
    rows = jnp.concatenate(rows, axis=0)
    places = jnp.concatenate([own_places[...], near_places[...], mid_places[...]], axis=0)
    found = jnp.full((64, META), -1.0, jnp.float32)
    for part in range(CAPL // META):
        values = rows[:, part * META : (part + 1) * META]
        picked = jnp.take_along_axis(values, places & (META - 1), axis=1, mode="promise_in_bounds")
        found = jnp.where((places >> 7) == part, picked, found)
    found = found + OVER * over
    messages = GROUPS * 8
    row, column = iota((messages, messages), 0), iota((messages, messages), 1)
    core = row & 1
    away = my_z - ((row >> 2) & 7)
    steps = jnp.where(core == 0, away, -away) & 7
    x_away = signed(my_core, (row >> 5) + (row & 2) - my_x) & 3
    block = jnp.where(x_away == 2, 3, jnp.where(x_away == 3, 2, x_away))
    wanted = block * 16 + (core ^ my_core) * GROUPS + steps
    order = jnp.where(column == wanted, 1.0, 0.0).astype(jnp.bfloat16)
    out = dot(jnp.concatenate([order] * 3, axis=1), jnp.concatenate(split3(found), axis=0), ((1,), (0,)))
    for i in range(messages):
        out_ref[i] = out[i : i + 1, :]


def final_kernel(slot_ref, ans_ref, out_ref, flag_ref):
    target, within = slot_ref[0:1, :], slot_ref[1:2, :]
    one_hot = jnp.where(iota((META, ROWS), 0) == within, 1.0, 0.0).astype(jnp.bfloat16)
    groups = []
    for g in range(GROUPS):
        rows = [ans_ref[xl * 32 + g * 4 + i] for xl in range(2) for i in range(4)]
        groups.append(functools.reduce(jnp.maximum, rows))
    best = jnp.concatenate(groups, axis=0)
    got = pick_rows(best, one_hot)
    out_ref[...] = jnp.sum(jnp.where(iota((GROUPS, ROWS), 0) == target, got, 0.0), axis=0, keepdims=True)
    flag_ref[0] = jnp.where(jnp.max(best) > 0.5 * OVER, 1, 0).astype(jnp.int32)


def slow_path(arrived, target, within, live):
    def unpack(v):
        marks = v[ROUTED : ROUTED + 3 * GROUPS, :SLOTS].astype(jnp.float32).reshape(3, ROUTED)
        return v[:ROUTED], marks[0], 256.0 * marks[1] + marks[2]

    rows, ids, ranks = unpack(arrived)
    ring = ("y", "xl", "xh", "core")
    size = 32

    def step(_, carry):
        moving, best = carry
        key_rows, key_ids, key_ranks = unpack(moving)
        scores = dot(rows, key_rows, ((1,), (1,)))
        allowed = (
            (ids[:, None] == key_ids[None, :])
            & (key_ids[None, :] > 0)
            & (key_ranks[None, :] < ranks[:, None])
        )
        best = jnp.maximum(best, jnp.max(jnp.where(allowed, scores, -1.0), axis=1))
        moving = lax.ppermute(moving, ring, [(i, (i + 1) % size) for i in range(size)])
        return moving, best

    _, best = lax.fori_loop(0, size, step, (arrived, jnp.full((ROUTED,), -1.0, jnp.float32)))
    steps = signed(lax.axis_index("core"), lax.axis_index("z") - jnp.arange(GROUPS)) & (GROUPS - 1)
    answered = lax.all_to_all(best.reshape(GROUPS, SLOTS)[steps], "z", 0, 0, tiled=True)
    picked = answered[jnp.maximum(target, 0), jnp.minimum(within, SLOTS - 1)]
    return jnp.where(live, picked, 0.0)


def column_shift(steps):
    pairs = []
    for z in range(8):
        for core in range(2):
            to = (z + (steps if core == 0 else -steps)) % 8
            pairs.append((z * 2 + core, to * 2 + core))
    return pairs


def plane_shift(dx, dy):
    def flat(x, y, core):
        return ((y % 4 * 2 + x % 4 % 2) * 2 + x % 4 // 2) * 2 + core

    pairs = []
    for core in range(2):
        s = 1 if core == 0 else -1
        for x in range(4):
            for y in range(4):
                pairs.append((flat(x + s * dx, y + s * dy, core), flat(x, y, core)))
    return pairs


def body(embeddings, cluster_id, order_rank, row_count):
    f32, bf16, i32 = jnp.float32, jnp.bfloat16, jnp.int32
    shape = jax.ShapeDtypeStruct
    slots_shape = shape((8, ROWS), i32)
    where_to, marks, slots = call(
        slot_kernel,
        (shape((ROUTED, ROWS), bf16), shape((16, ROWS), bf16), slots_shape),
        (cluster_id + 16 * order_rank).reshape(1, ROWS),
    )
    *pieces, slots = call(
        piece_kernel,
        tuple(shape((n * PIECE, META), bf16) for n in PIECES) + (slots_shape,),
        row_count,
        embeddings,
        where_to,
        marks,
        slots,
        smem=(0,),
    )
    send = lambda v, steps: lax.ppermute(v, COLUMN, column_shift(steps))
    two_four = send(pieces[2], 2)
    three, five, six = send(pieces[3], 3), send(pieces[4], 5), send(pieces[5], 6)
    four = send(two_four[PIECE:], 2)
    one, seven = send(pieces[1], 1), send(pieces[6], 7)
    arrived = call(
        collect_kernel,
        shape((ROUTED + MARKS, WIDTH), bf16),
        pieces[0],
        one,
        two_four,
        three,
        four,
        five,
        six,
        seven,
    )
    other = lax.ppermute(arrived, "core", [(0, 1), (1, 0)])
    first = call(
        first_kernel,
        (
            shape((CAP, WIDTH), bf16),
            shape((8, ROUTED), i32),
            shape((8, CAPL), f32),
            shape((8, META), f32),
        ),
        arrived,
    )
    block = call(compact_kernel, shape((CAP, WIDTH), bf16), other, *first)
    bring = lambda v, dx, dy: lax.ppermute(v, PLANE, plane_shift(dx, dy))
    x_first, y_first = bring(block, 1, 0), bring(block, 0, -1)
    best_shape, places_shape = shape((8, CAPL), f32), shape((16, META), i32)
    own_best, own_columns, own_places = call(
        own_kernel, (best_shape, shape((CAP, META), f32), places_shape), block
    )
    own, own_best = lax.optimization_barrier((block, own_best))
    x_second, y_second = bring(own, -1, 0), bring(own, 0, 1)
    x_far, y_far = bring(x_first, 1, 0), bring(y_first, 0, -1)
    near_blocks = (block, x_first, x_second, y_first, y_second)
    near, columns, near_places = call(
        near_kernel,
        (best_shape, shape((2, CAP, META), f32), shape((32, META), i32)),
        *near_blocks,
        own_best,
        own_columns,
        cost=8,
    )
    mid, mid_places = call(
        mid_kernel,
        (best_shape, places_shape),
        block,
        y_first,
        y_second,
        x_far,
        own_columns,
        columns,
        cost=3,
    )
    message = call(
        far_kernel,
        shape((64, 1, META), f32),
        *near_blocks,
        x_far,
        y_far,
        own_places,
        near,
        near_places,
        mid,
        mid_places,
        cost=4,
    )
    answer = lax.all_to_all(message, RETURN, split_axis=0, concat_axis=0, tiled=True)
    out, flag = call(final_kernel, (shape((1, ROWS), f32), shape((1,), i32)), slots, answer, smem_out=(1,))
    target, within = slots[0], slots[1]
    return lax.cond(
        flag[0] > 0,
        lambda: slow_path(arrived, target, within, target >= 0),
        lambda: out.reshape(ROWS),
    )


def solution(mesh):
    axes = ("y", "xl", "z", "xh", "core")
    fine = Mesh(mesh.devices.reshape(4, 2, 8, 2, 2), axes)
    return jax.shard_map(
        body,
        mesh=fine,
        in_specs=(P(axes, None), P(axes), P(axes), P(axes)),
        out_specs=P(axes),
        check_vma=False,
    )
```

```python
import functools

import jax
import jax.numpy as jnp
from jax import lax
from jax.experimental import pallas as pl
from jax.experimental.pallas import tpu as pltpu
from jax.sharding import Mesh, PartitionSpec as P

norm_eps = 1e-06
ROWS = 256
WIDTH = 768
META = 128
GROUPS = 8
SLOTS = 48
ROUTED = GROUPS * SLOTS
CAP = 304
HELD = CAP - 3
CAPL = 384
LAST = CAP - 16
NEVER = 512.0
CHUNKS = WIDTH // META
PIECE = CHUNKS * SLOTS + 16
MARKS = 32
PIECES = (1, 1, 2, 1, 1, 1, 1)
OVER = 100.0
VMEM_LIMIT = 50 * 1024 * 1024
PLANE = ("y", "xl", "xh", "core")
COLUMN = ("z", "core")
RETURN = ("xl", "z", "xh", "core")


def dot(a, b, contract):
    return lax.dot_general(a, b, (contract, ((), ())), preferred_element_type=jnp.float32)


def iota(shape, axis):
    return lax.broadcasted_iota(jnp.int32, shape, axis)


def split3(v):
    hi = v.astype(jnp.bfloat16)
    rest = v - hi.astype(jnp.float32)
    mid = rest.astype(jnp.bfloat16)
    low = (rest - mid.astype(jnp.float32)).astype(jnp.bfloat16)
    return hi, mid, low


def pick_rows(v, one_hot):
    n = v.shape[0]
    parts = dot(jnp.concatenate(split3(v), axis=0), one_hot, ((1,), (0,)))
    return (parts[:n] + parts[n : 2 * n]) + parts[2 * n :]


def call(kernel, out, *args, smem=(), smem_out=(), cost=1, scratch=()):
    space = lambda i, scalars: pl.BlockSpec(memory_space=pltpu.SMEM if i in scalars else pltpu.VMEM)
    out_specs = space(0, smem_out)
    if isinstance(out, tuple):
        out_specs = tuple(space(i, smem_out) for i in range(len(out)))
    return pl.pallas_call(
        kernel,
        out_shape=out,
        in_specs=[space(i, smem) for i in range(len(args))],
        out_specs=out_specs,
        scratch_shapes=list(scratch),
        cost_estimate=pl.CostEstimate(
            flops=2 * cost * CAP * CAP * WIDTH, bytes_accessed=4 * CAP * WIDTH, transcendentals=0
        ),
        compiler_params=pltpu.CompilerParams(vmem_limit_bytes=VMEM_LIMIT),
    )(*args)


def signed(core, value):
    return jnp.where(core == 0, value, -value)


def slot_kernel(both_ref, where_ref, marks_ref, slot_ref):
    ids, ranks = both_ref[...] & 15, both_ref[...] >> 4
    target = ids & (GROUPS - 1)
    chosen = jnp.where(iota((GROUPS, ROWS), 0) == target, 1.0, 0.0)
    upper = jnp.where(iota((ROWS, ROWS), 0) < iota((ROWS, ROWS), 1), 1.0, 0.0).astype(jnp.bfloat16)
    before = dot(chosen.astype(jnp.bfloat16), upper, ((1,), (0,)))
    within = jnp.sum(before * chosen, axis=0, keepdims=True).astype(jnp.int32)
    steps = signed(lax.axis_index("core"), target - lax.axis_index("z")) & (GROUPS - 1)
    at = jnp.where(steps == 3, 4, jnp.where(steps == 4, 3, steps))
    slot = jnp.where(within < SLOTS, at * SLOTS + within, -1)
    where_ref[...] = jnp.where(iota((ROUTED, ROWS), 0) == slot, 1.0, 0.0).astype(jnp.bfloat16)
    high = ranks >> 8
    row = iota((16, ROWS), 0)
    meta = jnp.where(
        row == 0, ids + 1, jnp.where(row == 1, high, jnp.where(row == 2, ranks - (high << 8), 0))
    )
    marks_ref[...] = meta.astype(jnp.float32).astype(jnp.bfloat16)
    slot_ref[0:1, :] = target
    slot_ref[1:2, :] = within
    slot_ref[2:8, :] = jnp.zeros((6, ROWS), jnp.int32)


def piece_kernel(count_ref, emb_ref, where_ref, marks_ref, slot_ref, *refs):
    *out_refs, live_slot_ref = refs
    live = iota((1, ROWS), 1) < count_ref[0]
    live_slot_ref[0:1, :] = jnp.where(live, slot_ref[0:1, :], -1)
    live_slot_ref[1:8, :] = slot_ref[1:8, :]
    x = emb_ref[...].astype(jnp.float32)
    unit = x * lax.rsqrt(jnp.sum(x * x, axis=1, keepdims=True) + norm_eps)
    unit = jnp.where(iota((ROWS, 1), 0) < count_ref[0], unit, 0.0).astype(jnp.bfloat16)
    where_to = where_ref[...]
    rows = dot(where_to, unit, ((1,), (0,))).astype(jnp.bfloat16)
    meta = jnp.where(live, marks_ref[...].astype(jnp.float32), 0.0).astype(jnp.bfloat16)
    marks = dot(meta, where_to, ((1,), (1,)))
    at = 0
    for ref in out_refs:
        for first in range(0, ref.shape[0], PIECE):
            for i in range(CHUNKS):
                ref[first + i * SLOTS : first + (i + 1) * SLOTS, :] = rows[
                    at : at + SLOTS, i * META : (i + 1) * META
                ]
            tail = jnp.concatenate(
                [marks[:, at : at + SLOTS], jnp.zeros((16, META - SLOTS), jnp.float32)], axis=1
            )
            ref[first + CHUNKS * SLOTS : first + PIECE, :] = tail.astype(jnp.bfloat16)
            at += SLOTS


def collect_kernel(*refs):
    out_ref = refs[-1]
    marks = []
    for j, ref in enumerate(refs[:-1]):
        for i in range(CHUNKS):
            out_ref[j * SLOTS : (j + 1) * SLOTS, i * META : (i + 1) * META] = ref[
                i * SLOTS : (i + 1) * SLOTS, :
            ]
        marks.append(ref[CHUNKS * SLOTS : PIECE, :].astype(jnp.float32))
    by_kind = [mark[i : i + 1, :] for i in range(3) for mark in marks]
    kinds = jnp.concatenate(by_kind + [jnp.zeros((MARKS - 3 * GROUPS, META), jnp.float32)], axis=0)
    out_ref[ROUTED:, :META] = kinds.astype(jnp.bfloat16)
    out_ref[ROUTED:, META:] = jnp.zeros((MARKS, WIDTH - META), jnp.bfloat16)


def slot_fold(both):
    slot = iota((both, META), 0)
    slot = slot - SLOTS * ((slot * 1366) >> 16)
    return jnp.where(slot == iota((both, META), 1), 1.0, 0.0).astype(jnp.bfloat16)


def place_rows(arrived_ref, first):
    marks = arrived_ref[ROUTED:, :META]
    spread = dot(marks, slot_fold(ROUTED), ((1,), (1,)))
    here = iota((GROUPS, ROUTED), 0) == ((iota((GROUPS, ROUTED), 1) * 1366) >> 16)
    meta = [
        jnp.sum(jnp.where(here, spread[GROUPS * i : GROUPS * (i + 1), :], 0.0), axis=0, keepdims=True)
        for i in range(3)
    ]
    mine = lax.axis_index("z") + GROUPS * lax.axis_index("core") + 1
    ones = jnp.where(meta[0] == mine.astype(jnp.float32), 1.0, 0.0)
    chunks = [ones[:, i : i + META] for i in range(0, ROUTED, META)]
    upper = jnp.where(iota((META, META), 0) < iota((META, META), 1), 1.0, 0.0).astype(jnp.bfloat16)
    stacked = jnp.concatenate(chunks + [jnp.zeros((8 - len(chunks), META), jnp.float32)], axis=0)
    before = dot(stacked.astype(jnp.bfloat16), upper, ((1,), (0,)))
    total, counted = first, []
    for i, chunk in enumerate(chunks):
        counted.append(jnp.where(chunk > 0.5, before[i : i + 1, :] + total, -1.0))
        total = total + jnp.sum(chunk, axis=1, keepdims=True)
    pos = jnp.concatenate(counted, axis=1).astype(jnp.int32)
    where_to = jnp.where((iota((CAPL, ROUTED), 0) == pos) & (pos < HELD), 1.0, 0.0).astype(jnp.bfloat16)
    meta = jnp.concatenate(meta + [jnp.zeros((5, ROUTED), jnp.float32)], axis=0)
    ranks = dot(meta.astype(jnp.bfloat16), where_to, ((1,), (1,)))
    return pos, where_to, ranks, total


def first_kernel(own_ref, rows_ref, pos_ref, ranks_ref, total_ref):
    pos, where_to, ranks, total = place_rows(own_ref, jnp.zeros((1, 1), jnp.float32))
    rows_ref[...] = dot(where_to[:CAP, :], own_ref[:ROUTED, :], ((1,), (0,))).astype(jnp.bfloat16)
    pos_ref[...] = jnp.broadcast_to(pos, (8, ROUTED))
    ranks_ref[...] = ranks
    total_ref[...] = jnp.broadcast_to(total, (8, META))


def compact_kernel(other_ref, rows_ref, pos_ref, ranks_ref, total_ref, block_ref):
    other_pos, where_to, other_ranks, total = place_rows(other_ref, total_ref[0:1, 0:1])
    rows = dot(where_to[:CAP, :], other_ref[:ROUTED, :], ((1,), (0,))) + rows_ref[...].astype(jnp.float32)
    pos = jnp.concatenate([pos_ref[0:1, :], other_pos], axis=1)
    ranks = ranks_ref[...] + other_ranks
    lane = iota((1, CAPL), 1)
    filled = (lane.astype(jnp.float32) < total) & (lane < HELD)
    high = jnp.where(filled, ranks[1:2, :], NEVER)
    high = jnp.where((lane == CAPL - 1) & (total > HELD), 2 * NEVER, high)
    low = jnp.where(filled, ranks[2:3, :], 0.0)
    place = pos + 1
    marks = (jnp.concatenate([high, low], axis=1), (place >> 8).astype(jnp.float32), (place & 255).astype(jnp.float32))
    row = iota((16, WIDTH), 0)
    last = rows[LAST:, :]
    for i, mark in enumerate(marks):
        last = jnp.where(row == 13 + i, mark, last)
    block_ref[:LAST, :] = rows[:LAST, :].astype(jnp.bfloat16)
    block_ref[LAST:, :] = last.astype(jnp.bfloat16)


def row_ranks(block):
    tail = block[LAST:, :].astype(jnp.float32)
    return (256.0 * tail[13:14, :CAPL] + tail[13:14, CAPL:])[:, :CAP]


def column_ranks(block, eye):
    high = dot(eye, block[LAST:, :CAPL], ((1,), (1,)))
    low = dot(eye, block[LAST:, CAPL:], ((1,), (1,)))
    return 256.0 * high[:, 13:14] + low[:, 13:14]


def slot_places(block):
    both = 2 * ROUTED
    tail = block[LAST:, :].astype(jnp.float32)
    first = iota((16, both), 0) * SLOTS
    lane = iota((16, both), 1)
    here = (lane >= first) & (lane < first + SLOTS)
    parts = jnp.concatenate([jnp.where(here, tail[i : i + 1, :], 0.0) for i in (14, 15)], axis=0)
    folded = dot(parts.astype(jnp.bfloat16), slot_fold(both), ((1,), (0,)))
    return (256.0 * folded[:16] + folded[16:]).astype(jnp.int32) - 1


def make_eye():
    return jnp.where(iota((CAP, CAPL), 0) == iota((CAP, CAPL), 1), 1.0, 0.0).astype(jnp.bfloat16)


def earlier_best(query, query_ranks, key, key_ranks):
    scores = dot(key[...], query[...], ((1,), (1,)))
    return jnp.max(jnp.where(key_ranks < query_ranks, scores, -1.0), axis=0, keepdims=True)


def own_kernel(own, best_ref, columns_ref, places_ref):
    columns = column_ranks(own, make_eye())
    columns_ref[...] = jnp.broadcast_to(columns, (CAP, META))
    best_ref[...] = jnp.full((8, CAPL), -1.0, jnp.float32)
    best_ref[0:1, :CAP] = earlier_best(own, row_ranks(own), own, columns)
    places_ref[...] = slot_places(own)


def near_kernel(
    own, x_first, x_second, y_first, y_second, own_best, own_columns, best_ref, columns_ref, places_ref
):
    eye = make_eye()
    ys = (y_first, y_second)
    columns = [column_ranks(key, eye) for key in ys]
    for i in range(2):
        columns_ref[i] = jnp.broadcast_to(columns[i], (CAP, META))
    best_ref[...] = own_best[...]
    for i, query in enumerate((own, x_first, x_second)):
        ranks = row_ranks(query)
        if i == 0:
            best = own_best[0:1, :CAP]
        else:
            best = earlier_best(query, ranks, own, own_columns[:, 0:1])
            places_ref[16 * (i - 1) : 16 * i, :] = slot_places(query)
        for key, ranked in zip(ys, columns):
            best = jnp.maximum(best, earlier_best(query, ranks, key, ranked))
        best_ref[i : i + 1, :CAP] = best


def overflow(blocks):
    over = jnp.zeros((1, 1), jnp.float32)
    for block in blocks:
        tail = block[LAST:, CAPL - META : CAPL].astype(jnp.float32)
        over = jnp.maximum(over, tail[13:14, META - 1 :])
    return jnp.where(over > NEVER, OVER, 0.0)


def message_order():
    my_core, my_z = lax.axis_index("core"), lax.axis_index("z")
    my_x = 2 * lax.axis_index("xh") + lax.axis_index("xl")
    messages = GROUPS * 8
    row, column = iota((messages, messages), 0), iota((messages, messages), 1)
    core = row & 1
    away = my_z - ((row >> 2) & 7)
    steps = jnp.where(core == 0, away, -away) & 7
    x_away = signed(my_core, (row >> 5) + (row & 2) - my_x) & 3
    block = jnp.where(x_away == 2, 3, jnp.where(x_away == 3, 2, x_away))
    wanted = block * 16 + (core ^ my_core) * GROUPS + steps
    return jnp.where(column == wanted, 1.0, 0.0).astype(jnp.bfloat16)


def mid_kernel(
    own, x_first, x_second, y_first, y_second, x_far, own_columns, columns_ref, own_places, near_places,
    out_ref, places_ref, order_ref, over_ref,
):
    ranks = row_ranks(x_far)
    best = earlier_best(x_far, ranks, own, own_columns[:, 0:1])
    for i, key in enumerate((y_first, y_second)):
        best = jnp.maximum(best, earlier_best(x_far, ranks, key, columns_ref[i, :, 0:1]))
    out_ref[...] = jnp.full((8, CAPL), -1.0, jnp.float32)
    out_ref[0:1, :CAP] = best
    places_ref[:16, :] = own_places[...]
    places_ref[16:48, :] = near_places[...]
    places_ref[48:, :] = slot_places(x_far)
    order_ref[...] = jnp.concatenate([message_order()] * 3, axis=1)
    over = overflow((own, x_first, x_second, y_first, y_second, x_far))
    over_ref[...] = jnp.broadcast_to(over, (8, META))


def far_kernel(
    own, x_first, x_second, x_far, y_far, near_ref, mid_ref, places_ref, order_ref, over_ref, out_ref
):
    far_columns = column_ranks(y_far, make_eye())
    over = jnp.maximum(overflow((y_far,)), over_ref[0:1, 0:1])
    rows = []
    for i, query in enumerate((own, x_first, x_second, x_far)):
        best = earlier_best(query, row_ranks(query), y_far, far_columns)
        best = jnp.maximum(best, near_ref[i : i + 1, :CAP] if i < 3 else mid_ref[0:1, :CAP])
        best = jnp.concatenate([best, jnp.full((1, CAPL - CAP), -1.0, jnp.float32)], axis=1)
        rows.append(jnp.broadcast_to(best, (16, CAPL)))
    rows = jnp.concatenate(rows, axis=0)
    places = places_ref[...]
    found = jnp.full((64, META), -1.0, jnp.float32)
    for part in range(CAPL // META):
        values = rows[:, part * META : (part + 1) * META]
        picked = jnp.take_along_axis(values, places & (META - 1), axis=1, mode="promise_in_bounds")
        found = jnp.where((places >> 7) == part, picked, found)
    out = dot(order_ref[...], jnp.concatenate(split3(found + over), axis=0), ((1,), (0,)))
    for i in range(GROUPS * 8):
        out_ref[i] = out[i : i + 1, :]


def final_kernel(slot_ref, ans_ref, out_ref, flag_ref):
    target, within = slot_ref[0:1, :], slot_ref[1:2, :]
    one_hot = jnp.where(iota((META, ROWS), 0) == within, 1.0, 0.0).astype(jnp.bfloat16)
    groups = []
    for g in range(GROUPS):
        rows = [ans_ref[xl * 32 + g * 4 + i] for xl in range(2) for i in range(4)]
        groups.append(functools.reduce(jnp.maximum, rows))
    best = jnp.concatenate(groups, axis=0)
    got = pick_rows(best, one_hot)
    out_ref[...] = jnp.sum(jnp.where(iota((GROUPS, ROWS), 0) == target, got, 0.0), axis=0, keepdims=True)
    flag_ref[0] = jnp.where(jnp.max(best) > 0.5 * OVER, 1, 0).astype(jnp.int32)


def slow_path(arrived, target, within, live):
    def unpack(v):
        marks = v[ROUTED : ROUTED + 3 * GROUPS, :SLOTS].astype(jnp.float32).reshape(3, ROUTED)
        return v[:ROUTED], marks[0], 256.0 * marks[1] + marks[2]

    rows, ids, ranks = unpack(arrived)
    ring = ("y", "xl", "xh", "core")
    size = 32

    def step(_, carry):
        moving, best = carry
        key_rows, key_ids, key_ranks = unpack(moving)
        scores = dot(rows, key_rows, ((1,), (1,)))
        allowed = (
            (ids[:, None] == key_ids[None, :])
            & (key_ids[None, :] > 0)
            & (key_ranks[None, :] < ranks[:, None])
        )
        best = jnp.maximum(best, jnp.max(jnp.where(allowed, scores, -1.0), axis=1))
        moving = lax.ppermute(moving, ring, [(i, (i + 1) % size) for i in range(size)])
        return moving, best

    _, best = lax.fori_loop(0, size, step, (arrived, jnp.full((ROUTED,), -1.0, jnp.float32)))
    steps = signed(lax.axis_index("core"), lax.axis_index("z") - jnp.arange(GROUPS)) & (GROUPS - 1)
    answered = lax.all_to_all(best.reshape(GROUPS, SLOTS)[steps], "z", 0, 0, tiled=True)
    picked = answered[jnp.maximum(target, 0), jnp.minimum(within, SLOTS - 1)]
    return jnp.where(live, picked, 0.0)


def column_shift(steps):
    pairs = []
    for z in range(8):
        for core in range(2):
            to = (z + (steps if core == 0 else -steps)) % 8
            pairs.append((z * 2 + core, to * 2 + core))
    return pairs


def plane_shift(dx, dy):
    def flat(x, y, core):
        return ((y % 4 * 2 + x % 4 % 2) * 2 + x % 4 // 2) * 2 + core

    pairs = []
    for core in range(2):
        s = 1 if core == 0 else -1
        for x in range(4):
            for y in range(4):
                pairs.append((flat(x + s * dx, y + s * dy, core), flat(x, y, core)))
    return pairs


def body(embeddings, cluster_id, order_rank, row_count):
    f32, bf16, i32 = jnp.float32, jnp.bfloat16, jnp.int32
    shape = jax.ShapeDtypeStruct
    slots_shape = shape((8, ROWS), i32)
    where_to, marks, slots = call(
        slot_kernel,
        (shape((ROUTED, ROWS), bf16), shape((16, ROWS), bf16), slots_shape),
        (cluster_id + 16 * order_rank).reshape(1, ROWS),
    )
    *pieces, slots = call(
        piece_kernel,
        tuple(shape((n * PIECE, META), bf16) for n in PIECES) + (slots_shape,),
        row_count,
        embeddings,
        where_to,
        marks,
        slots,
        smem=(0,),
    )
    send = lambda v, steps: lax.ppermute(v, COLUMN, column_shift(steps))
    two_four = send(pieces[2], 2)
    three, five, six = send(pieces[3], 3), send(pieces[4], 5), send(pieces[5], 6)
    four = send(two_four[PIECE:], 2)
    one, seven = send(pieces[1], 1), send(pieces[6], 7)
    arrived = call(
        collect_kernel,
        shape((ROUTED + MARKS, WIDTH), bf16),
        pieces[0],
        one,
        two_four,
        three,
        four,
        five,
        six,
        seven,
    )
    other = lax.ppermute(arrived, "core", [(0, 1), (1, 0)])
    first = call(
        first_kernel,
        (
            shape((CAP, WIDTH), bf16),
            shape((8, ROUTED), i32),
            shape((8, CAPL), f32),
            shape((8, META), f32),
        ),
        arrived,
    )
    block = call(compact_kernel, shape((CAP, WIDTH), bf16), other, *first)
    bring = lambda v, dx, dy: lax.ppermute(v, PLANE, plane_shift(dx, dy))
    x_first, y_first = bring(block, 1, 0), bring(block, 0, -1)
    best_shape, places_shape = shape((8, CAPL), f32), shape((16, META), i32)
    own_best, own_columns, own_places = call(
        own_kernel, (best_shape, shape((CAP, META), f32), places_shape), block
    )
    own, own_best = lax.optimization_barrier((block, own_best))
    x_second, y_second = bring(own, -1, 0), bring(own, 0, 1)
    x_far, y_far = bring(x_first, 1, 0), bring(y_first, 0, -1)
    near_blocks = (block, x_first, x_second, y_first, y_second)
    near, columns, near_places = call(
        near_kernel,
        (best_shape, shape((2, CAP, META), f32), shape((32, META), i32)),
        *near_blocks,
        own_best,
        own_columns,
        cost=8,
    )
    mid, places, order, over = call(
        mid_kernel,
        (best_shape, shape((64, META), i32), shape((64, 192), bf16), shape((8, META), f32)),
        *near_blocks,
        x_far,
        own_columns,
        columns,
        own_places,
        near_places,
        cost=3,
    )
    message = call(
        far_kernel,
        shape((64, 1, META), f32),
        *near_blocks[:3],
        x_far,
        y_far,
        near,
        mid,
        places,
        order,
        over,
        cost=4,
    )
    answer = lax.all_to_all(message, RETURN, split_axis=0, concat_axis=0, tiled=True)
    out, flag = call(final_kernel, (shape((1, ROWS), f32), shape((1,), i32)), slots, answer, smem_out=(1,))
    target, within = slots[0], slots[1]
    return lax.cond(
        flag[0] > 0,
        lambda: slow_path(arrived, target, within, target >= 0),
        lambda: out.reshape(ROWS),
    )


def solution(mesh):
    axes = ("y", "xl", "z", "xh", "core")
    fine = Mesh(mesh.devices.reshape(4, 2, 8, 2, 2), axes)
    return jax.shard_map(
        body,
        mesh=fine,
        in_specs=(P(axes, None), P(axes), P(axes), P(axes)),
        out_specs=P(axes),
        check_vma=False,
    )
```

```python
import functools

import jax
import jax.numpy as jnp
from jax import lax
from jax.experimental import pallas as pl
from jax.experimental.pallas import tpu as pltpu
from jax.sharding import Mesh, PartitionSpec as P

norm_eps = 1e-06
ROWS = 256
WIDTH = 768
META = 128
GROUPS = 8
SLOTS = 48
ROUTED = GROUPS * SLOTS
CAP = 304
HELD = CAP - 3
CAPL = 384
LAST = CAP - 16
NEVER = 512.0
CHUNKS = WIDTH // META
PIECE = CHUNKS * SLOTS + 16
MARKS = 32
PIECES = (1, 1, 2, 1, 1, 1, 1)
OVER = 100.0
VMEM_LIMIT = 50 * 1024 * 1024
PLANE = ("y", "xl", "xh", "core")
COLUMN = ("z", "core")
RETURN = ("xl", "z", "xh", "core")


def dot(a, b, contract):
    return lax.dot_general(a, b, (contract, ((), ())), preferred_element_type=jnp.float32)


def iota(shape, axis):
    return lax.broadcasted_iota(jnp.int32, shape, axis)


def split3(v):
    hi = v.astype(jnp.bfloat16)
    rest = v - hi.astype(jnp.float32)
    mid = rest.astype(jnp.bfloat16)
    low = (rest - mid.astype(jnp.float32)).astype(jnp.bfloat16)
    return hi, mid, low


def pick_rows(v, one_hot):
    n = v.shape[0]
    parts = dot(jnp.concatenate(split3(v), axis=0), one_hot, ((1,), (0,)))
    return (parts[:n] + parts[n : 2 * n]) + parts[2 * n :]


def call(kernel, out, *args, smem=(), smem_out=(), cost=1, scratch=()):
    space = lambda i, scalars: pl.BlockSpec(memory_space=pltpu.SMEM if i in scalars else pltpu.VMEM)
    out_specs = space(0, smem_out)
    if isinstance(out, tuple):
        out_specs = tuple(space(i, smem_out) for i in range(len(out)))
    return pl.pallas_call(
        kernel,
        out_shape=out,
        in_specs=[space(i, smem) for i in range(len(args))],
        out_specs=out_specs,
        scratch_shapes=list(scratch),
        cost_estimate=pl.CostEstimate(
            flops=2 * cost * CAP * CAP * WIDTH, bytes_accessed=4 * CAP * WIDTH, transcendentals=0
        ),
        compiler_params=pltpu.CompilerParams(vmem_limit_bytes=VMEM_LIMIT),
    )(*args)


def signed(core, value):
    return jnp.where(core == 0, value, -value)


def slot_kernel(both_ref, where_ref, marks_ref, slot_ref):
    ids, ranks = both_ref[...] & 15, both_ref[...] >> 4
    target = ids & (GROUPS - 1)
    chosen = jnp.where(iota((GROUPS, ROWS), 0) == target, 1.0, 0.0)
    upper = jnp.where(iota((ROWS, ROWS), 0) < iota((ROWS, ROWS), 1), 1.0, 0.0).astype(jnp.bfloat16)
    before = dot(chosen.astype(jnp.bfloat16), upper, ((1,), (0,)))
    within = jnp.sum(before * chosen, axis=0, keepdims=True).astype(jnp.int32)
    steps = signed(lax.axis_index("core"), target - lax.axis_index("z")) & (GROUPS - 1)
    at = jnp.where(steps == 3, 4, jnp.where(steps == 4, 3, steps))
    slot = jnp.where(within < SLOTS, at * SLOTS + within, -1)
    where_ref[...] = jnp.where(iota((ROUTED, ROWS), 0) == slot, 1.0, 0.0).astype(jnp.bfloat16)
    high = ranks >> 8
    row = iota((16, ROWS), 0)
    meta = jnp.where(
        row == 0, ids + 1, jnp.where(row == 1, high, jnp.where(row == 2, ranks - (high << 8), 0))
    )
    marks_ref[...] = meta.astype(jnp.float32).astype(jnp.bfloat16)
    slot_ref[0:1, :] = target
    slot_ref[1:2, :] = within
    slot_ref[2:8, :] = jnp.zeros((6, ROWS), jnp.int32)


def piece_kernel(count_ref, emb_ref, where_ref, marks_ref, slot_ref, *refs):
    *out_refs, live_slot_ref = refs
    live = iota((1, ROWS), 1) < count_ref[0]
    live_slot_ref[0:1, :] = jnp.where(live, slot_ref[0:1, :], -1)
    live_slot_ref[1:8, :] = slot_ref[1:8, :]
    x = emb_ref[...].astype(jnp.float32)
    unit = x * lax.rsqrt(jnp.sum(x * x, axis=1, keepdims=True) + norm_eps)
    unit = jnp.where(iota((ROWS, 1), 0) < count_ref[0], unit, 0.0).astype(jnp.bfloat16)
    where_to = where_ref[...]
    rows = dot(where_to, unit, ((1,), (0,))).astype(jnp.bfloat16)
    meta = jnp.where(live, marks_ref[...].astype(jnp.float32), 0.0).astype(jnp.bfloat16)
    marks = dot(meta, where_to, ((1,), (1,)))
    at = 0
    for ref in out_refs:
        for first in range(0, ref.shape[0], PIECE):
            for i in range(CHUNKS):
                ref[first + i * SLOTS : first + (i + 1) * SLOTS, :] = rows[
                    at : at + SLOTS, i * META : (i + 1) * META
                ]
            tail = jnp.concatenate(
                [marks[:, at : at + SLOTS], jnp.zeros((16, META - SLOTS), jnp.float32)], axis=1
            )
            ref[first + CHUNKS * SLOTS : first + PIECE, :] = tail.astype(jnp.bfloat16)
            at += SLOTS


def collect_kernel(*refs):
    out_ref = refs[-1]
    marks = []
    for j, ref in enumerate(refs[:-1]):
        for i in range(CHUNKS):
            out_ref[j * SLOTS : (j + 1) * SLOTS, i * META : (i + 1) * META] = ref[
                i * SLOTS : (i + 1) * SLOTS, :
            ]
        marks.append(ref[CHUNKS * SLOTS : PIECE, :].astype(jnp.float32))
    by_kind = [mark[i : i + 1, :] for i in range(3) for mark in marks]
    kinds = jnp.concatenate(by_kind + [jnp.zeros((MARKS - 3 * GROUPS, META), jnp.float32)], axis=0)
    out_ref[ROUTED:, :META] = kinds.astype(jnp.bfloat16)
    out_ref[ROUTED:, META:] = jnp.zeros((MARKS, WIDTH - META), jnp.bfloat16)


def slot_fold(both):
    slot = iota((both, META), 0)
    slot = slot - SLOTS * ((slot * 1366) >> 16)
    return jnp.where(slot == iota((both, META), 1), 1.0, 0.0).astype(jnp.bfloat16)


def place_rows(arrived_ref, first):
    marks = arrived_ref[ROUTED:, :META]
    spread = dot(marks, slot_fold(ROUTED), ((1,), (1,)))
    here = iota((GROUPS, ROUTED), 0) == ((iota((GROUPS, ROUTED), 1) * 1366) >> 16)
    meta = [
        jnp.sum(jnp.where(here, spread[GROUPS * i : GROUPS * (i + 1), :], 0.0), axis=0, keepdims=True)
        for i in range(3)
    ]
    mine = lax.axis_index("z") + GROUPS * lax.axis_index("core") + 1
    ones = jnp.where(meta[0] == mine.astype(jnp.float32), 1.0, 0.0)
    chunks = [ones[:, i : i + META] for i in range(0, ROUTED, META)]
    upper = jnp.where(iota((META, META), 0) < iota((META, META), 1), 1.0, 0.0).astype(jnp.bfloat16)
    stacked = jnp.concatenate(chunks + [jnp.zeros((8 - len(chunks), META), jnp.float32)], axis=0)
    before = dot(stacked.astype(jnp.bfloat16), upper, ((1,), (0,)))
    total, counted = first, []
    for i, chunk in enumerate(chunks):
        counted.append(jnp.where(chunk > 0.5, before[i : i + 1, :] + total, -1.0))
        total = total + jnp.sum(chunk, axis=1, keepdims=True)
    pos = jnp.concatenate(counted, axis=1).astype(jnp.int32)
    where_to = jnp.where((iota((CAPL, ROUTED), 0) == pos) & (pos < HELD), 1.0, 0.0).astype(jnp.bfloat16)
    meta = jnp.concatenate(meta + [jnp.zeros((5, ROUTED), jnp.float32)], axis=0)
    ranks = dot(meta.astype(jnp.bfloat16), where_to, ((1,), (1,)))
    return pos, where_to, ranks, total


def first_kernel(own_ref, rows_ref, pos_ref, ranks_ref, total_ref):
    pos, where_to, ranks, total = place_rows(own_ref, jnp.zeros((1, 1), jnp.float32))
    rows_ref[...] = dot(where_to[:CAP, :], own_ref[:ROUTED, :], ((1,), (0,))).astype(jnp.bfloat16)
    pos_ref[...] = jnp.broadcast_to(pos, (8, ROUTED))
    ranks_ref[...] = ranks
    total_ref[...] = jnp.broadcast_to(total, (8, META))


def compact_kernel(other_ref, rows_ref, pos_ref, ranks_ref, total_ref, block_ref):
    other_pos, where_to, other_ranks, total = place_rows(other_ref, total_ref[0:1, 0:1])
    rows = dot(where_to[:CAP, :], other_ref[:ROUTED, :], ((1,), (0,))) + rows_ref[...].astype(jnp.float32)
    pos = jnp.concatenate([pos_ref[0:1, :], other_pos], axis=1)
    ranks = ranks_ref[...] + other_ranks
    lane = iota((1, CAPL), 1)
    filled = (lane.astype(jnp.float32) < total) & (lane < HELD)
    high = jnp.where(filled, ranks[1:2, :], NEVER)
    high = jnp.where((lane == CAPL - 1) & (total > HELD), 2 * NEVER, high)
    low = jnp.where(filled, ranks[2:3, :], 0.0)
    place = pos + 1
    marks = (jnp.concatenate([high, low], axis=1), (place >> 8).astype(jnp.float32), (place & 255).astype(jnp.float32))
    row = iota((16, WIDTH), 0)
    last = rows[LAST:, :]
    for i, mark in enumerate(marks):
        last = jnp.where(row == 13 + i, mark, last)
    block_ref[:LAST, :] = rows[:LAST, :].astype(jnp.bfloat16)
    block_ref[LAST:, :] = last.astype(jnp.bfloat16)


def row_ranks(block):
    tail = block[LAST:, :].astype(jnp.float32)
    return (256.0 * tail[13:14, :CAPL] + tail[13:14, CAPL:])[:, :CAP]


def column_ranks(block, eye):
    high = dot(eye, block[LAST:, :CAPL], ((1,), (1,)))
    low = dot(eye, block[LAST:, CAPL:], ((1,), (1,)))
    return 256.0 * high[:, 13:14] + low[:, 13:14]


def slot_places(block):
    both = 2 * ROUTED
    tail = block[LAST:, :].astype(jnp.float32)
    first = iota((16, both), 0) * SLOTS
    lane = iota((16, both), 1)
    here = (lane >= first) & (lane < first + SLOTS)
    parts = jnp.concatenate([jnp.where(here, tail[i : i + 1, :], 0.0) for i in (14, 15)], axis=0)
    folded = dot(parts.astype(jnp.bfloat16), slot_fold(both), ((1,), (0,)))
    return (256.0 * folded[:16] + folded[16:]).astype(jnp.int32) - 1


def make_eye():
    return jnp.where(iota((CAP, CAPL), 0) == iota((CAP, CAPL), 1), 1.0, 0.0).astype(jnp.bfloat16)


def earlier_best(query, query_ranks, key, key_ranks):
    scores = dot(key[...], query[...], ((1,), (1,)))
    return jnp.max(jnp.where(key_ranks < query_ranks, scores, -1.0), axis=0, keepdims=True)


def own_kernel(own, best_ref, columns_ref, places_ref):
    columns = column_ranks(own, make_eye())
    columns_ref[...] = jnp.broadcast_to(columns, (CAP, META))
    best_ref[...] = jnp.full((8, CAPL), -1.0, jnp.float32)
    best_ref[0:1, :CAP] = earlier_best(own, row_ranks(own), own, columns)
    places_ref[...] = slot_places(own)


def near_kernel(
    own, x_first, x_second, y_first, y_second, own_best, own_columns, best_ref, columns_ref, places_ref
):
    eye = make_eye()
    ys = (y_first, y_second)
    columns = [column_ranks(key, eye) for key in ys]
    for i in range(2):
        columns_ref[i] = jnp.broadcast_to(columns[i], (CAP, META))
    best_ref[...] = own_best[...]
    for i, query in enumerate((own, x_first, x_second)):
        ranks = row_ranks(query)
        if i == 0:
            best = own_best[0:1, :CAP]
        else:
            best = earlier_best(query, ranks, own, own_columns[:, 0:1])
            places_ref[16 * (i - 1) : 16 * i, :] = slot_places(query)
        for key, ranked in zip(ys, columns):
            best = jnp.maximum(best, earlier_best(query, ranks, key, ranked))
        best_ref[i : i + 1, :CAP] = best


def mid_kernel(own, y_first, y_second, x_far, own_columns, columns_ref, out_ref, places_ref):
    ranks = row_ranks(x_far)
    best = earlier_best(x_far, ranks, own, own_columns[:, 0:1])
    for i, key in enumerate((y_first, y_second)):
        best = jnp.maximum(best, earlier_best(x_far, ranks, key, columns_ref[i, :, 0:1]))
    out_ref[...] = jnp.full((8, CAPL), -1.0, jnp.float32)
    out_ref[0:1, :CAP] = best
    places_ref[...] = slot_places(x_far)


def far_kernel(
    own, x_first, x_second, y_first, y_second, x_far, y_far,
    own_places, near_ref, near_places, mid_ref, mid_places, out_ref,
):
    queries, keys = (own, x_first, x_second, x_far), (y_first, y_second, y_far)
    far_columns = column_ranks(y_far, make_eye())
    over = 0.0
    for block in queries + keys:
        tail = block[LAST:, CAPL - META : CAPL].astype(jnp.float32)
        over = jnp.maximum(over, tail[13:14, META - 1 :])
    over = jnp.where(over > NEVER, 1.0, 0.0)
    my_core, my_z = lax.axis_index("core"), lax.axis_index("z")
    my_x = 2 * lax.axis_index("xh") + lax.axis_index("xl")
    rows = []
    for i, query in enumerate(queries):
        best = earlier_best(query, row_ranks(query), y_far, far_columns)
        best = jnp.maximum(best, near_ref[i : i + 1, :CAP] if i < 3 else mid_ref[0:1, :CAP])
        best = jnp.concatenate([best, jnp.full((1, CAPL - CAP), -1.0, jnp.float32)], axis=1)
        rows.append(jnp.broadcast_to(best, (16, CAPL)))
    rows = jnp.concatenate(rows, axis=0)
    places = jnp.concatenate([own_places[...], near_places[...], mid_places[...]], axis=0)
    found = jnp.full((64, META), -1.0, jnp.float32)
    for part in range(CAPL // META):
        values = rows[:, part * META : (part + 1) * META]
        picked = jnp.take_along_axis(values, places & (META - 1), axis=1, mode="promise_in_bounds")
        found = jnp.where((places >> 7) == part, picked, found)
    found = found + OVER * over
    messages = GROUPS * 8
    row, column = iota((messages, messages), 0), iota((messages, messages), 1)
    core = row & 1
    away = my_z - ((row >> 2) & 7)
    steps = jnp.where(core == 0, away, -away) & 7
    x_away = signed(my_core, my_x - (row >> 5) - (row & 2)) & 3
    block = jnp.where(x_away == 2, 3, jnp.where(x_away == 3, 2, x_away))
    wanted = block * 16 + (core ^ my_core) * GROUPS + steps
    order = jnp.where(column == wanted, 1.0, 0.0).astype(jnp.bfloat16)
    out = dot(jnp.concatenate([order] * 3, axis=1), jnp.concatenate(split3(found), axis=0), ((1,), (0,)))
    for i in range(messages):
        out_ref[i] = out[i : i + 1, :]


def final_kernel(slot_ref, ans_ref, out_ref, flag_ref):
    target, within = slot_ref[0:1, :], slot_ref[1:2, :]
    one_hot = jnp.where(iota((META, ROWS), 0) == within, 1.0, 0.0).astype(jnp.bfloat16)
    groups = []
    for g in range(GROUPS):
        rows = [ans_ref[xl * 32 + g * 4 + i] for xl in range(2) for i in range(4)]
        groups.append(functools.reduce(jnp.maximum, rows))
    best = jnp.concatenate(groups, axis=0)
    got = pick_rows(best, one_hot)
    out_ref[...] = jnp.sum(jnp.where(iota((GROUPS, ROWS), 0) == target, got, 0.0), axis=0, keepdims=True)
    flag_ref[0] = jnp.where(jnp.max(best) > 0.5 * OVER, 1, 0).astype(jnp.int32)


def slow_path(arrived, target, within, live):
    def unpack(v):
        marks = v[ROUTED : ROUTED + 3 * GROUPS, :SLOTS].astype(jnp.float32).reshape(3, ROUTED)
        return v[:ROUTED], marks[0], 256.0 * marks[1] + marks[2]

    rows, ids, ranks = unpack(arrived)
    ring = ("y", "xl", "xh", "core")
    size = 32

    def step(_, carry):
        moving, best = carry
        key_rows, key_ids, key_ranks = unpack(moving)
        scores = dot(rows, key_rows, ((1,), (1,)))
        allowed = (
            (ids[:, None] == key_ids[None, :])
            & (key_ids[None, :] > 0)
            & (key_ranks[None, :] < ranks[:, None])
        )
        best = jnp.maximum(best, jnp.max(jnp.where(allowed, scores, -1.0), axis=1))
        moving = lax.ppermute(moving, ring, [(i, (i + 1) % size) for i in range(size)])
        return moving, best

    _, best = lax.fori_loop(0, size, step, (arrived, jnp.full((ROUTED,), -1.0, jnp.float32)))
    steps = signed(lax.axis_index("core"), lax.axis_index("z") - jnp.arange(GROUPS)) & (GROUPS - 1)
    answered = lax.all_to_all(best.reshape(GROUPS, SLOTS)[steps], "z", 0, 0, tiled=True)
    picked = answered[jnp.maximum(target, 0), jnp.minimum(within, SLOTS - 1)]
    return jnp.where(live, picked, 0.0)


def column_shift(steps):
    pairs = []
    for z in range(8):
        for core in range(2):
            to = (z + (steps if core == 0 else -steps)) % 8
            pairs.append((z * 2 + core, to * 2 + core))
    return pairs


def plane_shift(dx, dy):
    def flat(x, y, core):
        return ((y % 4 * 2 + x % 4 % 2) * 2 + x % 4 // 2) * 2 + core

    pairs = []
    for core in range(2):
        s = 1 if core == 0 else -1
        for x in range(4):
            for y in range(4):
                pairs.append((flat(x + s * dx, y + s * dy, core), flat(x, y, core)))
    return pairs


def body(embeddings, cluster_id, order_rank, row_count):
    f32, bf16, i32 = jnp.float32, jnp.bfloat16, jnp.int32
    shape = jax.ShapeDtypeStruct
    slots_shape = shape((8, ROWS), i32)
    where_to, marks, slots = call(
        slot_kernel,
        (shape((ROUTED, ROWS), bf16), shape((16, ROWS), bf16), slots_shape),
        (cluster_id + 16 * order_rank).reshape(1, ROWS),
    )
    *pieces, slots = call(
        piece_kernel,
        tuple(shape((n * PIECE, META), bf16) for n in PIECES) + (slots_shape,),
        row_count,
        embeddings,
        where_to,
        marks,
        slots,
        smem=(0,),
    )
    send = lambda v, steps: lax.ppermute(v, COLUMN, column_shift(steps))
    two_four = send(pieces[2], 2)
    three, five, six = send(pieces[3], 3), send(pieces[4], 5), send(pieces[5], 6)
    four = send(two_four[PIECE:], 2)
    one, seven = send(pieces[1], 1), send(pieces[6], 7)
    arrived = call(
        collect_kernel,
        shape((ROUTED + MARKS, WIDTH), bf16),
        pieces[0],
        one,
        two_four,
        three,
        four,
        five,
        six,
        seven,
    )
    other = lax.ppermute(arrived, "core", [(0, 1), (1, 0)])
    first = call(
        first_kernel,
        (
            shape((CAP, WIDTH), bf16),
            shape((8, ROUTED), i32),
            shape((8, CAPL), f32),
            shape((8, META), f32),
        ),
        arrived,
    )
    block = call(compact_kernel, shape((CAP, WIDTH), bf16), other, *first)
    bring = lambda v, dx, dy: lax.ppermute(v, PLANE, plane_shift(dx, dy))
    x_first, y_first = bring(block, -1, 0), bring(block, 0, -1)
    best_shape, places_shape = shape((8, CAPL), f32), shape((16, META), i32)
    own_best, own_columns, own_places = call(
        own_kernel, (best_shape, shape((CAP, META), f32), places_shape), block
    )
    own, own_best = lax.optimization_barrier((block, own_best))
    x_second, y_second = bring(own, 1, 0), bring(own, 0, 1)
    x_far, y_far = bring(x_first, -1, 0), bring(y_first, 0, -1)
    near_blocks = (block, x_first, x_second, y_first, y_second)
    near, columns, near_places = call(
        near_kernel,
        (best_shape, shape((2, CAP, META), f32), shape((32, META), i32)),
        *near_blocks,
        own_best,
        own_columns,
        cost=8,
    )
    mid, mid_places = call(
        mid_kernel,
        (best_shape, places_shape),
        block,
        y_first,
        y_second,
        x_far,
        own_columns,
        columns,
        cost=3,
    )
    message = call(
        far_kernel,
        shape((64, 1, META), f32),
        *near_blocks,
        x_far,
        y_far,
        own_places,
        near,
        near_places,
        mid,
        mid_places,
        cost=4,
    )
    answer = lax.all_to_all(message, RETURN, split_axis=0, concat_axis=0, tiled=True)
    out, flag = call(final_kernel, (shape((1, ROWS), f32), shape((1,), i32)), slots, answer, smem_out=(1,))
    target, within = slots[0], slots[1]
    return lax.cond(
        flag[0] > 0,
        lambda: slow_path(arrived, target, within, target >= 0),
        lambda: out.reshape(ROWS),
    )


def solution(mesh):
    axes = ("y", "xl", "z", "xh", "core")
    fine = Mesh(mesh.devices.reshape(4, 2, 8, 2, 2), axes)
    return jax.shard_map(
        body,
        mesh=fine,
        in_specs=(P(axes, None), P(axes), P(axes), P(axes)),
        out_specs=P(axes),
        check_vma=False,
    )
```

```python
import functools

import jax
import jax.numpy as jnp
from jax import lax
from jax.experimental import pallas as pl
from jax.experimental.pallas import tpu as pltpu
from jax.sharding import Mesh, PartitionSpec as P

norm_eps = 1e-06
ROWS = 256
WIDTH = 768
META = 128
GROUPS = 8
SLOTS = 48
ROUTED = GROUPS * SLOTS
CAP = 304
HELD = CAP - 3
CAPL = 384
LAST = CAP - 16
NEVER = 512.0
CHUNKS = WIDTH // META
PIECE = CHUNKS * SLOTS + 16
MARKS = 32
PIECES = (1, 1, 2, 1, 1, 1, 1)
OVER = 100.0
VMEM_LIMIT = 50 * 1024 * 1024
PLANE = ("y", "xl", "xh", "core")
COLUMN = ("z", "core")
RETURN = ("xl", "z", "xh", "core")


def dot(a, b, contract):
    return lax.dot_general(a, b, (contract, ((), ())), preferred_element_type=jnp.float32)


def iota(shape, axis):
    return lax.broadcasted_iota(jnp.int32, shape, axis)


def split3(v):
    hi = v.astype(jnp.bfloat16)
    rest = v - hi.astype(jnp.float32)
    mid = rest.astype(jnp.bfloat16)
    low = (rest - mid.astype(jnp.float32)).astype(jnp.bfloat16)
    return hi, mid, low


def pick_rows(v, one_hot):
    n = v.shape[0]
    parts = dot(jnp.concatenate(split3(v), axis=0), one_hot, ((1,), (0,)))
    return (parts[:n] + parts[n : 2 * n]) + parts[2 * n :]


def call(kernel, out, *args, smem=(), smem_out=(), cost=1, scratch=()):
    space = lambda i, scalars: pl.BlockSpec(memory_space=pltpu.SMEM if i in scalars else pltpu.VMEM)
    out_specs = space(0, smem_out)
    if isinstance(out, tuple):
        out_specs = tuple(space(i, smem_out) for i in range(len(out)))
    return pl.pallas_call(
        kernel,
        out_shape=out,
        in_specs=[space(i, smem) for i in range(len(args))],
        out_specs=out_specs,
        scratch_shapes=list(scratch),
        cost_estimate=pl.CostEstimate(
            flops=2 * cost * CAP * CAP * WIDTH, bytes_accessed=4 * CAP * WIDTH, transcendentals=0
        ),
        compiler_params=pltpu.CompilerParams(vmem_limit_bytes=VMEM_LIMIT),
    )(*args)


def signed(core, value):
    return jnp.where(core == 0, value, -value)


def slot_kernel(both_ref, where_ref, marks_ref, slot_ref):
    ids, ranks = both_ref[...] & 15, both_ref[...] >> 4
    target = ids & (GROUPS - 1)
    chosen = jnp.where(iota((GROUPS, ROWS), 0) == target, 1.0, 0.0)
    upper = jnp.where(iota((ROWS, ROWS), 0) < iota((ROWS, ROWS), 1), 1.0, 0.0).astype(jnp.bfloat16)
    before = dot(chosen.astype(jnp.bfloat16), upper, ((1,), (0,)))
    within = jnp.sum(before * chosen, axis=0, keepdims=True).astype(jnp.int32)
    steps = signed(lax.axis_index("core"), target - lax.axis_index("z")) & (GROUPS - 1)
    at = jnp.where(steps == 3, 4, jnp.where(steps == 4, 3, steps))
    slot = jnp.where(within < SLOTS, at * SLOTS + within, -1)
    where_ref[...] = jnp.where(iota((ROUTED, ROWS), 0) == slot, 1.0, 0.0).astype(jnp.bfloat16)
    high = ranks >> 8
    row = iota((16, ROWS), 0)
    meta = jnp.where(
        row == 0, ids + 1, jnp.where(row == 1, high, jnp.where(row == 2, ranks - (high << 8), 0))
    )
    marks_ref[...] = meta.astype(jnp.float32).astype(jnp.bfloat16)
    slot_ref[0:1, :] = target
    slot_ref[1:2, :] = within
    slot_ref[2:8, :] = jnp.zeros((6, ROWS), jnp.int32)


def piece_kernel(count_ref, emb_ref, where_ref, marks_ref, slot_ref, *refs):
    *out_refs, live_slot_ref = refs
    live = iota((1, ROWS), 1) < count_ref[0]
    live_slot_ref[0:1, :] = jnp.where(live, slot_ref[0:1, :], -1)
    live_slot_ref[1:8, :] = slot_ref[1:8, :]
    x = emb_ref[...].astype(jnp.float32)
    unit = x * lax.rsqrt(jnp.sum(x * x, axis=1, keepdims=True) + norm_eps)
    unit = jnp.where(iota((ROWS, 1), 0) < count_ref[0], unit, 0.0).astype(jnp.bfloat16)
    where_to = where_ref[...]
    rows = dot(where_to, unit, ((1,), (0,))).astype(jnp.bfloat16)
    meta = jnp.where(live, marks_ref[...].astype(jnp.float32), 0.0).astype(jnp.bfloat16)
    marks = dot(meta, where_to, ((1,), (1,)))
    at = 0
    for ref in out_refs:
        for first in range(0, ref.shape[0], PIECE):
            for i in range(CHUNKS):
                ref[first + i * SLOTS : first + (i + 1) * SLOTS, :] = rows[
                    at : at + SLOTS, i * META : (i + 1) * META
                ]
            tail = jnp.concatenate(
                [marks[:, at : at + SLOTS], jnp.zeros((16, META - SLOTS), jnp.float32)], axis=1
            )
            ref[first + CHUNKS * SLOTS : first + PIECE, :] = tail.astype(jnp.bfloat16)
            at += SLOTS


def collect_kernel(*refs):
    out_ref = refs[-1]
    marks = []
    for j, ref in enumerate(refs[:-1]):
        for i in range(CHUNKS):
            out_ref[j * SLOTS : (j + 1) * SLOTS, i * META : (i + 1) * META] = ref[
                i * SLOTS : (i + 1) * SLOTS, :
            ]
        marks.append(ref[CHUNKS * SLOTS : PIECE, :].astype(jnp.float32))
    by_kind = [mark[i : i + 1, :] for i in range(3) for mark in marks]
    kinds = jnp.concatenate(by_kind + [jnp.zeros((MARKS - 3 * GROUPS, META), jnp.float32)], axis=0)
    out_ref[ROUTED:, :META] = kinds.astype(jnp.bfloat16)
    out_ref[ROUTED:, META:] = jnp.zeros((MARKS, WIDTH - META), jnp.bfloat16)


def slot_fold(both):
    slot = iota((both, META), 0)
    slot = slot - SLOTS * ((slot * 1366) >> 16)
    return jnp.where(slot == iota((both, META), 1), 1.0, 0.0).astype(jnp.bfloat16)


def place_rows(arrived_ref, first):
    marks = arrived_ref[ROUTED:, :META]
    spread = dot(marks, slot_fold(ROUTED), ((1,), (1,)))
    here = iota((GROUPS, ROUTED), 0) == ((iota((GROUPS, ROUTED), 1) * 1366) >> 16)
    meta = [
        jnp.sum(jnp.where(here, spread[GROUPS * i : GROUPS * (i + 1), :], 0.0), axis=0, keepdims=True)
        for i in range(3)
    ]
    mine = lax.axis_index("z") + GROUPS * lax.axis_index("core") + 1
    ones = jnp.where(meta[0] == mine.astype(jnp.float32), 1.0, 0.0)
    chunks = [ones[:, i : i + META] for i in range(0, ROUTED, META)]
    upper = jnp.where(iota((META, META), 0) < iota((META, META), 1), 1.0, 0.0).astype(jnp.bfloat16)
    stacked = jnp.concatenate(chunks + [jnp.zeros((8 - len(chunks), META), jnp.float32)], axis=0)
    before = dot(stacked.astype(jnp.bfloat16), upper, ((1,), (0,)))
    total, counted = first, []
    for i, chunk in enumerate(chunks):
        counted.append(jnp.where(chunk > 0.5, before[i : i + 1, :] + total, -1.0))
        total = total + jnp.sum(chunk, axis=1, keepdims=True)
    pos = jnp.concatenate(counted, axis=1).astype(jnp.int32)
    where_to = jnp.where((iota((CAPL, ROUTED), 0) == pos) & (pos < HELD), 1.0, 0.0).astype(jnp.bfloat16)
    meta = jnp.concatenate(meta + [jnp.zeros((5, ROUTED), jnp.float32)], axis=0)
    ranks = dot(meta.astype(jnp.bfloat16), where_to, ((1,), (1,)))
    return pos, where_to, ranks, total


def first_kernel(own_ref, rows_ref, pos_ref, ranks_ref, total_ref):
    pos, where_to, ranks, total = place_rows(own_ref, jnp.zeros((1, 1), jnp.float32))
    rows_ref[...] = dot(where_to[:CAP, :], own_ref[:ROUTED, :], ((1,), (0,))).astype(jnp.bfloat16)
    pos_ref[...] = jnp.broadcast_to(pos, (8, ROUTED))
    ranks_ref[...] = ranks
    total_ref[...] = jnp.broadcast_to(total, (8, META))


def compact_kernel(other_ref, rows_ref, pos_ref, ranks_ref, total_ref, block_ref):
    other_pos, where_to, other_ranks, total = place_rows(other_ref, total_ref[0:1, 0:1])
    rows = dot(where_to[:CAP, :], other_ref[:ROUTED, :], ((1,), (0,))) + rows_ref[...].astype(jnp.float32)
    pos = jnp.concatenate([pos_ref[0:1, :], other_pos], axis=1)
    ranks = ranks_ref[...] + other_ranks
    lane = iota((1, CAPL), 1)
    filled = (lane.astype(jnp.float32) < total) & (lane < HELD)
    high = jnp.where(filled, ranks[1:2, :], NEVER)
    high = jnp.where((lane == CAPL - 1) & (total > HELD), 2 * NEVER, high)
    low = jnp.where(filled, ranks[2:3, :], 0.0)
    place = pos + 1
    marks = (jnp.concatenate([high, low], axis=1), (place >> 8).astype(jnp.float32), (place & 255).astype(jnp.float32))
    row = iota((16, WIDTH), 0)
    last = rows[LAST:, :]
    for i, mark in enumerate(marks):
        last = jnp.where(row == 13 + i, mark, last)
    block_ref[:LAST, :] = rows[:LAST, :].astype(jnp.bfloat16)
    block_ref[LAST:, :] = last.astype(jnp.bfloat16)


def row_ranks(block):
    tail = block[LAST:, :].astype(jnp.float32)
    return (256.0 * tail[13:14, :CAPL] + tail[13:14, CAPL:])[:, :CAP]


def column_ranks(block, eye):
    high = dot(eye, block[LAST:, :CAPL], ((1,), (1,)))
    low = dot(eye, block[LAST:, CAPL:], ((1,), (1,)))
    return 256.0 * high[:, 13:14] + low[:, 13:14]


def slot_places(block):
    both = 2 * ROUTED
    tail = block[LAST:, :].astype(jnp.float32)
    first = iota((16, both), 0) * SLOTS
    lane = iota((16, both), 1)
    here = (lane >= first) & (lane < first + SLOTS)
    parts = jnp.concatenate([jnp.where(here, tail[i : i + 1, :], 0.0) for i in (14, 15)], axis=0)
    folded = dot(parts.astype(jnp.bfloat16), slot_fold(both), ((1,), (0,)))
    return (256.0 * folded[:16] + folded[16:]).astype(jnp.int32) - 1


def make_eye():
    return jnp.where(iota((CAP, CAPL), 0) == iota((CAP, CAPL), 1), 1.0, 0.0).astype(jnp.bfloat16)


def earlier_best(query, query_ranks, key, key_ranks):
    scores = dot(key[...], query[...], ((1,), (1,)))
    return jnp.max(jnp.where(key_ranks < query_ranks, scores, -1.0), axis=0, keepdims=True)


def own_kernel(own, best_ref, columns_ref, places_ref):
    columns = column_ranks(own, make_eye())
    columns_ref[...] = jnp.broadcast_to(columns, (CAP, META))
    best_ref[...] = jnp.full((8, CAPL), -1.0, jnp.float32)
    best_ref[0:1, :CAP] = earlier_best(own, row_ranks(own), own, columns)
    places_ref[...] = slot_places(own)


def near_kernel(
    own, x_first, x_second, y_first, y_second, own_best, own_columns, best_ref, columns_ref, places_ref
):
    eye = make_eye()
    ys = (y_first, y_second)
    columns = [column_ranks(key, eye) for key in ys]
    for i in range(2):
        columns_ref[i] = jnp.broadcast_to(columns[i], (CAP, META))
    best_ref[...] = own_best[...]
    for i, query in enumerate((own, x_first, x_second)):
        ranks = row_ranks(query)
        if i == 0:
            best = own_best[0:1, :CAP]
        else:
            best = earlier_best(query, ranks, own, own_columns[:, 0:1])
            places_ref[16 * (i - 1) : 16 * i, :] = slot_places(query)
        for key, ranked in zip(ys, columns):
            best = jnp.maximum(best, earlier_best(query, ranks, key, ranked))
        best_ref[i : i + 1, :CAP] = best


def mid_kernel(own, y_first, y_second, x_far, own_columns, columns_ref, out_ref, places_ref):
    ranks = row_ranks(x_far)
    best = earlier_best(x_far, ranks, own, own_columns[:, 0:1])
    for i, key in enumerate((y_first, y_second)):
        best = jnp.maximum(best, earlier_best(x_far, ranks, key, columns_ref[i, :, 0:1]))
    out_ref[...] = jnp.full((8, CAPL), -1.0, jnp.float32)
    out_ref[0:1, :CAP] = best
    places_ref[...] = slot_places(x_far)


def far_kernel(
    own, x_first, x_second, y_first, y_second, x_far, y_far,
    own_places, near_ref, near_places, mid_ref, mid_places, out_ref,
):
    queries, keys = (own, x_first, x_second, x_far), (y_first, y_second, y_far)
    far_columns = column_ranks(y_far, make_eye())
    over = 0.0
    for block in queries + keys:
        tail = block[LAST:, CAPL - META : CAPL].astype(jnp.float32)
        over = jnp.maximum(over, tail[13:14, META - 1 :])
    over = jnp.where(over > NEVER, 1.0, 0.0)
    my_core, my_z = lax.axis_index("core"), lax.axis_index("z")
    my_x = 2 * lax.axis_index("xh") + lax.axis_index("xl")
    rows = []
    for i, query in enumerate(queries):
        best = earlier_best(query, row_ranks(query), y_far, far_columns)
        best = jnp.maximum(best, near_ref[i : i + 1, :CAP] if i < 3 else mid_ref[0:1, :CAP])
        best = jnp.concatenate([best, jnp.full((1, CAPL - CAP), -1.0, jnp.float32)], axis=1)
        rows.append(jnp.broadcast_to(best, (16, CAPL)))
    rows = jnp.concatenate(rows, axis=0)
    places = jnp.concatenate([own_places[...], near_places[...], mid_places[...]], axis=0)
    found = jnp.full((64, META), -1.0, jnp.float32)
    for part in range(CAPL // META):
        values = rows[:, part * META : (part + 1) * META]
        picked = jnp.take_along_axis(values, places & (META - 1), axis=1, mode="promise_in_bounds")
        found = jnp.where((places >> 7) == part, picked, found)
    found = found + OVER * over
    messages = GROUPS * 8
    row, column = iota((messages, messages), 0), iota((messages, messages), 1)
    core = row & 1
    away = my_z - ((row >> 2) & 7)
    steps = jnp.where(core == 0, away, -away) & 7
    x_away = signed(my_core, my_x - (row >> 5) - (row & 2)) & 3
    block = jnp.where(x_away == 2, 3, jnp.where(x_away == 3, 2, x_away))
    wanted = block * 16 + (core ^ my_core) * GROUPS + steps
    order = jnp.where(column == wanted, 1.0, 0.0).astype(jnp.bfloat16)
    out = dot(jnp.concatenate([order] * 3, axis=1), jnp.concatenate(split3(found), axis=0), ((1,), (0,)))
    for i in range(messages):
        out_ref[i] = out[i : i + 1, :]


def final_kernel(slot_ref, ans_ref, out_ref, flag_ref):
    target, within = slot_ref[0:1, :], slot_ref[1:2, :]
    one_hot = jnp.where(iota((META, ROWS), 0) == within, 1.0, 0.0).astype(jnp.bfloat16)
    groups = []
    for g in range(GROUPS):
        rows = [ans_ref[xl * 32 + g * 4 + i] for xl in range(2) for i in range(4)]
        groups.append(functools.reduce(jnp.maximum, rows))
    best = jnp.concatenate(groups, axis=0)
    got = pick_rows(best, one_hot)
    out_ref[...] = jnp.sum(jnp.where(iota((GROUPS, ROWS), 0) == target, got, 0.0), axis=0, keepdims=True)
    flag_ref[0] = jnp.where(jnp.max(best) > 0.5 * OVER, 1, 0).astype(jnp.int32)


def slow_path(arrived, target, within, live):
    def unpack(v):
        marks = v[ROUTED : ROUTED + 3 * GROUPS, :SLOTS].astype(jnp.float32).reshape(3, ROUTED)
        return v[:ROUTED], marks[0], 256.0 * marks[1] + marks[2]

    rows, ids, ranks = unpack(arrived)
    ring = ("y", "xl", "xh", "core")
    size = 32

    def step(_, carry):
        moving, best = carry
        key_rows, key_ids, key_ranks = unpack(moving)
        scores = dot(rows, key_rows, ((1,), (1,)))
        allowed = (
            (ids[:, None] == key_ids[None, :])
            & (key_ids[None, :] > 0)
            & (key_ranks[None, :] < ranks[:, None])
        )
        best = jnp.maximum(best, jnp.max(jnp.where(allowed, scores, -1.0), axis=1))
        moving = lax.ppermute(moving, ring, [(i, (i + 1) % size) for i in range(size)])
        return moving, best

    _, best = lax.fori_loop(0, size, step, (arrived, jnp.full((ROUTED,), -1.0, jnp.float32)))
    steps = signed(lax.axis_index("core"), lax.axis_index("z") - jnp.arange(GROUPS)) & (GROUPS - 1)
    answered = lax.all_to_all(best.reshape(GROUPS, SLOTS)[steps], "z", 0, 0, tiled=True)
    picked = answered[jnp.maximum(target, 0), jnp.minimum(within, SLOTS - 1)]
    return jnp.where(live, picked, 0.0)


def column_shift(steps):
    pairs = []
    for z in range(8):
        for core in range(2):
            to = (z + (steps if core == 0 else -steps)) % 8
            pairs.append((z * 2 + core, to * 2 + core))
    return pairs


def plane_shift(dx, dy):
    def flat(x, y, core):
        return ((y % 4 * 2 + x % 4 % 2) * 2 + x % 4 // 2) * 2 + core

    pairs = []
    for core in range(2):
        s = 1 if core == 0 else -1
        for x in range(4):
            for y in range(4):
                pairs.append((flat(x + s * dx, y + s * dy, core), flat(x, y, core)))
    return pairs


def body(embeddings, cluster_id, order_rank, row_count):
    f32, bf16, i32 = jnp.float32, jnp.bfloat16, jnp.int32
    shape = jax.ShapeDtypeStruct
    slots_shape = shape((8, ROWS), i32)
    where_to, marks, slots = call(
        slot_kernel,
        (shape((ROUTED, ROWS), bf16), shape((16, ROWS), bf16), slots_shape),
        (cluster_id + 16 * order_rank).reshape(1, ROWS),
    )
    *pieces, slots = call(
        piece_kernel,
        tuple(shape((n * PIECE, META), bf16) for n in PIECES) + (slots_shape,),
        row_count,
        embeddings,
        where_to,
        marks,
        slots,
        smem=(0,),
    )
    send = lambda v, steps: lax.ppermute(v, COLUMN, column_shift(steps))
    two_four = send(pieces[2], 2)
    three, five = send(pieces[3], 3), send(pieces[4], 5)
    two_four, *near_pieces = lax.optimization_barrier((two_four, pieces[5], pieces[1], pieces[6]))
    four = send(two_four[PIECE:], 2)
    six, one, seven = send(near_pieces[0], 6), send(near_pieces[1], 1), send(near_pieces[2], 7)
    arrived = call(
        collect_kernel,
        shape((ROUTED + MARKS, WIDTH), bf16),
        pieces[0],
        one,
        two_four,
        three,
        four,
        five,
        six,
        seven,
    )
    other = lax.ppermute(arrived, "core", [(0, 1), (1, 0)])
    first = call(
        first_kernel,
        (
            shape((CAP, WIDTH), bf16),
            shape((8, ROUTED), i32),
            shape((8, CAPL), f32),
            shape((8, META), f32),
        ),
        arrived,
    )
    block = call(compact_kernel, shape((CAP, WIDTH), bf16), other, *first)
    bring = lambda v, dx, dy: lax.ppermute(v, PLANE, plane_shift(dx, dy))
    x_first, y_first = bring(block, -1, 0), bring(block, 0, -1)
    best_shape, places_shape = shape((8, CAPL), f32), shape((16, META), i32)
    own_best, own_columns, own_places = call(
        own_kernel, (best_shape, shape((CAP, META), f32), places_shape), block
    )
    own, own_best = lax.optimization_barrier((block, own_best))
    x_second, y_second = bring(own, 1, 0), bring(own, 0, 1)
    x_far, y_far = bring(x_first, -1, 0), bring(y_first, 0, -1)
    near_blocks = (block, x_first, x_second, y_first, y_second)
    near, columns, near_places = call(
        near_kernel,
        (best_shape, shape((2, CAP, META), f32), shape((32, META), i32)),
        *near_blocks,
        own_best,
        own_columns,
        cost=8,
    )
    mid, mid_places = call(
        mid_kernel,
        (best_shape, places_shape),
        block,
        y_first,
        y_second,
        x_far,
        own_columns,
        columns,
        cost=3,
    )
    message = call(
        far_kernel,
        shape((64, 1, META), f32),
        *near_blocks,
        x_far,
        y_far,
        own_places,
        near,
        near_places,
        mid,
        mid_places,
        cost=4,
    )
    answer = lax.all_to_all(message, RETURN, split_axis=0, concat_axis=0, tiled=True)
    out, flag = call(final_kernel, (shape((1, ROWS), f32), shape((1,), i32)), slots, answer, smem_out=(1,))
    target, within = slots[0], slots[1]
    return lax.cond(
        flag[0] > 0,
        lambda: slow_path(arrived, target, within, target >= 0),
        lambda: out.reshape(ROWS),
    )


def solution(mesh):
    axes = ("y", "xl", "z", "xh", "core")
    fine = Mesh(mesh.devices.reshape(4, 2, 8, 2, 2), axes)
    return jax.shard_map(
        body,
        mesh=fine,
        in_specs=(P(axes, None), P(axes), P(axes), P(axes)),
        out_specs=P(axes),
        check_vma=False,
    )
```

```python
import functools

import jax
import jax.numpy as jnp
from jax import lax
from jax.experimental import pallas as pl
from jax.experimental.pallas import tpu as pltpu
from jax.sharding import Mesh, PartitionSpec as P

norm_eps = 1e-06
ROWS = 256
WIDTH = 768
META = 128
GROUPS = 8
SLOTS = 48
ROUTED = GROUPS * SLOTS
CAP = 304
HELD = CAP - 3
CAPL = 384
LAST = CAP - 16
NEVER = 512.0
CHUNKS = WIDTH // META
PIECE = CHUNKS * SLOTS + 16
MARKS = 32
PIECES = (1, 1, 2, 1, 1, 1, 1)
OVER = 100.0
VMEM_LIMIT = 50 * 1024 * 1024
PLANE = ("y", "xl", "xh", "core")
COLUMN = ("z", "core")
RETURN = ("xl", "z", "xh", "core")


def dot(a, b, contract):
    return lax.dot_general(a, b, (contract, ((), ())), preferred_element_type=jnp.float32)


def iota(shape, axis):
    return lax.broadcasted_iota(jnp.int32, shape, axis)


def split3(v):
    hi = v.astype(jnp.bfloat16)
    rest = v - hi.astype(jnp.float32)
    mid = rest.astype(jnp.bfloat16)
    low = (rest - mid.astype(jnp.float32)).astype(jnp.bfloat16)
    return hi, mid, low


def pick_rows(v, one_hot):
    n = v.shape[0]
    parts = dot(jnp.concatenate(split3(v), axis=0), one_hot, ((1,), (0,)))
    return (parts[:n] + parts[n : 2 * n]) + parts[2 * n :]


def call(kernel, out, *args, smem=(), smem_out=(), cost=1, scratch=()):
    space = lambda i, scalars: pl.BlockSpec(memory_space=pltpu.SMEM if i in scalars else pltpu.VMEM)
    out_specs = space(0, smem_out)
    if isinstance(out, tuple):
        out_specs = tuple(space(i, smem_out) for i in range(len(out)))
    return pl.pallas_call(
        kernel,
        out_shape=out,
        in_specs=[space(i, smem) for i in range(len(args))],
        out_specs=out_specs,
        scratch_shapes=list(scratch),
        cost_estimate=pl.CostEstimate(
            flops=2 * cost * CAP * CAP * WIDTH, bytes_accessed=4 * CAP * WIDTH, transcendentals=0
        ),
        compiler_params=pltpu.CompilerParams(vmem_limit_bytes=VMEM_LIMIT),
    )(*args)


def signed(core, value):
    return jnp.where(core == 0, value, -value)


def slot_kernel(both_ref, where_ref, marks_ref, slot_ref):
    both = both_ref[...]
    live = both >= 0
    ids, ranks = both & 15, both >> 4
    target = ids & (GROUPS - 1)
    chosen = jnp.where((iota((GROUPS, ROWS), 0) == target) & live, 1.0, 0.0)
    upper = jnp.where(iota((ROWS, ROWS), 0) < iota((ROWS, ROWS), 1), 1.0, 0.0).astype(jnp.bfloat16)
    before = dot(chosen.astype(jnp.bfloat16), upper, ((1,), (0,)))
    within = jnp.sum(before * chosen, axis=0, keepdims=True).astype(jnp.int32)
    steps = signed(lax.axis_index("core"), target - lax.axis_index("z")) & (GROUPS - 1)
    at = jnp.where(steps == 3, 4, jnp.where(steps == 4, 3, steps))
    slot = jnp.where(live, at * SLOTS + within, -1)
    where_ref[...] = jnp.where(iota((ROUTED, ROWS), 0) == slot, 1.0, 0.0).astype(jnp.bfloat16)
    high = ranks >> 8
    row = iota((16, ROWS), 0)
    meta = jnp.where(
        row == 0, ids + 1, jnp.where(row == 1, high, jnp.where(row == 2, ranks - (high << 8), 0))
    )
    marks_ref[...] = meta.astype(jnp.float32).astype(jnp.bfloat16)
    slot_ref[0:1, :] = jnp.where(live, target, -1)
    slot_ref[1:2, :] = within
    slot_ref[2:8, :] = jnp.zeros((6, ROWS), jnp.int32)


def piece_kernel(emb_ref, where_ref, marks_ref, *out_refs):
    x = emb_ref[...].astype(jnp.float32)
    unit = (x * lax.rsqrt(jnp.sum(x * x, axis=1, keepdims=True) + norm_eps)).astype(jnp.bfloat16)
    where_to = where_ref[...]
    rows = dot(where_to, unit, ((1,), (0,))).astype(jnp.bfloat16)
    marks = dot(marks_ref[...], where_to, ((1,), (1,)))
    at = 0
    for ref in out_refs:
        for first in range(0, ref.shape[0], PIECE):
            for i in range(CHUNKS):
                ref[first + i * SLOTS : first + (i + 1) * SLOTS, :] = rows[
                    at : at + SLOTS, i * META : (i + 1) * META
                ]
            tail = jnp.concatenate(
                [marks[:, at : at + SLOTS], jnp.zeros((16, META - SLOTS), jnp.float32)], axis=1
            )
            ref[first + CHUNKS * SLOTS : first + PIECE, :] = tail.astype(jnp.bfloat16)
            at += SLOTS


def collect_kernel(*refs):
    out_ref = refs[-1]
    marks = []
    for j, ref in enumerate(refs[:-1]):
        for i in range(CHUNKS):
            out_ref[j * SLOTS : (j + 1) * SLOTS, i * META : (i + 1) * META] = ref[
                i * SLOTS : (i + 1) * SLOTS, :
            ]
        marks.append(ref[CHUNKS * SLOTS : PIECE, :].astype(jnp.float32))
    by_kind = [mark[i : i + 1, :] for i in range(3) for mark in marks]
    kinds = jnp.concatenate(by_kind + [jnp.zeros((MARKS - 3 * GROUPS, META), jnp.float32)], axis=0)
    out_ref[ROUTED:, :META] = kinds.astype(jnp.bfloat16)
    out_ref[ROUTED:, META:] = jnp.zeros((MARKS, WIDTH - META), jnp.bfloat16)


def slot_fold(both):
    slot = iota((both, META), 0)
    slot = slot - SLOTS * ((slot * 1366) >> 16)
    return jnp.where(slot == iota((both, META), 1), 1.0, 0.0).astype(jnp.bfloat16)


def place_rows(arrived_ref, first):
    marks = arrived_ref[ROUTED:, :META]
    spread = dot(marks, slot_fold(ROUTED), ((1,), (1,)))
    here = iota((GROUPS, ROUTED), 0) == ((iota((GROUPS, ROUTED), 1) * 1366) >> 16)
    meta = [
        jnp.sum(jnp.where(here, spread[GROUPS * i : GROUPS * (i + 1), :], 0.0), axis=0, keepdims=True)
        for i in range(3)
    ]
    mine = lax.axis_index("z") + GROUPS * lax.axis_index("core") + 1
    ones = jnp.where(meta[0] == mine.astype(jnp.float32), 1.0, 0.0)
    chunks = [ones[:, i : i + META] for i in range(0, ROUTED, META)]
    upper = jnp.where(iota((META, META), 0) < iota((META, META), 1), 1.0, 0.0).astype(jnp.bfloat16)
    stacked = jnp.concatenate(chunks + [jnp.zeros((8 - len(chunks), META), jnp.float32)], axis=0)
    before = dot(stacked.astype(jnp.bfloat16), upper, ((1,), (0,)))
    total, counted = first, []
    for i, chunk in enumerate(chunks):
        counted.append(jnp.where(chunk > 0.5, before[i : i + 1, :] + total, -1.0))
        total = total + jnp.sum(chunk, axis=1, keepdims=True)
    pos = jnp.concatenate(counted, axis=1).astype(jnp.int32)
    where_to = jnp.where((iota((CAPL, ROUTED), 0) == pos) & (pos < HELD), 1.0, 0.0).astype(jnp.bfloat16)
    meta = jnp.concatenate(meta + [jnp.zeros((5, ROUTED), jnp.float32)], axis=0)
    ranks = dot(meta.astype(jnp.bfloat16), where_to, ((1,), (1,)))
    return pos, where_to, ranks, total


def first_kernel(own_ref, rows_ref, pos_ref, ranks_ref, total_ref):
    pos, where_to, ranks, total = place_rows(own_ref, jnp.zeros((1, 1), jnp.float32))
    rows_ref[...] = dot(where_to[:CAP, :], own_ref[:ROUTED, :], ((1,), (0,))).astype(jnp.bfloat16)
    pos_ref[...] = jnp.broadcast_to(pos, (8, ROUTED))
    ranks_ref[...] = ranks
    total_ref[...] = jnp.broadcast_to(total, (8, META))


def compact_kernel(other_ref, rows_ref, pos_ref, ranks_ref, total_ref, block_ref):
    other_pos, where_to, other_ranks, total = place_rows(other_ref, total_ref[0:1, 0:1])
    rows = dot(where_to[:CAP, :], other_ref[:ROUTED, :], ((1,), (0,))) + rows_ref[...].astype(jnp.float32)
    pos = jnp.concatenate([pos_ref[0:1, :], other_pos], axis=1)
    ranks = ranks_ref[...] + other_ranks
    lane = iota((1, CAPL), 1)
    filled = (lane.astype(jnp.float32) < total) & (lane < HELD)
    high = jnp.where(filled, ranks[1:2, :], NEVER)
    high = jnp.where((lane == CAPL - 1) & (total > HELD), 2 * NEVER, high)
    low = jnp.where(filled, ranks[2:3, :], 0.0)
    place = pos + 1
    marks = (jnp.concatenate([high, low], axis=1), (place >> 8).astype(jnp.float32), (place & 255).astype(jnp.float32))
    row = iota((16, WIDTH), 0)
    last = rows[LAST:, :]
    for i, mark in enumerate(marks):
        last = jnp.where(row == 13 + i, mark, last)
    block_ref[:LAST, :] = rows[:LAST, :].astype(jnp.bfloat16)
    block_ref[LAST:, :] = last.astype(jnp.bfloat16)


def row_ranks(block):
    tail = block[LAST:, :].astype(jnp.float32)
    return (256.0 * tail[13:14, :CAPL] + tail[13:14, CAPL:])[:, :CAP]


def column_ranks(block, eye):
    high = dot(eye, block[LAST:, :CAPL], ((1,), (1,)))
    low = dot(eye, block[LAST:, CAPL:], ((1,), (1,)))
    return 256.0 * high[:, 13:14] + low[:, 13:14]


def slot_places(block):
    both = 2 * ROUTED
    tail = block[LAST:, :].astype(jnp.float32)
    first = iota((16, both), 0) * SLOTS
    lane = iota((16, both), 1)
    here = (lane >= first) & (lane < first + SLOTS)
    parts = jnp.concatenate([jnp.where(here, tail[i : i + 1, :], 0.0) for i in (14, 15)], axis=0)
    folded = dot(parts.astype(jnp.bfloat16), slot_fold(both), ((1,), (0,)))
    return (256.0 * folded[:16] + folded[16:]).astype(jnp.int32) - 1


def make_eye():
    return jnp.where(iota((CAP, CAPL), 0) == iota((CAP, CAPL), 1), 1.0, 0.0).astype(jnp.bfloat16)


def earlier_best(query, query_ranks, key, key_ranks):
    scores = dot(key[...], query[...], ((1,), (1,)))
    return jnp.max(jnp.where(key_ranks < query_ranks, scores, -1.0), axis=0, keepdims=True)


def own_kernel(own, best_ref, columns_ref, places_ref):
    columns = column_ranks(own, make_eye())
    columns_ref[...] = jnp.broadcast_to(columns, (CAP, META))
    best_ref[...] = jnp.full((8, CAPL), -1.0, jnp.float32)
    best_ref[0:1, :CAP] = earlier_best(own, row_ranks(own), own, columns)
    places_ref[...] = slot_places(own)


def near_kernel(
    own, x_first, x_second, y_first, y_second, own_best, own_columns, best_ref, columns_ref, places_ref
):
    eye = make_eye()
    ys = (y_first, y_second)
    columns = [column_ranks(key, eye) for key in ys]
    for i in range(2):
        columns_ref[i] = jnp.broadcast_to(columns[i], (CAP, META))
    best_ref[...] = own_best[...]
    for i, query in enumerate((own, x_first, x_second)):
        ranks = row_ranks(query)
        if i == 0:
            best = own_best[0:1, :CAP]
        else:
            best = earlier_best(query, ranks, own, own_columns[:, 0:1])
            places_ref[16 * (i - 1) : 16 * i, :] = slot_places(query)
        for key, ranked in zip(ys, columns):
            best = jnp.maximum(best, earlier_best(query, ranks, key, ranked))
        best_ref[i : i + 1, :CAP] = best


def mid_kernel(own, y_first, y_second, x_far, own_columns, columns_ref, out_ref, places_ref):
    ranks = row_ranks(x_far)
    best = earlier_best(x_far, ranks, own, own_columns[:, 0:1])
    for i, key in enumerate((y_first, y_second)):
        best = jnp.maximum(best, earlier_best(x_far, ranks, key, columns_ref[i, :, 0:1]))
    out_ref[...] = jnp.full((8, CAPL), -1.0, jnp.float32)
    out_ref[0:1, :CAP] = best
    places_ref[...] = slot_places(x_far)


def far_kernel(
    own, x_first, x_second, y_first, y_second, x_far, y_far,
    own_places, near_ref, near_places, mid_ref, mid_places, out_ref,
):
    queries, keys = (own, x_first, x_second, x_far), (y_first, y_second, y_far)
    far_columns = column_ranks(y_far, make_eye())
    over = 0.0
    for block in queries + keys:
        tail = block[LAST:, CAPL - META : CAPL].astype(jnp.float32)
        over = jnp.maximum(over, tail[13:14, META - 1 :])
    over = jnp.where(over > NEVER, 1.0, 0.0)
    my_core, my_z = lax.axis_index("core"), lax.axis_index("z")
    my_x = 2 * lax.axis_index("xh") + lax.axis_index("xl")
    rows = []
    for i, query in enumerate(queries):
        best = earlier_best(query, row_ranks(query), y_far, far_columns)
        best = jnp.maximum(best, near_ref[i : i + 1, :CAP] if i < 3 else mid_ref[0:1, :CAP])
        best = jnp.concatenate([best, jnp.full((1, CAPL - CAP), -1.0, jnp.float32)], axis=1)
        rows.append(jnp.broadcast_to(best, (16, CAPL)))
    rows = jnp.concatenate(rows, axis=0)
    places = jnp.concatenate([own_places[...], near_places[...], mid_places[...]], axis=0)
    found = jnp.full((64, META), -1.0, jnp.float32)
    for part in range(CAPL // META):
        values = rows[:, part * META : (part + 1) * META]
        picked = jnp.take_along_axis(values, places & (META - 1), axis=1, mode="promise_in_bounds")
        found = jnp.where((places >> 7) == part, picked, found)
    found = found + OVER * over
    messages = GROUPS * 8
    row, column = iota((messages, messages), 0), iota((messages, messages), 1)
    core = row & 1
    away = my_z - ((row >> 2) & 7)
    steps = jnp.where(core == 0, away, -away) & 7
    x_away = signed(my_core, my_x - (row >> 5) - (row & 2)) & 3
    block = jnp.where(x_away == 2, 3, jnp.where(x_away == 3, 2, x_away))
    wanted = block * 16 + (core ^ my_core) * GROUPS + steps
    order = jnp.where(column == wanted, 1.0, 0.0).astype(jnp.bfloat16)
    out = dot(jnp.concatenate([order] * 3, axis=1), jnp.concatenate(split3(found), axis=0), ((1,), (0,)))
    for i in range(messages):
        out_ref[i] = out[i : i + 1, :]


def final_kernel(slot_ref, ans_ref, out_ref, flag_ref):
    target, within = slot_ref[0:1, :], slot_ref[1:2, :]
    one_hot = jnp.where(iota((META, ROWS), 0) == within, 1.0, 0.0).astype(jnp.bfloat16)
    groups = []
    for g in range(GROUPS):
        rows = [ans_ref[xl * 32 + g * 4 + i] for xl in range(2) for i in range(4)]
        groups.append(functools.reduce(jnp.maximum, rows))
    best = jnp.concatenate(groups, axis=0)
    got = pick_rows(best, one_hot)
    out_ref[...] = jnp.sum(jnp.where(iota((GROUPS, ROWS), 0) == target, got, 0.0), axis=0, keepdims=True)
    flag_ref[0] = jnp.where(jnp.max(best) > 0.5 * OVER, 1, 0).astype(jnp.int32)


def slow_path(arrived, target, within, live):
    def unpack(v):
        marks = v[ROUTED : ROUTED + 3 * GROUPS, :SLOTS].astype(jnp.float32).reshape(3, ROUTED)
        return v[:ROUTED], marks[0], 256.0 * marks[1] + marks[2]

    rows, ids, ranks = unpack(arrived)
    ring = ("y", "xl", "xh", "core")
    size = 32

    def step(_, carry):
        moving, best = carry
        key_rows, key_ids, key_ranks = unpack(moving)
        scores = dot(rows, key_rows, ((1,), (1,)))
        allowed = (
            (ids[:, None] == key_ids[None, :])
            & (key_ids[None, :] > 0)
            & (key_ranks[None, :] < ranks[:, None])
        )
        best = jnp.maximum(best, jnp.max(jnp.where(allowed, scores, -1.0), axis=1))
        moving = lax.ppermute(moving, ring, [(i, (i + 1) % size) for i in range(size)])
        return moving, best

    _, best = lax.fori_loop(0, size, step, (arrived, jnp.full((ROUTED,), -1.0, jnp.float32)))
    steps = signed(lax.axis_index("core"), lax.axis_index("z") - jnp.arange(GROUPS)) & (GROUPS - 1)
    answered = lax.all_to_all(best.reshape(GROUPS, SLOTS)[steps], "z", 0, 0, tiled=True)
    picked = answered[jnp.maximum(target, 0), jnp.minimum(within, SLOTS - 1)]
    return jnp.where(live, picked, 0.0)


def column_shift(steps):
    pairs = []
    for z in range(8):
        for core in range(2):
            to = (z + (steps if core == 0 else -steps)) % 8
            pairs.append((z * 2 + core, to * 2 + core))
    return pairs


def plane_shift(dx, dy):
    def flat(x, y, core):
        return ((y % 4 * 2 + x % 4 % 2) * 2 + x % 4 // 2) * 2 + core

    pairs = []
    for core in range(2):
        s = 1 if core == 0 else -1
        for x in range(4):
            for y in range(4):
                pairs.append((flat(x + s * dx, y + s * dy, core), flat(x, y, core)))
    return pairs


def body(embeddings, cluster_id, order_rank, row_count):
    f32, bf16, i32 = jnp.float32, jnp.bfloat16, jnp.int32
    shape = jax.ShapeDtypeStruct
    live = jnp.arange(ROWS, dtype=i32) < row_count[0]
    both = jnp.where(live, cluster_id + 16 * order_rank, -1)
    where_to, marks, slots = call(
        slot_kernel,
        (shape((ROUTED, ROWS), bf16), shape((16, ROWS), bf16), shape((8, ROWS), i32)),
        both.reshape(1, ROWS),
    )
    pieces = call(
        piece_kernel,
        tuple(shape((n * PIECE, META), bf16) for n in PIECES),
        embeddings,
        where_to,
        marks,
    )
    send = lambda v, steps: lax.ppermute(v, COLUMN, column_shift(steps))
    two_four = send(pieces[2], 2)
    three, five, six = send(pieces[3], 3), send(pieces[4], 5), send(pieces[5], 6)
    four = send(two_four[PIECE:], 2)
    one, seven = send(pieces[1], 1), send(pieces[6], 7)
    arrived = call(
        collect_kernel,
        shape((ROUTED + MARKS, WIDTH), bf16),
        pieces[0],
        one,
        two_four,
        three,
        four,
        five,
        six,
        seven,
    )
    other = lax.ppermute(arrived, "core", [(0, 1), (1, 0)])
    first = call(
        first_kernel,
        (
            shape((CAP, WIDTH), bf16),
            shape((8, ROUTED), i32),
            shape((8, CAPL), f32),
            shape((8, META), f32),
        ),
        arrived,
    )
    block = call(compact_kernel, shape((CAP, WIDTH), bf16), other, *first)
    bring = lambda v, dx, dy: lax.ppermute(v, PLANE, plane_shift(dx, dy))
    x_first, y_first = bring(block, -1, 0), bring(block, 0, -1)
    best_shape, places_shape = shape((8, CAPL), f32), shape((16, META), i32)
    own_best, own_columns, own_places = call(
        own_kernel, (best_shape, shape((CAP, META), f32), places_shape), block
    )
    own, own_best = lax.optimization_barrier((block, own_best))
    x_second, y_second = bring(own, 1, 0), bring(own, 0, 1)
    x_far, y_far = bring(x_first, -1, 0), bring(y_first, 0, -1)
    near_blocks = (block, x_first, x_second, y_first, y_second)
    near, columns, near_places = call(
        near_kernel,
        (best_shape, shape((2, CAP, META), f32), shape((32, META), i32)),
        *near_blocks,
        own_best,
        own_columns,
        cost=8,
    )
    mid, mid_places = call(
        mid_kernel,
        (best_shape, places_shape),
        block,
        y_first,
        y_second,
        x_far,
        own_columns,
        columns,
        cost=3,
    )
    message = call(
        far_kernel,
        shape((64, 1, META), f32),
        *near_blocks,
        x_far,
        y_far,
        own_places,
        near,
        near_places,
        mid,
        mid_places,
        cost=4,
    )
    answer = lax.all_to_all(message, RETURN, split_axis=0, concat_axis=0, tiled=True)
    out, flag = call(final_kernel, (shape((1, ROWS), f32), shape((1,), i32)), slots, answer, smem_out=(1,))
    target, within = slots[0], slots[1]
    return lax.cond(
        flag[0] > 0,
        lambda: slow_path(arrived, target, within, target >= 0),
        lambda: out.reshape(ROWS),
    )


def solution(mesh):
    axes = ("y", "xl", "z", "xh", "core")
    fine = Mesh(mesh.devices.reshape(4, 2, 8, 2, 2), axes)
    return jax.shard_map(
        body,
        mesh=fine,
        in_specs=(P(axes, None), P(axes), P(axes), P(axes)),
        out_specs=P(axes),
        check_vma=False,
    )
```

```python
import functools

import jax
import jax.numpy as jnp
from jax import lax
from jax.experimental import pallas as pl
from jax.experimental.pallas import tpu as pltpu
from jax.sharding import Mesh, PartitionSpec as P

norm_eps = 1e-06
ROWS = 256
WIDTH = 768
META = 128
GROUPS = 8
SLOTS = 48
ROUTED = GROUPS * SLOTS
CAP = 304
HELD = CAP - 3
CAPL = 384
LAST = CAP - 16
NEVER = 512.0
CHUNKS = WIDTH // META
PIECE = CHUNKS * SLOTS + 16
MARKS = 32
PIECES = (1, 1, 2, 1, 1, 1, 1)
OVER = 100.0
VMEM_LIMIT = 50 * 1024 * 1024
PLANE = ("y", "xl", "xh", "core")
COLUMN = ("z", "core")
RETURN = ("xl", "z", "xh", "core")


def dot(a, b, contract):
    return lax.dot_general(a, b, (contract, ((), ())), preferred_element_type=jnp.float32)


def iota(shape, axis):
    return lax.broadcasted_iota(jnp.int32, shape, axis)


def split3(v):
    hi = v.astype(jnp.bfloat16)
    rest = v - hi.astype(jnp.float32)
    mid = rest.astype(jnp.bfloat16)
    low = (rest - mid.astype(jnp.float32)).astype(jnp.bfloat16)
    return hi, mid, low


def pick_rows(v, one_hot):
    n = v.shape[0]
    parts = dot(jnp.concatenate(split3(v), axis=0), one_hot, ((1,), (0,)))
    return (parts[:n] + parts[n : 2 * n]) + parts[2 * n :]


def call(kernel, out, *args, smem=(), smem_out=(), cost=1, scratch=()):
    space = lambda i, scalars: pl.BlockSpec(memory_space=pltpu.SMEM if i in scalars else pltpu.VMEM)
    out_specs = space(0, smem_out)
    if isinstance(out, tuple):
        out_specs = tuple(space(i, smem_out) for i in range(len(out)))
    return pl.pallas_call(
        kernel,
        out_shape=out,
        in_specs=[space(i, smem) for i in range(len(args))],
        out_specs=out_specs,
        scratch_shapes=list(scratch),
        cost_estimate=pl.CostEstimate(
            flops=2 * cost * CAP * CAP * WIDTH, bytes_accessed=4 * CAP * WIDTH, transcendentals=0
        ),
        compiler_params=pltpu.CompilerParams(vmem_limit_bytes=VMEM_LIMIT),
    )(*args)


def signed(core, value):
    return jnp.where(core == 0, value, -value)


def slot_kernel(both_ref, where_ref, marks_ref, slot_ref):
    ids, ranks = both_ref[...] & 15, both_ref[...] >> 4
    target = ids & (GROUPS - 1)
    chosen = jnp.where(iota((GROUPS, ROWS), 0) == target, 1.0, 0.0)
    upper = jnp.where(iota((ROWS, ROWS), 0) < iota((ROWS, ROWS), 1), 1.0, 0.0).astype(jnp.bfloat16)
    before = dot(chosen.astype(jnp.bfloat16), upper, ((1,), (0,)))
    within = jnp.sum(before * chosen, axis=0, keepdims=True).astype(jnp.int32)
    steps = signed(lax.axis_index("core"), target - lax.axis_index("z")) & (GROUPS - 1)
    at = jnp.where(steps == 3, 4, jnp.where(steps == 4, 3, steps))
    slot = jnp.where(within < SLOTS, at * SLOTS + within, -1)
    where_ref[...] = jnp.where(iota((ROUTED, ROWS), 0) == slot, 1.0, 0.0).astype(jnp.bfloat16)
    high = ranks >> 8
    row = iota((16, ROWS), 0)
    meta = jnp.where(
        row == 0, ids + 1, jnp.where(row == 1, high, jnp.where(row == 2, ranks - (high << 8), 0))
    )
    marks_ref[...] = meta.astype(jnp.float32).astype(jnp.bfloat16)
    slot_ref[0:1, :] = target
    slot_ref[1:2, :] = within
    slot_ref[2:8, :] = jnp.zeros((6, ROWS), jnp.int32)


def piece_kernel(count_ref, emb_ref, where_ref, marks_ref, slot_ref, *refs):
    *out_refs, live_slot_ref = refs
    live = iota((1, ROWS), 1) < count_ref[0]
    live_slot_ref[0:1, :] = jnp.where(live, slot_ref[0:1, :], -1)
    live_slot_ref[1:8, :] = slot_ref[1:8, :]
    x = emb_ref[...].astype(jnp.float32)
    unit = x * lax.rsqrt(jnp.sum(x * x, axis=1, keepdims=True) + norm_eps)
    unit = jnp.where(iota((ROWS, 1), 0) < count_ref[0], unit, 0.0).astype(jnp.bfloat16)
    where_to = where_ref[...]
    rows = dot(where_to, unit, ((1,), (0,))).astype(jnp.bfloat16)
    meta = jnp.where(live, marks_ref[...].astype(jnp.float32), 0.0).astype(jnp.bfloat16)
    marks = dot(meta, where_to, ((1,), (1,)))
    at = 0
    for ref in out_refs:
        for first in range(0, ref.shape[0], PIECE):
            for i in range(CHUNKS):
                ref[first + i * SLOTS : first + (i + 1) * SLOTS, :] = rows[
                    at : at + SLOTS, i * META : (i + 1) * META
                ]
            tail = jnp.concatenate(
                [marks[:, at : at + SLOTS], jnp.zeros((16, META - SLOTS), jnp.float32)], axis=1
            )
            ref[first + CHUNKS * SLOTS : first + PIECE, :] = tail.astype(jnp.bfloat16)
            at += SLOTS


def collect_kernel(*refs):
    out_ref = refs[-1]
    marks = []
    for j, ref in enumerate(refs[:-1]):
        for i in range(CHUNKS):
            out_ref[j * SLOTS : (j + 1) * SLOTS, i * META : (i + 1) * META] = ref[
                i * SLOTS : (i + 1) * SLOTS, :
            ]
        marks.append(ref[CHUNKS * SLOTS : PIECE, :].astype(jnp.float32))
    by_kind = [mark[i : i + 1, :] for i in range(3) for mark in marks]
    kinds = jnp.concatenate(by_kind + [jnp.zeros((MARKS - 3 * GROUPS, META), jnp.float32)], axis=0)
    out_ref[ROUTED:, :META] = kinds.astype(jnp.bfloat16)
    out_ref[ROUTED:, META:] = jnp.zeros((MARKS, WIDTH - META), jnp.bfloat16)


def slot_fold(both):
    slot = iota((both, META), 0)
    slot = slot - SLOTS * ((slot * 1366) >> 16)
    return jnp.where(slot == iota((both, META), 1), 1.0, 0.0).astype(jnp.bfloat16)


def place_rows(arrived_ref, first):
    marks = arrived_ref[ROUTED:, :META]
    spread = dot(marks, slot_fold(ROUTED), ((1,), (1,)))
    here = iota((GROUPS, ROUTED), 0) == ((iota((GROUPS, ROUTED), 1) * 1366) >> 16)
    meta = [
        jnp.sum(jnp.where(here, spread[GROUPS * i : GROUPS * (i + 1), :], 0.0), axis=0, keepdims=True)
        for i in range(3)
    ]
    mine = lax.axis_index("z") + GROUPS * lax.axis_index("core") + 1
    ones = jnp.where(meta[0] == mine.astype(jnp.float32), 1.0, 0.0)
    chunks = [ones[:, i : i + META] for i in range(0, ROUTED, META)]
    upper = jnp.where(iota((META, META), 0) < iota((META, META), 1), 1.0, 0.0).astype(jnp.bfloat16)
    stacked = jnp.concatenate(chunks + [jnp.zeros((8 - len(chunks), META), jnp.float32)], axis=0)
    before = dot(stacked.astype(jnp.bfloat16), upper, ((1,), (0,)))
    total, counted = first, []
    for i, chunk in enumerate(chunks):
        counted.append(jnp.where(chunk > 0.5, before[i : i + 1, :] + total, -1.0))
        total = total + jnp.sum(chunk, axis=1, keepdims=True)
    pos = jnp.concatenate(counted, axis=1).astype(jnp.int32)
    where_to = jnp.where((iota((CAPL, ROUTED), 0) == pos) & (pos < HELD), 1.0, 0.0).astype(jnp.bfloat16)
    meta = jnp.concatenate(meta + [jnp.zeros((5, ROUTED), jnp.float32)], axis=0)
    ranks = dot(meta.astype(jnp.bfloat16), where_to, ((1,), (1,)))
    return pos, where_to, ranks, total


def first_kernel(own_ref, rows_ref, pos_ref, ranks_ref, total_ref):
    pos, where_to, ranks, total = place_rows(own_ref, jnp.zeros((1, 1), jnp.float32))
    rows_ref[...] = dot(where_to[:CAP, :], own_ref[:ROUTED, :], ((1,), (0,))).astype(jnp.bfloat16)
    pos_ref[...] = jnp.broadcast_to(pos, (8, ROUTED))
    ranks_ref[...] = ranks
    total_ref[...] = jnp.broadcast_to(total, (8, META))


def compact_kernel(other_ref, rows_ref, pos_ref, ranks_ref, total_ref, block_ref):
    other_pos, where_to, other_ranks, total = place_rows(other_ref, total_ref[0:1, 0:1])
    rows = dot(where_to[:CAP, :], other_ref[:ROUTED, :], ((1,), (0,))) + rows_ref[...].astype(jnp.float32)
    pos = jnp.concatenate([pos_ref[0:1, :], other_pos], axis=1)
    ranks = ranks_ref[...] + other_ranks
    lane = iota((1, CAPL), 1)
    filled = (lane.astype(jnp.float32) < total) & (lane < HELD)
    high = jnp.where(filled, ranks[1:2, :], NEVER)
    high = jnp.where((lane == CAPL - 1) & (total > HELD), 2 * NEVER, high)
    low = jnp.where(filled, ranks[2:3, :], 0.0)
    place = pos + 1
    marks = (jnp.concatenate([high, low], axis=1), (place >> 8).astype(jnp.float32), (place & 255).astype(jnp.float32))
    row = iota((16, WIDTH), 0)
    last = rows[LAST:, :]
    for i, mark in enumerate(marks):
        last = jnp.where(row == 13 + i, mark, last)
    block_ref[:LAST, :] = rows[:LAST, :].astype(jnp.bfloat16)
    block_ref[LAST:, :] = last.astype(jnp.bfloat16)


def row_ranks(block):
    tail = block[LAST:, :].astype(jnp.float32)
    return (256.0 * tail[13:14, :CAPL] + tail[13:14, CAPL:])[:, :CAP]


def column_ranks(block, eye):
    high = dot(eye, block[LAST:, :CAPL], ((1,), (1,)))
    low = dot(eye, block[LAST:, CAPL:], ((1,), (1,)))
    return 256.0 * high[:, 13:14] + low[:, 13:14]


def slot_places(block):
    both = 2 * ROUTED
    tail = block[LAST:, :].astype(jnp.float32)
    first = iota((16, both), 0) * SLOTS
    lane = iota((16, both), 1)
    here = (lane >= first) & (lane < first + SLOTS)
    parts = jnp.concatenate([jnp.where(here, tail[i : i + 1, :], 0.0) for i in (14, 15)], axis=0)
    folded = dot(parts.astype(jnp.bfloat16), slot_fold(both), ((1,), (0,)))
    return (256.0 * folded[:16] + folded[16:]).astype(jnp.int32) - 1


def make_eye():
    return jnp.where(iota((CAP, CAPL), 0) == iota((CAP, CAPL), 1), 1.0, 0.0).astype(jnp.bfloat16)


def earlier_best(query, query_ranks, key, key_ranks):
    scores = dot(key[...], query[...], ((1,), (1,)))
    return jnp.max(jnp.where(key_ranks < query_ranks, scores, -1.0), axis=0, keepdims=True)


def own_kernel(own, best_ref, columns_ref, places_ref):
    columns = column_ranks(own, make_eye())
    columns_ref[...] = jnp.broadcast_to(columns, (CAP, META))
    best_ref[...] = jnp.full((8, CAPL), -1.0, jnp.float32)
    best_ref[0:1, :CAP] = earlier_best(own, row_ranks(own), own, columns)
    places_ref[...] = slot_places(own)


def near_kernel(
    own, x_first, x_second, y_first, y_second, own_best, own_columns, best_ref, columns_ref, places_ref
):
    eye = make_eye()
    ys = (y_first, y_second)
    columns = [column_ranks(key, eye) for key in ys]
    for i in range(2):
        columns_ref[i] = jnp.broadcast_to(columns[i], (CAP, META))
    best_ref[...] = own_best[...]
    for i, query in enumerate((own, x_first, x_second)):
        ranks = row_ranks(query)
        if i == 0:
            best = own_best[0:1, :CAP]
        else:
            best = earlier_best(query, ranks, own, own_columns[:, 0:1])
            places_ref[16 * (i - 1) : 16 * i, :] = slot_places(query)
        for key, ranked in zip(ys, columns):
            best = jnp.maximum(best, earlier_best(query, ranks, key, ranked))
        best_ref[i : i + 1, :CAP] = best


def mid_kernel(own, y_first, y_second, x_far, own_columns, columns_ref, out_ref, places_ref):
    ranks = row_ranks(x_far)
    best = earlier_best(x_far, ranks, own, own_columns[:, 0:1])
    for i, key in enumerate((y_first, y_second)):
        best = jnp.maximum(best, earlier_best(x_far, ranks, key, columns_ref[i, :, 0:1]))
    out_ref[...] = jnp.full((8, CAPL), -1.0, jnp.float32)
    out_ref[0:1, :CAP] = best
    places_ref[...] = slot_places(x_far)


def far_kernel(
    own, x_first, x_second, y_first, y_second, x_far, y_far,
    own_places, near_ref, near_places, mid_ref, mid_places, out_ref,
):
    queries, keys = (own, x_first, x_second, x_far), (y_first, y_second, y_far)
    far_columns = column_ranks(y_far, make_eye())
    over = 0.0
    for block in queries + keys:
        tail = block[LAST:, CAPL - META : CAPL].astype(jnp.float32)
        over = jnp.maximum(over, tail[13:14, META - 1 :])
    over = jnp.where(over > NEVER, 1.0, 0.0)
    my_core, my_z = lax.axis_index("core"), lax.axis_index("z")
    my_x = 2 * lax.axis_index("xh") + lax.axis_index("xl")
    rows = []
    for i, query in enumerate(queries):
        best = earlier_best(query, row_ranks(query), y_far, far_columns)
        best = jnp.maximum(best, near_ref[i : i + 1, :CAP] if i < 3 else mid_ref[0:1, :CAP])
        best = jnp.concatenate([best, jnp.full((1, CAPL - CAP), -1.0, jnp.float32)], axis=1)
        rows.append(jnp.broadcast_to(best, (16, CAPL)))
    rows = jnp.concatenate(rows, axis=0)
    places = jnp.concatenate([own_places[...], near_places[...], mid_places[...]], axis=0)
    found = jnp.full((64, META), -1.0, jnp.float32)
    for part in range(CAPL // META):
        values = rows[:, part * META : (part + 1) * META]
        picked = jnp.take_along_axis(values, places & (META - 1), axis=1, mode="promise_in_bounds")
        found = jnp.where((places >> 7) == part, picked, found)
    found = found + OVER * over
    messages = GROUPS * 8
    row, column = iota((messages, messages), 0), iota((messages, messages), 1)
    core = row & 1
    away = my_z - ((row >> 2) & 7)
    steps = jnp.where(core == 0, away, -away) & 7
    x_away = signed(my_core, my_x - (row >> 5) - (row & 2)) & 3
    block = jnp.where(x_away == 2, 3, jnp.where(x_away == 3, 2, x_away))
    wanted = block * 16 + (core ^ my_core) * GROUPS + steps
    order = jnp.where(column == wanted, 1.0, 0.0).astype(jnp.bfloat16)
    out = dot(jnp.concatenate([order] * 3, axis=1), jnp.concatenate(split3(found), axis=0), ((1,), (0,)))
    out_ref[...] = out.reshape(messages, 1, META)


def final_kernel(slot_ref, ans_ref, out_ref, flag_ref):
    target, within = slot_ref[0:1, :], slot_ref[1:2, :]
    one_hot = jnp.where(iota((META, ROWS), 0) == within, 1.0, 0.0).astype(jnp.bfloat16)
    groups = []
    for g in range(GROUPS):
        rows = [ans_ref[xl * 32 + g * 4 + i] for xl in range(2) for i in range(4)]
        groups.append(functools.reduce(jnp.maximum, rows))
    best = jnp.concatenate(groups, axis=0)
    got = pick_rows(best, one_hot)
    out_ref[...] = jnp.sum(jnp.where(iota((GROUPS, ROWS), 0) == target, got, 0.0), axis=0, keepdims=True)
    flag_ref[0] = jnp.where(jnp.max(best) > 0.5 * OVER, 1, 0).astype(jnp.int32)


def slow_path(arrived, target, within, live):
    def unpack(v):
        marks = v[ROUTED : ROUTED + 3 * GROUPS, :SLOTS].astype(jnp.float32).reshape(3, ROUTED)
        return v[:ROUTED], marks[0], 256.0 * marks[1] + marks[2]

    rows, ids, ranks = unpack(arrived)
    ring = ("y", "xl", "xh", "core")
    size = 32

    def step(_, carry):
        moving, best = carry
        key_rows, key_ids, key_ranks = unpack(moving)
        scores = dot(rows, key_rows, ((1,), (1,)))
        allowed = (
            (ids[:, None] == key_ids[None, :])
            & (key_ids[None, :] > 0)
            & (key_ranks[None, :] < ranks[:, None])
        )
        best = jnp.maximum(best, jnp.max(jnp.where(allowed, scores, -1.0), axis=1))
        moving = lax.ppermute(moving, ring, [(i, (i + 1) % size) for i in range(size)])
        return moving, best

    _, best = lax.fori_loop(0, size, step, (arrived, jnp.full((ROUTED,), -1.0, jnp.float32)))
    steps = signed(lax.axis_index("core"), lax.axis_index("z") - jnp.arange(GROUPS)) & (GROUPS - 1)
    answered = lax.all_to_all(best.reshape(GROUPS, SLOTS)[steps], "z", 0, 0, tiled=True)
    picked = answered[jnp.maximum(target, 0), jnp.minimum(within, SLOTS - 1)]
    return jnp.where(live, picked, 0.0)


def column_shift(steps):
    pairs = []
    for z in range(8):
        for core in range(2):
            to = (z + (steps if core == 0 else -steps)) % 8
            pairs.append((z * 2 + core, to * 2 + core))
    return pairs


def plane_shift(dx, dy):
    def flat(x, y, core):
        return ((y % 4 * 2 + x % 4 % 2) * 2 + x % 4 // 2) * 2 + core

    pairs = []
    for core in range(2):
        s = 1 if core == 0 else -1
        for x in range(4):
            for y in range(4):
                pairs.append((flat(x + s * dx, y + s * dy, core), flat(x, y, core)))
    return pairs


def body(embeddings, cluster_id, order_rank, row_count):
    f32, bf16, i32 = jnp.float32, jnp.bfloat16, jnp.int32
    shape = jax.ShapeDtypeStruct
    slots_shape = shape((8, ROWS), i32)
    where_to, marks, slots = call(
        slot_kernel,
        (shape((ROUTED, ROWS), bf16), shape((16, ROWS), bf16), slots_shape),
        (cluster_id + 16 * order_rank).reshape(1, ROWS),
    )
    *pieces, slots = call(
        piece_kernel,
        tuple(shape((n * PIECE, META), bf16) for n in PIECES) + (slots_shape,),
        row_count,
        embeddings,
        where_to,
        marks,
        slots,
        smem=(0,),
    )
    send = lambda v, steps: lax.ppermute(v, COLUMN, column_shift(steps))
    two_four = send(pieces[2], 2)
    three, five, six = send(pieces[3], 3), send(pieces[4], 5), send(pieces[5], 6)
    four = send(two_four[PIECE:], 2)
    one, seven = send(pieces[1], 1), send(pieces[6], 7)
    arrived = call(
        collect_kernel,
        shape((ROUTED + MARKS, WIDTH), bf16),
        pieces[0],
        one,
        two_four,
        three,
        four,
        five,
        six,
        seven,
    )
    other = lax.ppermute(arrived, "core", [(0, 1), (1, 0)])
    first = call(
        first_kernel,
        (
            shape((CAP, WIDTH), bf16),
            shape((8, ROUTED), i32),
            shape((8, CAPL), f32),
            shape((8, META), f32),
        ),
        arrived,
    )
    block = call(compact_kernel, shape((CAP, WIDTH), bf16), other, *first)
    bring = lambda v, dx, dy: lax.ppermute(v, PLANE, plane_shift(dx, dy))
    x_first, y_first = bring(block, -1, 0), bring(block, 0, -1)
    best_shape, places_shape = shape((8, CAPL), f32), shape((16, META), i32)
    own_best, own_columns, own_places = call(
        own_kernel, (best_shape, shape((CAP, META), f32), places_shape), block
    )
    own, own_best = lax.optimization_barrier((block, own_best))
    x_second, y_second = bring(own, 1, 0), bring(own, 0, 1)
    x_far, y_far = bring(x_first, -1, 0), bring(y_first, 0, -1)
    near_blocks = (block, x_first, x_second, y_first, y_second)
    near, columns, near_places = call(
        near_kernel,
        (best_shape, shape((2, CAP, META), f32), shape((32, META), i32)),
        *near_blocks,
        own_best,
        own_columns,
        cost=8,
    )
    mid, mid_places = call(
        mid_kernel,
        (best_shape, places_shape),
        block,
        y_first,
        y_second,
        x_far,
        own_columns,
        columns,
        cost=3,
    )
    message = call(
        far_kernel,
        shape((64, 1, META), f32),
        *near_blocks,
        x_far,
        y_far,
        own_places,
        near,
        near_places,
        mid,
        mid_places,
        cost=4,
    )
    answer = lax.all_to_all(message, RETURN, split_axis=0, concat_axis=0, tiled=True)
    out, flag = call(final_kernel, (shape((1, ROWS), f32), shape((1,), i32)), slots, answer, smem_out=(1,))
    target, within = slots[0], slots[1]
    return lax.cond(
        flag[0] > 0,
        lambda: slow_path(arrived, target, within, target >= 0),
        lambda: out.reshape(ROWS),
    )


def solution(mesh):
    axes = ("y", "xl", "z", "xh", "core")
    fine = Mesh(mesh.devices.reshape(4, 2, 8, 2, 2), axes)
    return jax.shard_map(
        body,
        mesh=fine,
        in_specs=(P(axes, None), P(axes), P(axes), P(axes)),
        out_specs=P(axes),
        check_vma=False,
    )
```

```python
import functools

import jax
import jax.numpy as jnp
from jax import lax
from jax.experimental import pallas as pl
from jax.experimental.pallas import tpu as pltpu
from jax.sharding import Mesh, PartitionSpec as P

norm_eps = 1e-06
ROWS = 256
WIDTH = 768
META = 128
GROUPS = 8
SLOTS = 48
ROUTED = GROUPS * SLOTS
CAP = 304
HELD = CAP - 3
CAPL = 384
LAST = CAP - 16
NEVER = 512.0
CHUNKS = WIDTH // META
PIECE = CHUNKS * SLOTS + 16
MARKS = 32
PIECES = (1, 1, 2, 1, 1, 1, 1)
OVER = 100.0
VMEM_LIMIT = 50 * 1024 * 1024
PLANE = ("y", "xl", "xh", "core")
COLUMN = ("z", "core")
RETURN = ("xl", "z", "xh", "core")


def dot(a, b, contract):
    return lax.dot_general(a, b, (contract, ((), ())), preferred_element_type=jnp.float32)


def iota(shape, axis):
    return lax.broadcasted_iota(jnp.int32, shape, axis)


def split3(v):
    hi = v.astype(jnp.bfloat16)
    rest = v - hi.astype(jnp.float32)
    mid = rest.astype(jnp.bfloat16)
    low = (rest - mid.astype(jnp.float32)).astype(jnp.bfloat16)
    return hi, mid, low


def pick_rows(v, one_hot):
    n = v.shape[0]
    parts = dot(jnp.concatenate(split3(v), axis=0), one_hot, ((1,), (0,)))
    return (parts[:n] + parts[n : 2 * n]) + parts[2 * n :]


def call(kernel, out, *args, smem=(), smem_out=(), cost=1, scratch=()):
    space = lambda i, scalars: pl.BlockSpec(memory_space=pltpu.SMEM if i in scalars else pltpu.VMEM)
    out_specs = space(0, smem_out)
    if isinstance(out, tuple):
        out_specs = tuple(space(i, smem_out) for i in range(len(out)))
    return pl.pallas_call(
        kernel,
        out_shape=out,
        in_specs=[space(i, smem) for i in range(len(args))],
        out_specs=out_specs,
        scratch_shapes=list(scratch),
        cost_estimate=pl.CostEstimate(
            flops=2 * cost * CAP * CAP * WIDTH, bytes_accessed=4 * CAP * WIDTH, transcendentals=0
        ),
        compiler_params=pltpu.CompilerParams(vmem_limit_bytes=VMEM_LIMIT),
    )(*args)


def signed(core, value):
    return jnp.where(core == 0, value, -value)


def slot_kernel(both_ref, where_ref, marks_ref, slot_ref):
    ids, ranks = both_ref[...] & 15, both_ref[...] >> 4
    target = ids & (GROUPS - 1)
    chosen = jnp.where(iota((GROUPS, ROWS), 0) == target, 1.0, 0.0)
    upper = jnp.where(iota((ROWS, ROWS), 0) < iota((ROWS, ROWS), 1), 1.0, 0.0).astype(jnp.bfloat16)
    before = dot(chosen.astype(jnp.bfloat16), upper, ((1,), (0,)))
    within = jnp.sum(before * chosen, axis=0, keepdims=True).astype(jnp.int32)
    steps = signed(lax.axis_index("core"), target - lax.axis_index("z")) & (GROUPS - 1)
    at = jnp.where(steps == 3, 4, jnp.where(steps == 4, 3, steps))
    slot = jnp.where(within < SLOTS, at * SLOTS + within, -1)
    where_ref[...] = jnp.where(iota((ROUTED, ROWS), 0) == slot, 1.0, 0.0).astype(jnp.bfloat16)
    high = ranks >> 8
    row = iota((16, ROWS), 0)
    meta = jnp.where(
        row == 0, ids + 1, jnp.where(row == 1, high, jnp.where(row == 2, ranks - (high << 8), 0))
    )
    marks_ref[...] = meta.astype(jnp.float32).astype(jnp.bfloat16)
    slot_ref[0:1, :] = target
    slot_ref[1:2, :] = within
    slot_ref[2:8, :] = jnp.zeros((6, ROWS), jnp.int32)


def piece_kernel(count_ref, emb_ref, where_ref, marks_ref, slot_ref, *refs):
    *out_refs, live_slot_ref = refs
    live = iota((1, ROWS), 1) < count_ref[0]
    live_slot_ref[0:1, :] = jnp.where(live, slot_ref[0:1, :], -1)
    live_slot_ref[1:8, :] = slot_ref[1:8, :]
    x = emb_ref[...].astype(jnp.float32)
    unit = x * lax.rsqrt(jnp.sum(x * x, axis=1, keepdims=True) + norm_eps)
    unit = jnp.where(iota((ROWS, 1), 0) < count_ref[0], unit, 0.0).astype(jnp.bfloat16)
    where_to = where_ref[...]
    rows = dot(where_to, unit, ((1,), (0,))).astype(jnp.bfloat16)
    meta = jnp.where(live, marks_ref[...].astype(jnp.float32), 0.0).astype(jnp.bfloat16)
    marks = dot(meta, where_to, ((1,), (1,)))
    at = 0
    for ref in out_refs:
        for first in range(0, ref.shape[0], PIECE):
            for i in range(CHUNKS):
                ref[first + i * SLOTS : first + (i + 1) * SLOTS, :] = rows[
                    at : at + SLOTS, i * META : (i + 1) * META
                ]
            tail = jnp.concatenate(
                [marks[:, at : at + SLOTS], jnp.zeros((16, META - SLOTS), jnp.float32)], axis=1
            )
            ref[first + CHUNKS * SLOTS : first + PIECE, :] = tail.astype(jnp.bfloat16)
            at += SLOTS


def collect_kernel(*refs):
    out_ref = refs[-1]
    marks = []
    for j, ref in enumerate(refs[:-1]):
        for i in range(CHUNKS):
            out_ref[j * SLOTS : (j + 1) * SLOTS, i * META : (i + 1) * META] = ref[
                i * SLOTS : (i + 1) * SLOTS, :
            ]
        marks.append(ref[CHUNKS * SLOTS : PIECE, :].astype(jnp.float32))
    by_kind = [mark[i : i + 1, :] for i in range(3) for mark in marks]
    kinds = jnp.concatenate(by_kind + [jnp.zeros((MARKS - 3 * GROUPS, META), jnp.float32)], axis=0)
    out_ref[ROUTED:, :META] = kinds.astype(jnp.bfloat16)
    out_ref[ROUTED:, META:] = jnp.zeros((MARKS, WIDTH - META), jnp.bfloat16)


def slot_fold(both):
    slot = iota((both, META), 0)
    slot = slot - SLOTS * ((slot * 1366) >> 16)
    return jnp.where(slot == iota((both, META), 1), 1.0, 0.0).astype(jnp.bfloat16)


def place_rows(arrived_ref, first):
    marks = arrived_ref[ROUTED:, :META]
    spread = dot(marks, slot_fold(ROUTED), ((1,), (1,)))
    here = iota((GROUPS, ROUTED), 0) == ((iota((GROUPS, ROUTED), 1) * 1366) >> 16)
    meta = [
        jnp.sum(jnp.where(here, spread[GROUPS * i : GROUPS * (i + 1), :], 0.0), axis=0, keepdims=True)
        for i in range(3)
    ]
    mine = lax.axis_index("z") + GROUPS * lax.axis_index("core") + 1
    ones = jnp.where(meta[0] == mine.astype(jnp.float32), 1.0, 0.0)
    chunks = [ones[:, i : i + META] for i in range(0, ROUTED, META)]
    upper = jnp.where(iota((META, META), 0) < iota((META, META), 1), 1.0, 0.0).astype(jnp.bfloat16)
    stacked = jnp.concatenate(chunks + [jnp.zeros((8 - len(chunks), META), jnp.float32)], axis=0)
    before = dot(stacked.astype(jnp.bfloat16), upper, ((1,), (0,)))
    total, counted = first, []
    for i, chunk in enumerate(chunks):
        counted.append(jnp.where(chunk > 0.5, before[i : i + 1, :] + total, -1.0))
        total = total + jnp.sum(chunk, axis=1, keepdims=True)
    pos = jnp.concatenate(counted, axis=1).astype(jnp.int32)
    where_to = jnp.where((iota((CAPL, ROUTED), 0) == pos) & (pos < HELD), 1.0, 0.0).astype(jnp.bfloat16)
    meta = jnp.concatenate(meta + [jnp.zeros((5, ROUTED), jnp.float32)], axis=0)
    ranks = dot(meta.astype(jnp.bfloat16), where_to, ((1,), (1,)))
    return pos, where_to, ranks, total


def first_kernel(own_ref, rows_ref, pos_ref, ranks_ref, total_ref):
    pos, where_to, ranks, total = place_rows(own_ref, jnp.zeros((1, 1), jnp.float32))
    rows_ref[...] = dot(where_to[:CAP, :], own_ref[:ROUTED, :], ((1,), (0,))).astype(jnp.bfloat16)
    pos_ref[...] = jnp.broadcast_to(pos, (8, ROUTED))
    ranks_ref[...] = ranks
    total_ref[...] = jnp.broadcast_to(total, (8, META))


def compact_kernel(other_ref, rows_ref, pos_ref, ranks_ref, total_ref, block_ref):
    other_pos, where_to, other_ranks, total = place_rows(other_ref, total_ref[0:1, 0:1])
    rows = dot(where_to[:CAP, :], other_ref[:ROUTED, :], ((1,), (0,))) + rows_ref[...].astype(jnp.float32)
    pos = jnp.concatenate([pos_ref[0:1, :], other_pos], axis=1)
    ranks = ranks_ref[...] + other_ranks
    lane = iota((1, CAPL), 1)
    filled = (lane.astype(jnp.float32) < total) & (lane < HELD)
    high = jnp.where(filled, ranks[1:2, :], NEVER)
    high = jnp.where((lane == CAPL - 1) & (total > HELD), 2 * NEVER, high)
    low = jnp.where(filled, ranks[2:3, :], 0.0)
    place = pos + 1
    marks = (jnp.concatenate([high, low], axis=1), (place >> 8).astype(jnp.float32), (place & 255).astype(jnp.float32))
    row = iota((16, WIDTH), 0)
    last = rows[LAST:, :]
    for i, mark in enumerate(marks):
        last = jnp.where(row == 13 + i, mark, last)
    block_ref[:LAST, :] = rows[:LAST, :].astype(jnp.bfloat16)
    block_ref[LAST:, :] = last.astype(jnp.bfloat16)


def row_ranks(block):
    tail = block[LAST:, :].astype(jnp.float32)
    return (256.0 * tail[13:14, :CAPL] + tail[13:14, CAPL:])[:, :CAP]


def column_ranks(block, eye):
    high = dot(eye, block[LAST:, :CAPL], ((1,), (1,)))
    low = dot(eye, block[LAST:, CAPL:], ((1,), (1,)))
    return 256.0 * high[:, 13:14] + low[:, 13:14]


def slot_places(block):
    both = 2 * ROUTED
    tail = block[LAST:, :].astype(jnp.float32)
    first = iota((16, both), 0) * SLOTS
    lane = iota((16, both), 1)
    here = (lane >= first) & (lane < first + SLOTS)
    parts = jnp.concatenate([jnp.where(here, tail[i : i + 1, :], 0.0) for i in (14, 15)], axis=0)
    folded = dot(parts.astype(jnp.bfloat16), slot_fold(both), ((1,), (0,)))
    return (256.0 * folded[:16] + folded[16:]).astype(jnp.int32) - 1


def make_eye():
    return jnp.where(iota((CAP, CAPL), 0) == iota((CAP, CAPL), 1), 1.0, 0.0).astype(jnp.bfloat16)


def earlier_best(query, query_ranks, key, key_ranks):
    scores = dot(key[...], query[...], ((1,), (1,)))
    return jnp.max(jnp.where(key_ranks < query_ranks, scores, -1.0), axis=0, keepdims=True)


def own_kernel(own, best_ref, columns_ref, places_ref):
    columns = column_ranks(own, make_eye())
    columns_ref[...] = jnp.broadcast_to(columns, (CAP, META))
    best_ref[...] = jnp.full((8, CAPL), -1.0, jnp.float32)
    best_ref[0:1, :CAP] = earlier_best(own, row_ranks(own), own, columns)
    places_ref[...] = slot_places(own)


def near_kernel(
    own, x_first, x_second, y_first, y_second, own_best, own_columns, best_ref, columns_ref, places_ref
):
    eye = make_eye()
    ys = (y_first, y_second)
    columns = [column_ranks(key, eye) for key in ys]
    for i in range(2):
        columns_ref[i] = jnp.broadcast_to(columns[i], (CAP, META))
    best_ref[...] = own_best[...]
    for i, query in enumerate((own, x_first, x_second)):
        ranks = row_ranks(query)
        if i == 0:
            best = own_best[0:1, :CAP]
        else:
            best = earlier_best(query, ranks, own, own_columns[:, 0:1])
            places_ref[16 * (i - 1) : 16 * i, :] = slot_places(query)
        for key, ranked in zip(ys, columns):
            best = jnp.maximum(best, earlier_best(query, ranks, key, ranked))
        best_ref[i : i + 1, :CAP] = best


def mid_kernel(
    own, x_first, x_second, y_first, y_second, x_far, own_columns, columns_ref, near_ref,
    out_ref, places_ref, queries_ref, ranks_ref,
):
    ranks = row_ranks(x_far)
    best = earlier_best(x_far, ranks, own, own_columns[:, 0:1])
    for i, key in enumerate((y_first, y_second)):
        best = jnp.maximum(best, earlier_best(x_far, ranks, key, columns_ref[i, :, 0:1]))
    out_ref[...] = jnp.full((8, 4 * CAPL), -1.0, jnp.float32)
    ranks_ref[...] = jnp.zeros((8, 4 * CAPL), jnp.float32)
    for i, query in enumerate((own, x_first, x_second, x_far)):
        at = i * CAPL
        out_ref[0:1, at : at + CAP] = best if i == 3 else near_ref[i : i + 1, :CAP]
        ranks_ref[0:1, at : at + CAP] = row_ranks(query)
        queries_ref[at : at + CAP, :] = query[...]
        queries_ref[at + CAP : at + CAPL, :] = jnp.zeros((CAPL - CAP, WIDTH), jnp.bfloat16)
    places_ref[...] = slot_places(x_far)


def far_kernel(
    own, x_first, x_second, y_first, y_second, x_far, y_far,
    own_places, near_places, mid_ref, mid_places, queries_ref, ranks_ref, out_ref,
):
    queries, keys = (own, x_first, x_second, x_far), (y_first, y_second, y_far)
    far_columns = column_ranks(y_far, make_eye())
    over = 0.0
    for block in queries + keys:
        tail = block[LAST:, CAPL - META : CAPL].astype(jnp.float32)
        over = jnp.maximum(over, tail[13:14, META - 1 :])
    over = jnp.where(over > NEVER, 1.0, 0.0)
    my_core, my_z = lax.axis_index("core"), lax.axis_index("z")
    my_x = 2 * lax.axis_index("xh") + lax.axis_index("xl")
    rows = []
    for first in range(0, 4 * CAPL, 2 * CAPL):
        two = slice(first, first + 2 * CAPL)
        scores = dot(y_far[...], queries_ref[two, :], ((1,), (1,)))
        best = jnp.where(far_columns < ranks_ref[0:1, two], scores, -1.0)
        best = jnp.maximum(jnp.max(best, axis=0, keepdims=True), mid_ref[0:1, two])
        rows += [jnp.broadcast_to(best[:, at : at + CAPL], (16, CAPL)) for at in (0, CAPL)]
    rows = jnp.concatenate(rows, axis=0)
    places = jnp.concatenate([own_places[...], near_places[...], mid_places[...]], axis=0)
    found = jnp.full((64, META), -1.0, jnp.float32)
    for part in range(CAPL // META):
        values = rows[:, part * META : (part + 1) * META]
        picked = jnp.take_along_axis(values, places & (META - 1), axis=1, mode="promise_in_bounds")
        found = jnp.where((places >> 7) == part, picked, found)
    found = found + OVER * over
    messages = GROUPS * 8
    row, column = iota((messages, messages), 0), iota((messages, messages), 1)
    core = row & 1
    away = my_z - ((row >> 2) & 7)
    steps = jnp.where(core == 0, away, -away) & 7
    x_away = signed(my_core, my_x - (row >> 5) - (row & 2)) & 3
    block = jnp.where(x_away == 2, 3, jnp.where(x_away == 3, 2, x_away))
    wanted = block * 16 + (core ^ my_core) * GROUPS + steps
    order = jnp.where(column == wanted, 1.0, 0.0).astype(jnp.bfloat16)
    out = dot(jnp.concatenate([order] * 3, axis=1), jnp.concatenate(split3(found), axis=0), ((1,), (0,)))
    for i in range(messages):
        out_ref[i] = out[i : i + 1, :]


def final_kernel(slot_ref, ans_ref, out_ref, flag_ref):
    target, within = slot_ref[0:1, :], slot_ref[1:2, :]
    one_hot = jnp.where(iota((META, ROWS), 0) == within, 1.0, 0.0).astype(jnp.bfloat16)
    groups = []
    for g in range(GROUPS):
        rows = [ans_ref[xl * 32 + g * 4 + i] for xl in range(2) for i in range(4)]
        groups.append(functools.reduce(jnp.maximum, rows))
    best = jnp.concatenate(groups, axis=0)
    got = pick_rows(best, one_hot)
    out_ref[...] = jnp.sum(jnp.where(iota((GROUPS, ROWS), 0) == target, got, 0.0), axis=0, keepdims=True)
    flag_ref[0] = jnp.where(jnp.max(best) > 0.5 * OVER, 1, 0).astype(jnp.int32)


def slow_path(arrived, target, within, live):
    def unpack(v):
        marks = v[ROUTED : ROUTED + 3 * GROUPS, :SLOTS].astype(jnp.float32).reshape(3, ROUTED)
        return v[:ROUTED], marks[0], 256.0 * marks[1] + marks[2]

    rows, ids, ranks = unpack(arrived)
    ring = ("y", "xl", "xh", "core")
    size = 32

    def step(_, carry):
        moving, best = carry
        key_rows, key_ids, key_ranks = unpack(moving)
        scores = dot(rows, key_rows, ((1,), (1,)))
        allowed = (
            (ids[:, None] == key_ids[None, :])
            & (key_ids[None, :] > 0)
            & (key_ranks[None, :] < ranks[:, None])
        )
        best = jnp.maximum(best, jnp.max(jnp.where(allowed, scores, -1.0), axis=1))
        moving = lax.ppermute(moving, ring, [(i, (i + 1) % size) for i in range(size)])
        return moving, best

    _, best = lax.fori_loop(0, size, step, (arrived, jnp.full((ROUTED,), -1.0, jnp.float32)))
    steps = signed(lax.axis_index("core"), lax.axis_index("z") - jnp.arange(GROUPS)) & (GROUPS - 1)
    answered = lax.all_to_all(best.reshape(GROUPS, SLOTS)[steps], "z", 0, 0, tiled=True)
    picked = answered[jnp.maximum(target, 0), jnp.minimum(within, SLOTS - 1)]
    return jnp.where(live, picked, 0.0)


def column_shift(steps):
    pairs = []
    for z in range(8):
        for core in range(2):
            to = (z + (steps if core == 0 else -steps)) % 8
            pairs.append((z * 2 + core, to * 2 + core))
    return pairs


def plane_shift(dx, dy):
    def flat(x, y, core):
        return ((y % 4 * 2 + x % 4 % 2) * 2 + x % 4 // 2) * 2 + core

    pairs = []
    for core in range(2):
        s = 1 if core == 0 else -1
        for x in range(4):
            for y in range(4):
                pairs.append((flat(x + s * dx, y + s * dy, core), flat(x, y, core)))
    return pairs


def body(embeddings, cluster_id, order_rank, row_count):
    f32, bf16, i32 = jnp.float32, jnp.bfloat16, jnp.int32
    shape = jax.ShapeDtypeStruct
    slots_shape = shape((8, ROWS), i32)
    where_to, marks, slots = call(
        slot_kernel,
        (shape((ROUTED, ROWS), bf16), shape((16, ROWS), bf16), slots_shape),
        (cluster_id + 16 * order_rank).reshape(1, ROWS),
    )
    *pieces, slots = call(
        piece_kernel,
        tuple(shape((n * PIECE, META), bf16) for n in PIECES) + (slots_shape,),
        row_count,
        embeddings,
        where_to,
        marks,
        slots,
        smem=(0,),
    )
    send = lambda v, steps: lax.ppermute(v, COLUMN, column_shift(steps))
    two_four = send(pieces[2], 2)
    three, five, six = send(pieces[3], 3), send(pieces[4], 5), send(pieces[5], 6)
    four = send(two_four[PIECE:], 2)
    one, seven = send(pieces[1], 1), send(pieces[6], 7)
    arrived = call(
        collect_kernel,
        shape((ROUTED + MARKS, WIDTH), bf16),
        pieces[0],
        one,
        two_four,
        three,
        four,
        five,
        six,
        seven,
    )
    other = lax.ppermute(arrived, "core", [(0, 1), (1, 0)])
    first = call(
        first_kernel,
        (
            shape((CAP, WIDTH), bf16),
            shape((8, ROUTED), i32),
            shape((8, CAPL), f32),
            shape((8, META), f32),
        ),
        arrived,
    )
    block = call(compact_kernel, shape((CAP, WIDTH), bf16), other, *first)
    bring = lambda v, dx, dy: lax.ppermute(v, PLANE, plane_shift(dx, dy))
    x_first, y_first = bring(block, -1, 0), bring(block, 0, -1)
    best_shape, places_shape = shape((8, CAPL), f32), shape((16, META), i32)
    own_best, own_columns, own_places = call(
        own_kernel, (best_shape, shape((CAP, META), f32), places_shape), block
    )
    own, own_best = lax.optimization_barrier((block, own_best))
    x_second, y_second = bring(own, 1, 0), bring(own, 0, 1)
    x_far, y_far = bring(x_first, -1, 0), bring(y_first, 0, -1)
    near_blocks = (block, x_first, x_second, y_first, y_second)
    near, columns, near_places = call(
        near_kernel,
        (best_shape, shape((2, CAP, META), f32), shape((32, META), i32)),
        *near_blocks,
        own_best,
        own_columns,
        cost=8,
    )
    wide = shape((8, 4 * CAPL), f32)
    mid, mid_places, queries, ranks = call(
        mid_kernel,
        (wide, places_shape, shape((4 * CAPL, WIDTH), bf16), wide),
        *near_blocks,
        x_far,
        own_columns,
        columns,
        near,
        cost=3,
    )
    message = call(
        far_kernel,
        shape((64, 1, META), f32),
        *near_blocks,
        x_far,
        y_far,
        own_places,
        near_places,
        mid,
        mid_places,
        queries,
        ranks,
        cost=4,
    )
    answer = lax.all_to_all(message, RETURN, split_axis=0, concat_axis=0, tiled=True)
    out, flag = call(final_kernel, (shape((1, ROWS), f32), shape((1,), i32)), slots, answer, smem_out=(1,))
    target, within = slots[0], slots[1]
    return lax.cond(
        flag[0] > 0,
        lambda: slow_path(arrived, target, within, target >= 0),
        lambda: out.reshape(ROWS),
    )


def solution(mesh):
    axes = ("y", "xl", "z", "xh", "core")
    fine = Mesh(mesh.devices.reshape(4, 2, 8, 2, 2), axes)
    return jax.shard_map(
        body,
        mesh=fine,
        in_specs=(P(axes, None), P(axes), P(axes), P(axes)),
        out_specs=P(axes),
        check_vma=False,
    )
```

```python
import functools

import jax
import jax.numpy as jnp
from jax import lax
from jax.experimental import pallas as pl
from jax.experimental.pallas import tpu as pltpu
from jax.sharding import Mesh, PartitionSpec as P

norm_eps = 1e-06
ROWS = 256
WIDTH = 768
META = 128
GROUPS = 8
SLOTS = 48
ROUTED = GROUPS * SLOTS
CAP = 304
HELD = CAP - 3
CAPL = 384
LAST = CAP - 16
NEVER = 512.0
CHUNKS = WIDTH // META
PIECE = CHUNKS * SLOTS + 16
MARKS = 32
PIECES = (1, 1, 2, 1, 1, 1, 1)
OVER = 100.0
VMEM_LIMIT = 50 * 1024 * 1024
PLANE = ("y", "xl", "xh", "core")
COLUMN = ("z", "core")
RETURN = ("xl", "z", "xh", "core")


def dot(a, b, contract):
    return lax.dot_general(a, b, (contract, ((), ())), preferred_element_type=jnp.float32)


def iota(shape, axis):
    return lax.broadcasted_iota(jnp.int32, shape, axis)


def split3(v):
    hi = v.astype(jnp.bfloat16)
    rest = v - hi.astype(jnp.float32)
    mid = rest.astype(jnp.bfloat16)
    low = (rest - mid.astype(jnp.float32)).astype(jnp.bfloat16)
    return hi, mid, low


def pick_rows(v, one_hot):
    n = v.shape[0]
    parts = dot(jnp.concatenate(split3(v), axis=0), one_hot, ((1,), (0,)))
    return (parts[:n] + parts[n : 2 * n]) + parts[2 * n :]


def call(kernel, out, *args, smem=(), smem_out=(), cost=1, scratch=()):
    space = lambda i, scalars: pl.BlockSpec(memory_space=pltpu.SMEM if i in scalars else pltpu.VMEM)
    out_specs = space(0, smem_out)
    if isinstance(out, tuple):
        out_specs = tuple(space(i, smem_out) for i in range(len(out)))
    return pl.pallas_call(
        kernel,
        out_shape=out,
        in_specs=[space(i, smem) for i in range(len(args))],
        out_specs=out_specs,
        scratch_shapes=list(scratch),
        cost_estimate=pl.CostEstimate(
            flops=2 * cost * CAP * CAP * WIDTH, bytes_accessed=4 * CAP * WIDTH, transcendentals=0
        ),
        compiler_params=pltpu.CompilerParams(vmem_limit_bytes=VMEM_LIMIT),
    )(*args)


def signed(core, value):
    return jnp.where(core == 0, value, -value)


def slot_kernel(both_ref, where_ref, marks_ref, slot_ref):
    ids, ranks = both_ref[...] & 15, both_ref[...] >> 4
    target = ids & (GROUPS - 1)
    chosen = jnp.where(iota((GROUPS, ROWS), 0) == target, 1.0, 0.0)
    upper = jnp.where(iota((ROWS, ROWS), 0) < iota((ROWS, ROWS), 1), 1.0, 0.0).astype(jnp.bfloat16)
    before = dot(chosen.astype(jnp.bfloat16), upper, ((1,), (0,)))
    within = jnp.sum(before * chosen, axis=0, keepdims=True).astype(jnp.int32)
    steps = signed(lax.axis_index("core"), target - lax.axis_index("z")) & (GROUPS - 1)
    at = jnp.where(steps == 3, 4, jnp.where(steps == 4, 3, steps))
    slot = jnp.where(within < SLOTS, at * SLOTS + within, -1)
    where_ref[...] = jnp.where(iota((ROUTED, ROWS), 0) == slot, 1.0, 0.0).astype(jnp.bfloat16)
    high = ranks >> 8
    row = iota((16, ROWS), 0)
    meta = jnp.where(
        row == 0, ids + 1, jnp.where(row == 1, high, jnp.where(row == 2, ranks - (high << 8), 0))
    )
    marks_ref[...] = meta.astype(jnp.float32).astype(jnp.bfloat16)
    slot_ref[0:1, :] = target
    slot_ref[1:2, :] = within
    slot_ref[2:8, :] = jnp.zeros((6, ROWS), jnp.int32)


def piece_kernel(count_ref, emb_ref, where_ref, marks_ref, slot_ref, *refs):
    *out_refs, live_slot_ref = refs
    live = iota((1, ROWS), 1) < count_ref[0]
    live_slot_ref[0:1, :] = jnp.where(live, slot_ref[0:1, :], -1)
    live_slot_ref[1:8, :] = slot_ref[1:8, :]
    x = emb_ref[...].astype(jnp.float32)
    unit = x * lax.rsqrt(jnp.sum(x * x, axis=1, keepdims=True) + norm_eps)
    unit = jnp.where(iota((ROWS, 1), 0) < count_ref[0], unit, 0.0).astype(jnp.bfloat16)
    where_to = where_ref[...]
    rows = dot(where_to, unit, ((1,), (0,))).astype(jnp.bfloat16)
    meta = jnp.where(live, marks_ref[...].astype(jnp.float32), 0.0).astype(jnp.bfloat16)
    marks = dot(meta, where_to, ((1,), (1,)))
    at = 0
    for ref in out_refs:
        for first in range(0, ref.shape[0], PIECE):
            for i in range(CHUNKS):
                ref[first + i * SLOTS : first + (i + 1) * SLOTS, :] = rows[
                    at : at + SLOTS, i * META : (i + 1) * META
                ]
            tail = jnp.concatenate(
                [marks[:, at : at + SLOTS], jnp.zeros((16, META - SLOTS), jnp.float32)], axis=1
            )
            ref[first + CHUNKS * SLOTS : first + PIECE, :] = tail.astype(jnp.bfloat16)
            at += SLOTS


def collect_kernel(*refs):
    out_ref = refs[-1]
    marks = []
    for j, ref in enumerate(refs[:-1]):
        for i in range(CHUNKS):
            out_ref[j * SLOTS : (j + 1) * SLOTS, i * META : (i + 1) * META] = ref[
                i * SLOTS : (i + 1) * SLOTS, :
            ]
        marks.append(ref[CHUNKS * SLOTS : PIECE, :].astype(jnp.float32))
    by_kind = [mark[i : i + 1, :] for i in range(3) for mark in marks]
    kinds = jnp.concatenate(by_kind + [jnp.zeros((MARKS - 3 * GROUPS, META), jnp.float32)], axis=0)
    out_ref[ROUTED:, :META] = kinds.astype(jnp.bfloat16)
    out_ref[ROUTED:, META:] = jnp.zeros((MARKS, WIDTH - META), jnp.bfloat16)


def slot_fold(both):
    slot = iota((both, META), 0)
    slot = slot - SLOTS * ((slot * 1366) >> 16)
    return jnp.where(slot == iota((both, META), 1), 1.0, 0.0).astype(jnp.bfloat16)


def place_rows(arrived_ref, first):
    marks = arrived_ref[ROUTED:, :META]
    spread = dot(marks, slot_fold(ROUTED), ((1,), (1,)))
    here = iota((GROUPS, ROUTED), 0) == ((iota((GROUPS, ROUTED), 1) * 1366) >> 16)
    meta = [
        jnp.sum(jnp.where(here, spread[GROUPS * i : GROUPS * (i + 1), :], 0.0), axis=0, keepdims=True)
        for i in range(3)
    ]
    mine = lax.axis_index("z") + GROUPS * lax.axis_index("core") + 1
    ones = jnp.where(meta[0] == mine.astype(jnp.float32), 1.0, 0.0)
    chunks = [ones[:, i : i + META] for i in range(0, ROUTED, META)]
    upper = jnp.where(iota((META, META), 0) < iota((META, META), 1), 1.0, 0.0).astype(jnp.bfloat16)
    stacked = jnp.concatenate(chunks + [jnp.zeros((8 - len(chunks), META), jnp.float32)], axis=0)
    before = dot(stacked.astype(jnp.bfloat16), upper, ((1,), (0,)))
    total, counted = first, []
    for i, chunk in enumerate(chunks):
        counted.append(jnp.where(chunk > 0.5, before[i : i + 1, :] + total, -1.0))
        total = total + jnp.sum(chunk, axis=1, keepdims=True)
    pos = jnp.concatenate(counted, axis=1).astype(jnp.int32)
    where_to = jnp.where((iota((CAPL, ROUTED), 0) == pos) & (pos < HELD), 1.0, 0.0).astype(jnp.bfloat16)
    meta = jnp.concatenate(meta + [jnp.zeros((5, ROUTED), jnp.float32)], axis=0)
    ranks = dot(meta.astype(jnp.bfloat16), where_to, ((1,), (1,)))
    return pos, where_to, ranks, total


def first_kernel(own_ref, rows_ref, pos_ref, ranks_ref, total_ref):
    pos, where_to, ranks, total = place_rows(own_ref, jnp.zeros((1, 1), jnp.float32))
    rows_ref[...] = dot(where_to[:CAP, :], own_ref[:ROUTED, :], ((1,), (0,))).astype(jnp.bfloat16)
    pos_ref[...] = jnp.broadcast_to(pos, (8, ROUTED))
    ranks_ref[...] = ranks
    total_ref[...] = jnp.broadcast_to(total, (8, META))


def compact_kernel(other_ref, rows_ref, pos_ref, ranks_ref, total_ref, block_ref):
    other_pos, where_to, other_ranks, total = place_rows(other_ref, total_ref[0:1, 0:1])
    rows = dot(where_to[:CAP, :], other_ref[:ROUTED, :], ((1,), (0,))) + rows_ref[...].astype(jnp.float32)
    pos = jnp.concatenate([pos_ref[0:1, :], other_pos], axis=1)
    ranks = ranks_ref[...] + other_ranks
    lane = iota((1, CAPL), 1)
    filled = (lane.astype(jnp.float32) < total) & (lane < HELD)
    high = jnp.where(filled, ranks[1:2, :], NEVER)
    high = jnp.where((lane == CAPL - 1) & (total > HELD), 2 * NEVER, high)
    low = jnp.where(filled, ranks[2:3, :], 0.0)
    place = pos + 1
    marks = (jnp.concatenate([high, low], axis=1), (place >> 8).astype(jnp.float32), (place & 255).astype(jnp.float32))
    row = iota((16, WIDTH), 0)
    last = rows[LAST:, :]
    for i, mark in enumerate(marks):
        last = jnp.where(row == 13 + i, mark, last)
    block_ref[:LAST, :] = rows[:LAST, :].astype(jnp.bfloat16)
    block_ref[LAST:, :] = last.astype(jnp.bfloat16)


def row_ranks(block):
    tail = block[LAST:, :].astype(jnp.float32)
    return (256.0 * tail[13:14, :CAPL] + tail[13:14, CAPL:])[:, :CAP]


def column_ranks(block, eye):
    high = dot(eye, block[LAST:, :CAPL], ((1,), (1,)))
    low = dot(eye, block[LAST:, CAPL:], ((1,), (1,)))
    return 256.0 * high[:, 13:14] + low[:, 13:14]


def slot_places(block):
    both = 2 * ROUTED
    tail = block[LAST:, :].astype(jnp.float32)
    first = iota((16, both), 0) * SLOTS
    lane = iota((16, both), 1)
    here = (lane >= first) & (lane < first + SLOTS)
    parts = jnp.concatenate([jnp.where(here, tail[i : i + 1, :], 0.0) for i in (14, 15)], axis=0)
    folded = dot(parts.astype(jnp.bfloat16), slot_fold(both), ((1,), (0,)))
    return (256.0 * folded[:16] + folded[16:]).astype(jnp.int32) - 1


def make_eye():
    return jnp.where(iota((CAP, CAPL), 0) == iota((CAP, CAPL), 1), 1.0, 0.0).astype(jnp.bfloat16)


def earlier_best(query, query_ranks, key, key_ranks):
    scores = dot(key[...], query[...], ((1,), (1,)))
    return jnp.max(jnp.where(key_ranks < query_ranks, scores, -1.0), axis=0, keepdims=True)


def own_kernel(own, best_ref, columns_ref, places_ref):
    columns = column_ranks(own, make_eye())
    columns_ref[...] = jnp.broadcast_to(columns, (CAP, META))
    best_ref[...] = jnp.full((8, CAPL), -1.0, jnp.float32)
    best_ref[0:1, :CAP] = earlier_best(own, row_ranks(own), own, columns)
    places_ref[...] = slot_places(own)


def near_kernel(
    own, x_first, x_second, y_first, y_second, own_best, own_columns, best_ref, columns_ref, places_ref
):
    eye = make_eye()
    ys = (y_first, y_second)
    columns = [column_ranks(key, eye) for key in ys]
    for i in range(2):
        columns_ref[i] = jnp.broadcast_to(columns[i], (CAP, META))
    best_ref[...] = own_best[...]
    for i, query in enumerate((own, x_first, x_second)):
        ranks = row_ranks(query)
        if i == 0:
            best = own_best[0:1, :CAP]
        else:
            best = earlier_best(query, ranks, own, own_columns[:, 0:1])
            places_ref[16 * (i - 1) : 16 * i, :] = slot_places(query)
        for key, ranked in zip(ys, columns):
            best = jnp.maximum(best, earlier_best(query, ranks, key, ranked))
        best_ref[i : i + 1, :CAP] = best


def mid_kernel(own, y_first, y_second, x_far, own_columns, columns_ref, out_ref, places_ref):
    ranks = row_ranks(x_far)
    best = earlier_best(x_far, ranks, own, own_columns[:, 0:1])
    for i, key in enumerate((y_first, y_second)):
        best = jnp.maximum(best, earlier_best(x_far, ranks, key, columns_ref[i, :, 0:1]))
    out_ref[...] = jnp.full((8, CAPL), -1.0, jnp.float32)
    out_ref[0:1, :CAP] = best
    places_ref[...] = slot_places(x_far)


def far_kernel(
    own, x_first, x_second, y_first, y_second, x_far, y_far,
    own_places, near_ref, near_places, mid_ref, mid_places, out_ref,
):
    queries, keys = (own, x_first, x_second, x_far), (y_first, y_second, y_far)
    far_columns = column_ranks(y_far, make_eye())
    over = 0.0
    for block in queries + keys:
        tail = block[LAST:, CAPL - META : CAPL].astype(jnp.float32)
        over = jnp.maximum(over, tail[13:14, META - 1 :])
    over = jnp.where(over > NEVER, 1.0, 0.0)
    my_core, my_z = lax.axis_index("core"), lax.axis_index("z")
    my_x = 2 * lax.axis_index("xh") + lax.axis_index("xl")
    rows = []
    for i, query in enumerate(queries):
        best = earlier_best(query, row_ranks(query), y_far, far_columns)
        best = jnp.maximum(best, near_ref[i : i + 1, :CAP] if i < 3 else mid_ref[0:1, :CAP])
        best = jnp.concatenate([best, jnp.full((1, CAPL - CAP), -1.0, jnp.float32)], axis=1)
        rows.append(jnp.broadcast_to(best, (16, CAPL)))
    rows = jnp.concatenate(rows, axis=0)
    places = jnp.concatenate([own_places[...], near_places[...], mid_places[...]], axis=0)
    found = jnp.full((64, META), -1.0, jnp.float32)
    for part in range(CAPL // META):
        values = rows[:, part * META : (part + 1) * META]
        picked = jnp.take_along_axis(values, places & (META - 1), axis=1, mode="promise_in_bounds")
        found = jnp.where((places >> 7) == part, picked, found)
    found = found + OVER * over
    messages = GROUPS * 8
    row, column = iota((messages, messages), 0), iota((messages, messages), 1)
    core = row & 1
    away = my_z - ((row >> 2) & 7)
    steps = jnp.where(core == 0, away, -away) & 7
    x_away = signed(my_core, my_x - (row >> 5) - (row & 2)) & 3
    block = jnp.where(x_away == 2, 3, jnp.where(x_away == 3, 2, x_away))
    wanted = block * 16 + (core ^ my_core) * GROUPS + steps
    order = jnp.where(column == wanted, 1.0, 0.0).astype(jnp.bfloat16)
    out = dot(jnp.concatenate([order] * 3, axis=1), jnp.concatenate(split3(found), axis=0), ((1,), (0,)))
    for i in range(messages):
        out_ref[i] = out[i : i + 1, :]


def final_kernel(slot_ref, ans_ref, out_ref, flag_ref):
    target, within = slot_ref[0:1, :], slot_ref[1:2, :]
    one_hot = jnp.where(iota((META, ROWS), 0) == within, 1.0, 0.0).astype(jnp.bfloat16)
    groups = []
    for g in range(GROUPS):
        rows = [ans_ref[xl * 32 + g * 4 + i] for xl in range(2) for i in range(4)]
        groups.append(functools.reduce(jnp.maximum, rows))
    best = jnp.concatenate(groups, axis=0)
    got = pick_rows(best, one_hot)
    out_ref[...] = jnp.sum(jnp.where(iota((GROUPS, ROWS), 0) == target, got, 0.0), axis=0, keepdims=True)
    flag_ref[0] = jnp.where(jnp.max(best) > 0.5 * OVER, 1, 0).astype(jnp.int32)


def slow_path(arrived, target, within, live):
    def unpack(v):
        marks = v[ROUTED : ROUTED + 3 * GROUPS, :SLOTS].astype(jnp.float32).reshape(3, ROUTED)
        return v[:ROUTED], marks[0], 256.0 * marks[1] + marks[2]

    rows, ids, ranks = unpack(arrived)
    ring = ("y", "xl", "xh", "core")
    size = 32

    def step(_, carry):
        moving, best = carry
        key_rows, key_ids, key_ranks = unpack(moving)
        scores = dot(rows, key_rows, ((1,), (1,)))
        allowed = (
            (ids[:, None] == key_ids[None, :])
            & (key_ids[None, :] > 0)
            & (key_ranks[None, :] < ranks[:, None])
        )
        best = jnp.maximum(best, jnp.max(jnp.where(allowed, scores, -1.0), axis=1))
        moving = lax.ppermute(moving, ring, [(i, (i + 1) % size) for i in range(size)])
        return moving, best

    _, best = lax.fori_loop(0, size, step, (arrived, jnp.full((ROUTED,), -1.0, jnp.float32)))
    steps = signed(lax.axis_index("core"), lax.axis_index("z") - jnp.arange(GROUPS)) & (GROUPS - 1)
    answered = lax.all_to_all(best.reshape(GROUPS, SLOTS)[steps], "z", 0, 0, tiled=True)
    picked = answered[jnp.maximum(target, 0), jnp.minimum(within, SLOTS - 1)]
    return jnp.where(live, picked, 0.0)


def column_shift(steps):
    pairs = []
    for z in range(8):
        for core in range(2):
            to = (z + (steps if core == 0 else -steps)) % 8
            pairs.append((z * 2 + core, to * 2 + core))
    return pairs


def plane_shift(dx, dy):
    def flat(x, y, core):
        return ((y % 4 * 2 + x % 4 % 2) * 2 + x % 4 // 2) * 2 + core

    pairs = []
    for core in range(2):
        s = 1 if core == 0 else -1
        for x in range(4):
            for y in range(4):
                pairs.append((flat(x + s * dx, y + s * dy, core), flat(x, y, core)))
    return pairs


def body(embeddings, cluster_id, order_rank, row_count):
    f32, bf16, i32 = jnp.float32, jnp.bfloat16, jnp.int32
    shape = jax.ShapeDtypeStruct
    slots_shape = shape((8, ROWS), i32)
    where_to, marks, slots = call(
        slot_kernel,
        (shape((ROUTED, ROWS), bf16), shape((16, ROWS), bf16), slots_shape),
        (cluster_id + 16 * order_rank).reshape(1, ROWS),
    )
    *pieces, slots = call(
        piece_kernel,
        tuple(shape((n * PIECE, META), bf16) for n in PIECES) + (slots_shape,),
        row_count,
        embeddings,
        where_to,
        marks,
        slots,
        smem=(0,),
    )
    send = lambda v, steps: lax.ppermute(v, COLUMN, column_shift(steps))
    two_four = send(pieces[2], 2)
    three, five, six = send(pieces[3], 3), send(pieces[4], 5), send(pieces[5], 6)
    four = send(two_four[PIECE:], 2)
    one, seven = send(pieces[1], 1), send(pieces[6], 7)
    arrived = call(
        collect_kernel,
        shape((ROUTED + MARKS, WIDTH), bf16),
        pieces[0],
        one,
        two_four,
        three,
        four,
        five,
        six,
        seven,
    )
    other = lax.ppermute(arrived, "core", [(0, 1), (1, 0)])
    first = call(
        first_kernel,
        (
            shape((CAP, WIDTH), bf16),
            shape((8, ROUTED), i32),
            shape((8, CAPL), f32),
            shape((8, META), f32),
        ),
        arrived,
    )
    block = call(compact_kernel, shape((CAP, WIDTH), bf16), other, *first)
    bring = lambda v, dx, dy: lax.ppermute(v, PLANE, plane_shift(dx, dy))
    x_first, y_first = bring(block, -1, 0), bring(block, 0, 1)
    best_shape, places_shape = shape((8, CAPL), f32), shape((16, META), i32)
    own_best, own_columns, own_places = call(
        own_kernel, (best_shape, shape((CAP, META), f32), places_shape), block
    )
    own, own_best = lax.optimization_barrier((block, own_best))
    x_second, y_second = bring(own, 1, 0), bring(own, 0, -1)
    x_far, y_far = bring(x_first, -1, 0), bring(y_first, 0, 1)
    near_blocks = (block, x_first, x_second, y_first, y_second)
    near, columns, near_places = call(
        near_kernel,
        (best_shape, shape((2, CAP, META), f32), shape((32, META), i32)),
        *near_blocks,
        own_best,
        own_columns,
        cost=8,
    )
    mid, mid_places = call(
        mid_kernel,
        (best_shape, places_shape),
        block,
        y_first,
        y_second,
        x_far,
        own_columns,
        columns,
        cost=3,
    )
    message = call(
        far_kernel,
        shape((64, 1, META), f32),
        *near_blocks,
        x_far,
        y_far,
        own_places,
        near,
        near_places,
        mid,
        mid_places,
        cost=4,
    )
    answer = lax.all_to_all(message, RETURN, split_axis=0, concat_axis=0, tiled=True)
    out, flag = call(final_kernel, (shape((1, ROWS), f32), shape((1,), i32)), slots, answer, smem_out=(1,))
    target, within = slots[0], slots[1]
    return lax.cond(
        flag[0] > 0,
        lambda: slow_path(arrived, target, within, target >= 0),
        lambda: out.reshape(ROWS),
    )


def solution(mesh):
    axes = ("y", "xl", "z", "xh", "core")
    fine = Mesh(mesh.devices.reshape(4, 2, 8, 2, 2), axes)
    return jax.shard_map(
        body,
        mesh=fine,
        in_specs=(P(axes, None), P(axes), P(axes), P(axes)),
        out_specs=P(axes),
        check_vma=False,
    )
```
